32 devices in a mesh: dp: 16 (over z, x, core), seq: 2 (over y).
Axes of the slice: x: 2, y: 2, z: 4, core: 2. Of those that a mesh axis runs over, the one named last changes fastest.
Arguments:
- hidden_in: bfloat16 [16, 1024, 512], P('dp', 'seq'), may hold values from -6 to 6
- enc_states: bfloat16 [16, 1024, 512], P('dp', 'seq'), may hold values from -6 to 6
- segment_ids: int32 [16, 1024], P('dp', 'seq'), may hold values from 0 to 3, as said below
- edit_pass: int32 [16, 1024], P('dp', 'seq'), may hold values from 0 to 2, as said below
- enc_segments: int32 [16, 1024], P('dp', 'seq'), may hold values from 0 to 3, as said below
- target_tokens: int32 [16, 1024], P('dp', 'seq'), may hold values from 0 to 32767
- placeholder_counts: int32 [16, 1024], P('dp', 'seq'), may hold values from 0 to 255
- delete_labels: int32 [16, 1024], P('dp', 'seq'), may hold values from 0 to 1
- loss_mask: int32 [16, 1024], P('dp', 'seq'), may hold values 0 or 1
- w_self_qkv: bfloat16 [512, 1536], replicated, may hold values from -0.25 to 0.25
- w_self_out: bfloat16 [512, 512], replicated, may hold values from -4 to 4
- w_cross_q: bfloat16 [512, 512], replicated, may hold values from -0.25 to 0.25
- w_cross_kv: bfloat16 [512, 1024], replicated, may hold values from -0.25 to 0.25
- w_cross_out: bfloat16 [512, 512], replicated, may hold values from -4 to 4
- w_ffn_in: bfloat16 [512, 2048], replicated, may hold values from -0.25 to 0.25
- b_ffn_in: float32 [2048], replicated, may hold values from -3 to 3
- w_ffn_out: bfloat16 [2048, 512], replicated, may hold values from -0.25 to 0.25
- b_ffn_out: float32 [512], replicated, may hold values from -3 to 3
- norm_gains: float32 [3, 512], replicated, may hold values from 0.5 to 1.5
- norm_shifts: float32 [3, 512], replicated, may hold values from -3 to 3
- w_vocab: bfloat16 [32768, 512], replicated, may hold values from -0.75 to 0.75
- w_pair: bfloat16 [1024, 256], replicated, may hold values from -0.25 to 0.25
- b_pair: float32 [256], replicated, may hold values from -3 to 3
- w_delete: bfloat16 [512, 2], replicated, may hold values from -0.375 to 0.375
Outputs:
- block_out: bfloat16 [16, 1024, 512], P('dp', 'seq')
- d_hidden: float32 [16, 1024, 512], P('dp', 'seq')
- d_enc: float32 [16, 1024, 512], P('dp', 'seq')
- d_self_qkv: float32 [512, 1536], replicated
- d_self_out: float32 [512, 512], replicated
- d_cross_q: float32 [512, 512], replicated
- d_cross_kv: float32 [512, 1024], replicated
- d_cross_out: float32 [512, 512], replicated
- d_ffn_in: float32 [512, 2048], replicated
- d_b_ffn_in: float32 [2048], replicated
- d_ffn_out: float32 [2048, 512], replicated
- d_b_ffn_out: float32 [512], replicated
- d_gains: float32 [3, 512], replicated
- d_shifts: float32 [3, 512], replicated
- d_vocab: float32 [32768, 512], P(('dp', 'seq'))
- d_pair: float32 [1024, 256], replicated
- d_b_pair: float32 [256], replicated
- d_delete: float32 [512, 2], replicated
The draws below stay inside these ranges and needn't reach their ends.
Inputs may be any that keep to these rules, and one draw needn't show every extreme that they name: `segment_ids`: each row holds the four sentences 0 to 3 in order, none empty. `edit_pass`: constant within a sentence; every row holds all three passes. `enc_segments`: each row holds the four sentences 0 to 3 in order, none empty.
All inputs are finite; a program needn't handle non-finite values. No bound on the sum of `loss_mask` on one device may be relied on, other than what follows from the above.
Results may differ from the reference program's by a relative error of at most 0.025.
Values may be sent and summed in bfloat16 or wider, within the bound.
No kernel may reach another device: no remote copies, remote signals or barrier semaphores. Data moves between devices by JAX's collectives and lax.ppermute only.
A program may use at most 256 MiB of HBM per device.

```python
import math
import jax
import jax.numpy as jnp
import numpy as np
from jax import lax

D = 512
HEADS = 8
HEAD_DIM = 64
FF = 2048
VOCAB = 32768
PAIRS = 256
ROW_LEN = 1024
ENC_LEN = 1024
ROWS = 16
BLK = 512
EBLK = 512


def sentence_cuts(key, length, piece):
    cut_one = jax.random.randint(jax.random.fold_in(key, 1), (ROWS,), 1, piece)
    cut_two = jax.random.randint(jax.random.fold_in(key, 2), (ROWS,), length - piece + 1, length - 1)
    cut_three = jax.random.randint(jax.random.fold_in(key, 3), (ROWS,), cut_two + 1, length)
    position = jnp.arange(length, dtype=jnp.int32)[None, :]
    return (position >= cut_one[:, None]).astype(jnp.int32) + (position >= cut_two[:, None]).astype(jnp.int32) + (position >= cut_three[:, None]).astype(jnp.int32)


def draw_segment_ids(key, part):
    return sentence_cuts(key, ROW_LEN, BLK)


def draw_edit_pass(key, part):
    sentence = sentence_cuts(key, ROW_LEN, BLK)
    key = jax.random.fold_in(key, 11)
    offset = jax.random.randint(key, (ROWS, 1), 0, 3)
    return (sentence + offset) % 3


def draw_enc_segments(key, part):
    key = jax.random.fold_in(key, 23)
    return sentence_cuts(key, ENC_LEN, EBLK)


def plant(values, stream_key, least, top_value):
    extent = values.shape
    place = [jax.random.randint(jax.random.fold_in(stream_key, axis), (), 0, extent[axis]) for axis in range(len(extent))]
    values = values.at[tuple(place)].set(least)
    longest = extent.index(max(extent))
    place[longest] = (place[longest] + 1) % extent[longest]
    return values.at[tuple(place)].set(top_value)


def steps_of(rng, shape, shards, low, high):
    def one(dim, shards_of):
        steps = jax.random.uniform(jax.random.fold_in(jax.random.fold_in(rng, 6), dim), (shards_of,), jnp.float32, low / len(shards), high / len(shards))
        return jnp.repeat(jnp.exp(steps), shape[dim] // shards_of).reshape((-1,) + (1,) * (len(shape) - dim - 1))

    gain = one(*shards[0])
    for cut in shards[1:]:
        gain = gain * one(*cut)
    return gain


def rank_bounds(amount, lean):
    portions = [(1 << 20) // math.isqrt(standing ** lean) + 1 for standing in range(1, amount + 1)]
    scale = 1 + sum(portions) // (1 << 30)
    return np.cumsum(np.array([max(1, weight // scale) for weight in portions]))


def skewed_ids(key, shape, count, skew):
    listing = rank_bounds(count, skew)
    pick = jax.random.randint(jax.random.fold_in(key, 1), shape, 0, int(listing[count - 1]))
    rank = jnp.searchsorted(jnp.asarray(listing, jnp.int32), pick, side="right")
    return jax.random.permutation(jax.random.fold_in(key, 2), count)[rank].astype(jnp.int32)


def gaussian(own_key, shape, scale, bound, split=(), kind=jnp.bfloat16):
    result = jax.random.normal(own_key, shape, jnp.float32) * scale
    if len(split) > 0:
        result = steps_of(own_key, shape, split, -0.22, 0.18) * result
    return jnp.clip(result, min=-bound, max=bound).astype(kind)


def setup_inputs(seed: int = 0) -> dict:
    splits = jax.random.split(jax.random.key(seed), 25)
    hidden_in = gaussian(splits[0], (ROWS, ROW_LEN, D), 1.0, 6.0, ((0, 16), (1, 2)))
    enc_states = gaussian(splits[1], (ROWS, ENC_LEN, D), 1.0, 6.0, ((0, 16), (1, 2)))
    segment_ids = draw_segment_ids(jax.random.fold_in(splits[24], 71), 0)
    edit_pass = draw_edit_pass(jax.random.fold_in(splits[24], 71), 0)
    enc_segments = draw_enc_segments(jax.random.fold_in(splits[24], 71), 0)
    target_tokens = plant(jax.random.randint(splits[5], (ROWS, ROW_LEN), 0, VOCAB), jax.random.fold_in(splits[5], 1), 0, VOCAB - 1).astype(jnp.int32)
    placeholder_counts = plant(skewed_ids(splits[6], (ROWS, ROW_LEN), PAIRS, 2), jax.random.fold_in(splits[6], 3), 0, PAIRS - 1).astype(jnp.int32)
    delete_labels = plant(jax.random.randint(splits[7], (ROWS, ROW_LEN), 0, 2), jax.random.fold_in(splits[7], 1), 0, 1).astype(jnp.int32)
    loss_mask = plant((jax.random.randint(splits[8], (ROWS, ROW_LEN), 0, 4) < 3).astype(jnp.int32), jax.random.fold_in(splits[8], 1), 0, 1)
    w_self_qkv = gaussian(splits[9], (D, 3 * D), D ** -0.5, 0.25)
    w_self_out = gaussian(splits[10], (D, D), (max(D // 256, 1)) ** -0.5, 4.0)
    w_cross_q = gaussian(splits[11], (D, D), D ** -0.5, 0.25)
    w_cross_kv = gaussian(splits[12], (D, 2 * D), D ** -0.5, 0.25)
    w_cross_out = gaussian(splits[13], (D, D), (max(D // 256, 1)) ** -0.5, 4.0)
    w_ffn_in = gaussian(splits[14], (D, FF), D ** -0.5, 0.25)
    b_ffn_in = gaussian(splits[15], (FF,), 0.3, 3.0, (), jnp.float32)
    w_ffn_out = gaussian(splits[16], (FF, D), (FF // 4) ** -0.5, 0.25)
    b_ffn_out = gaussian(splits[17], (D,), 0.3, 3.0, (), jnp.float32)
    norm_gains = jnp.clip(1.0 + 0.1 * jax.random.normal(splits[18], (3, D), jnp.float32), 0.5, 1.5)
    norm_shifts = gaussian(splits[19], (3, D), 0.3, 3.0, (), jnp.float32)
    w_vocab = gaussian(splits[20], (VOCAB, D), (D // 8) ** -0.5, 0.75)
    w_pair = gaussian(splits[21], (2 * D, PAIRS), D ** -0.5, 0.25)
    b_pair = gaussian(splits[22], (PAIRS,), 0.5, 3.0, (), jnp.float32)
    w_delete = gaussian(splits[23], (D, 2), (D // 2) ** -0.5, 0.375)
    return dict(hidden_in=hidden_in, enc_states=enc_states, segment_ids=segment_ids, edit_pass=edit_pass, enc_segments=enc_segments, target_tokens=target_tokens, placeholder_counts=placeholder_counts, delete_labels=delete_labels, loss_mask=loss_mask, w_self_qkv=w_self_qkv, w_self_out=w_self_out, w_cross_q=w_cross_q, w_cross_kv=w_cross_kv, w_cross_out=w_cross_out, w_ffn_in=w_ffn_in, b_ffn_in=b_ffn_in, w_ffn_out=w_ffn_out, b_ffn_out=b_ffn_out, norm_gains=norm_gains, norm_shifts=norm_shifts, w_vocab=w_vocab, w_pair=w_pair, b_pair=b_pair, w_delete=w_delete)


@jax.custom_vjp
def low(v):
    return lax.optimization_barrier(v.astype(jnp.bfloat16)).astype(jnp.float32)

@jax.custom_vjp
def low_back(v):
    return v

def low_keep(v):
    return (low(v), None)

def low_pass(kept, grad):
    return (grad,)

def back_keep(v):
    return (v, None)

def back_low(kept, grad):
    return (low(grad),)
low.defvjp(low_keep, low_pass)
low_back.defvjp(back_keep, back_low)
HIGHEST = lax.Precision.HIGHEST
EPSILON = 1e-05
NEGATIVE = -1e+30

def product(left, right):
    return jnp.dot(left, right, precision=HIGHEST, preferred_element_type=jnp.float32)

def rounded(value):
    return low_back(low(value))

def layer_norm(summed, gain_row, shift_row):
    centered = summed - lax.optimization_barrier(jnp.mean(summed, -1, keepdims=True))
    spread = lax.optimization_barrier(jnp.mean(centered * centered, -1, keepdims=True))
    return centered * lax.rsqrt(spread + EPSILON) * gain_row + shift_row

def split_heads(matrix):
    return matrix.reshape(matrix.shape[0], HEADS, HEAD_DIM)

def attention(queries, key_rows, value_rows, allowed):
    scores = jnp.einsum('qhd,khd->hqk', split_heads(queries), split_heads(key_rows), precision=HIGHEST) * HEAD_DIM ** (-0.5)
    scores = low_back(jnp.where(allowed[None], scores, NEGATIVE))
    maximum = lax.optimization_barrier(jnp.max(scores, -1, keepdims=True))
    exponent = jnp.exp(scores - maximum)
    weights = low(exponent / lax.optimization_barrier(jnp.sum(exponent, -1, keepdims=True)))
    mixture = jnp.einsum('hqk,khd->qhd', weights, split_heads(value_rows), precision=HIGHEST)
    return rounded(mixture.reshape(queries.shape[0], HEADS * HEAD_DIM))

def cross_entropy(logits, labels):
    maximum = lax.optimization_barrier(jnp.max(logits, -1, keepdims=True))
    partition = maximum[:, 0] + jnp.log(lax.optimization_barrier(jnp.sum(jnp.exp(logits - maximum), -1)))
    picked = jnp.take_along_axis(logits, labels[:, None], 1)[:, 0]
    return partition - picked

def row_loss(weights, hidden, encoded, segment, passes, enc_segment, target, counts, labels, keep_mask):
    w_self_qkv, w_self_out, w_cross_q, w_cross_kv, w_cross_out, w_ffn_in, b_ffn_in, w_ffn_out, b_ffn_out, norm_gains, norm_shifts, w_vocab, w_pair, b_pair, w_delete = weights
    self_qkv = rounded(product(hidden, w_self_qkv))
    self_allowed = segment[:, None] == segment[None, :]
    self_mix = attention(self_qkv[:, :D], self_qkv[:, D:2 * D], self_qkv[:, 2 * D:], self_allowed)
    layer_one = layer_norm(hidden + low_back(product(self_mix, w_self_out)), norm_gains[0], norm_shifts[0])
    cross_query = rounded(product(low(layer_one), w_cross_q))
    source_kv = rounded(product(encoded, w_cross_kv))
    cross_allowed = segment[:, None] == enc_segment[None, :]
    cross_mix = attention(cross_query, source_kv[:, :D], source_kv[:, D:], cross_allowed)
    layer_two = layer_norm(layer_one + low_back(product(cross_mix, w_cross_out)), norm_gains[1], norm_shifts[1])
    pre_act = low_back(product(low(layer_two), w_ffn_in) + b_ffn_in)
    activ = low(jax.nn.gelu(pre_act, approximate=True))
    layer_three = layer_norm(layer_two + low_back(product(activ, w_ffn_out) + b_ffn_out), norm_gains[2], norm_shifts[2])
    head_in = low(layer_three)
    length = hidden.shape[0]
    position = jnp.arange(length, dtype=jnp.int32)
    follow = jnp.concatenate([head_in[1:], jnp.zeros((1, D), head_in.dtype)], 0)
    follow_seg = jnp.concatenate([segment[1:], segment[:1]], 0)
    pair_ok = (follow_seg == segment) & (position < length - 1)
    keep_float = keep_mask.astype(head_in.dtype)
    delete_keep = keep_float * (passes == 0).astype(head_in.dtype)
    pair_keep = keep_float * ((passes == 1) & pair_ok).astype(head_in.dtype)
    token_keep = keep_float * (passes == 2).astype(head_in.dtype)
    delete_loss = cross_entropy(low_back(product(head_in, w_delete)), labels)
    pair_loss = cross_entropy(low_back(product(jnp.concatenate([head_in, follow], 1), w_pair) + b_pair), counts)
    token_loss = cross_entropy(low_back(product(head_in, w_vocab.T)), target)
    summed = jnp.sum(delete_keep * delete_loss + pair_keep * pair_loss + token_keep * token_loss)
    return (summed, layer_three)

def reference(hidden_in, enc_states, segment_ids, edit_pass, enc_segments, target_tokens, placeholder_counts, delete_labels, loss_mask, w_self_qkv, w_self_out, w_cross_q, w_cross_kv, w_cross_out, w_ffn_in, b_ffn_in, w_ffn_out, b_ffn_out, norm_gains, norm_shifts, w_vocab, w_pair, b_pair, w_delete):
    floats = tuple((array.astype(jnp.float32) for array in (hidden_in, enc_states, w_self_qkv, w_self_out, w_cross_q, w_cross_kv, w_cross_out, w_ffn_in, b_ffn_in, w_ffn_out, b_ffn_out, norm_gains, norm_shifts, w_vocab, w_pair, b_pair, w_delete)))

    def forward(hidden, encoded, *weights):

        def scan_step(running, members):
            row_total, row_out = jax.checkpoint(row_loss)(weights, *members)
            return (running + row_total, row_out)
        return lax.scan(scan_step, jnp.zeros((), jnp.float32), (hidden, encoded, segment_ids, edit_pass, enc_segments, target_tokens, placeholder_counts, delete_labels, loss_mask))
    summed, pullback, outputs = jax.vjp(forward, *floats, has_aux=True)
    gradient = pullback(jnp.ones((), summed.dtype))
    return (outputs.astype(jnp.bfloat16), gradient[0], gradient[1], gradient[2], gradient[3], gradient[4], gradient[5], gradient[6], gradient[7], gradient[8], gradient[9], gradient[10], gradient[11], gradient[12], gradient[13], gradient[14], gradient[15], gradient[16])
```

```python
import functools

import jax
import jax.numpy as jnp
from jax import lax
from jax.experimental import pallas as pl
from jax.experimental.pallas import tpu as pltpu
from jax.sharding import PartitionSpec as P

HEADS = 8
HEAD_DIM = 64
LANES = 128
SCALE = HEAD_DIM**-0.5
EPSILON = 1e-05
NEGATIVE = -1e30
TILE = 256
VMEM_LIMIT = 56 * 1024 * 1024

SEQ_BIT, CORE_BIT, NEAR_BIT = 1, 2, 4
GROUP = 8

bf16 = jnp.bfloat16
f32 = jnp.float32


def matmul(left, right):
    return jnp.dot(left, right, preferred_element_type=f32)


def matmul_left(left, right):
    return lax.dot_general(left, right, (((0,), (0,)), ((), ())), preferred_element_type=f32)


def matmul_right(left, right):
    return lax.dot_general(left, right, (((1,), (1,)), ((), ())), preferred_element_type=f32)


def smooth_gate(value):
    return jax.nn.gelu(value, approximate=True)


def norm_forward(summed, gain_row, shift_row):
    centered = summed - jnp.mean(summed, -1, keepdims=True)
    invert = lax.rsqrt(jnp.mean(centered * centered, -1, keepdims=True) + EPSILON)
    normed = centered * invert
    return (normed * gain_row + shift_row, normed, invert)


def norm_backward(upstream, normed, invert, gain_row):
    scaled = upstream * gain_row
    centered = (
        scaled
        - jnp.mean(scaled, -1, keepdims=True)
        - normed * jnp.mean(scaled * normed, -1, keepdims=True)
    )
    return (centered * invert, jnp.sum(upstream * normed, 0), jnp.sum(upstream, 0))


def passed_along(value, axis, steps):
    count = lax.axis_size(axis)
    leading, last = (max(0, -steps), min(count, count - steps))
    return lax.ppermute(value, axis, [(source, source + steps) for source in range(leading, last)])


def place():
    return lax.axis_index("dp") * 2 + lax.axis_index("seq")


def swapped(value, mask):
    count = lax.axis_size("dp") * lax.axis_size("seq")
    return lax.ppermute(value, ("dp", "seq"), [(i, i ^ mask) for i in range(count)])


def far_bits():
    count = lax.axis_size("dp") * lax.axis_size("seq")
    bits = []
    bit = GROUP
    while bit < count:
        bits.append(bit)
        bit *= 2
    return bits


def summed_over_all(value, masks):
    me = place()
    for mask in masks:
        half = value.shape[0] // 2
        upper = ((me & mask) != 0).astype(jnp.int32)
        keep = lax.dynamic_slice_in_dim(value, upper * half, half)
        send = lax.dynamic_slice_in_dim(value, (1 - upper) * half, half)
        value = (keep.astype(f32) + swapped(send, mask).astype(f32)).astype(bf16)
    for mask in reversed(masks):
        other = swapped(value, mask)
        value = jnp.where(
            (me & mask) != 0,
            jnp.concatenate([other, value], 0),
            jnp.concatenate([value, other], 0),
        )
    return value


def kernel_call(body, grid, in_specs, out_specs, out_shape, scratch, flops, prefetch=0):
    return pl.pallas_call(
        body,
        grid_spec=pltpu.PrefetchScalarGridSpec(
            num_scalar_prefetch=prefetch,
            grid=grid,
            in_specs=in_specs,
            out_specs=out_specs,
            scratch_shapes=scratch,
        ),
        out_shape=out_shape,
        compiler_params=pltpu.CompilerParams(vmem_limit_bytes=VMEM_LIMIT),
        cost_estimate=pl.CostEstimate(flops=flops, bytes_accessed=8 << 20, transcendentals=0),
    )


def dot_nt(left, right):
    return lax.dot_general(left, right, (((1,), (1,)), ((), ())), preferred_element_type=f32)


def dot_tn(left, right):
    return lax.dot_general(left, right, (((0,), (0,)), ((), ())), preferred_element_type=f32)


def head_lanes(shape, head):
    lane = lax.broadcasted_iota(jnp.int32, shape, 1)
    return (lane >= HEAD_DIM) == (head == 1)


def attend_body(q_ref, ko_ref, kr_ref, vo_ref, vr_ref, sq_ref, so_ref, sr_ref, out_ref, lse_ref, stat):
    pair = pl.program_id(0)
    rows = q_ref.shape[0]

    @pl.when(pair == 0)
    def _():
        stat[...] = jnp.zeros_like(stat)

    for start in range(0, rows, TILE):
        part = pl.ds(start, TILE)
        queries = q_ref[part, :].astype(f32) * SCALE
        same_own = sq_ref[part, :] == so_ref[...]
        same_far = sq_ref[part, :] == sr_ref[...]
        lane = lax.broadcasted_iota(jnp.int32, (TILE, LANES), 1)
        mixed = None
        kept = stat[part, :]
        for head in range(2):
            masked = jnp.where(head_lanes((TILE, LANES), head), queries, 0.0).astype(bf16)
            s_own = jnp.where(same_own, dot_nt(masked, ko_ref[...]), NEGATIVE)
            s_far = jnp.where(same_far, dot_nt(masked, kr_ref[...]), NEGATIVE)
            top = jnp.maximum(
                jnp.max(s_own, 1, keepdims=True), jnp.max(s_far, 1, keepdims=True)
            )
            e_own = jnp.exp(s_own - top)
            e_far = jnp.exp(s_far - top)
            total = jnp.sum(e_own, 1, keepdims=True) + jnp.sum(e_far, 1, keepdims=True)
            mix = matmul(e_own.astype(bf16), vo_ref[...]) + matmul(e_far.astype(bf16), vr_ref[...])
            mix = mix / total
            kept = jnp.where(lane == 2 * pair + head, top + jnp.log(total), kept)
            mixed = mix if head == 0 else jnp.where(lane < HEAD_DIM, mixed, mix)
        out_ref[part, :] = mixed.astype(bf16)
        stat[part, :] = kept

    @pl.when(pair == HEADS // 2 - 1)
    def _():
        lse_ref[...] = jnp.transpose(stat[...])[:HEADS, :]


def attend(query, q_at, own, ko_at, vo_at, far, kr_at, vr_at, seg_q, seg_own, seg_far):
    rows, keys = query.shape[0], own.shape[0]
    pick = lambda n, at: pl.BlockSpec((n, LANES), lambda h, at=at: (0, at + h))
    whole = lambda *shape: pl.BlockSpec(shape, lambda h: (0, 0))
    return kernel_call(
        attend_body,
        (HEADS // 2,),
        [
            pick(rows, q_at),
            pick(keys, ko_at),
            pick(keys, kr_at),
            pick(keys, vo_at),
            pick(keys, vr_at),
            whole(rows, 1),
            whole(1, keys),
            whole(1, keys),
        ],
        [pick(rows, 0), whole(HEADS, rows)],
        [
            jax.ShapeDtypeStruct((rows, HEADS * HEAD_DIM), bf16),
            jax.ShapeDtypeStruct((HEADS, rows), f32),
        ],
        [pltpu.VMEM((rows, LANES), f32)],
        16 * rows * keys * 512,
    )(query, own, far, own, far, seg_q.reshape(rows, 1), seg_own.reshape(1, keys), seg_far.reshape(1, keys))


def attend_back_body(
    q_ref, g_ref, o_ref, lse_ref, ko_ref, kr_ref, vo_ref, vr_ref, sq_ref, so_ref, sr_ref,
    dq_ref, dko_ref, dvo_ref, dkr_ref, dvr_ref,
):
    rows = q_ref.shape[0]
    keys = ko_ref.shape[0]
    queries = q_ref[...].astype(f32) * SCALE
    upstream = g_ref[...].astype(f32)
    which = lax.broadcasted_iota(jnp.int32, (8, LANES), 0)
    lane = lax.broadcasted_iota(jnp.int32, (8, LANES), 1)
    chooser = jnp.where((lane >= HEAD_DIM) == (which == 1), 1.0, 0.0).astype(f32)
    along = lax.dot_general(
        chooser,
        upstream * o_ref[...].astype(f32),
        (((1,), (1,)), ((), ())),
        precision=lax.Precision.HIGHEST,
        preferred_element_type=f32,
    )
    q_of = [jnp.where(head_lanes((rows, LANES), h), queries, 0.0).astype(bf16) for h in range(2)]
    g_of = [jnp.where(head_lanes((rows, LANES), h), upstream, 0.0).astype(bf16) for h in range(2)]
    dq_of = [jnp.zeros((HEAD_DIM, rows), f32) for _ in range(2)]
    for k_ref, v_ref, s_ref, dk_ref, dv_ref in (
        (ko_ref, vo_ref, so_ref, dko_ref, dvo_ref),
        (kr_ref, vr_ref, sr_ref, dkr_ref, dvr_ref),
    ):
        for start in range(0, keys, TILE):
            part = pl.ds(start, TILE)
            key, value = k_ref[part, :], v_ref[part, :]
            same = s_ref[part, :] == sq_ref[...]
            key_t = jnp.transpose(key.astype(f32)).astype(bf16)
            dk = dv = None
            for h in range(2):
                scores = jnp.where(same, dot_nt(key, q_of[h]), NEGATIVE)
                weights = jnp.exp(scores - lse_ref[0, h : h + 1, :])
                back = dot_nt(value, g_of[h])
                grad = (weights * (back - along[h : h + 1, :])).astype(bf16)
                dv_h = matmul(weights.astype(bf16), g_of[h])
                dk_h = matmul(grad, q_of[h])
                dv = dv_h if dv is None else dv + dv_h
                dk = dk_h if dk is None else dk + dk_h
                dq_of[h] += matmul(key_t[h * HEAD_DIM : (h + 1) * HEAD_DIM, :], grad)
            dk_ref[part, :] = dk.astype(bf16)
            dv_ref[part, :] = dv.astype(bf16)
    dq = jnp.concatenate(dq_of, 0)
    dq_ref[...] = (jnp.transpose(dq) * SCALE).astype(bf16)


def attend_back(query, q_at, upstream, mixed, lse, own, ko_at, vo_at, far, kr_at, vr_at, seg_q, seg_own, seg_far):
    rows, keys = query.shape[0], own.shape[0]
    pick = lambda n, at: pl.BlockSpec((n, LANES), lambda h, at=at: (0, at + h))
    whole = lambda *shape: pl.BlockSpec(shape, lambda h: (0, 0))
    width = HEADS * HEAD_DIM
    return kernel_call(
        attend_back_body,
        (HEADS // 2,),
        [
            pick(rows, q_at),
            pick(rows, 0),
            pick(rows, 0),
            pl.BlockSpec((1, 2, rows), lambda h: (h, 0, 0)),
            pick(keys, ko_at),
            pick(keys, kr_at),
            pick(keys, vo_at),
            pick(keys, vr_at),
            whole(1, rows),
            whole(keys, 1),
            whole(keys, 1),
        ],
        [pick(rows, 0)] + [pick(keys, 0)] * 4,
        [jax.ShapeDtypeStruct((rows, width), bf16)] + [jax.ShapeDtypeStruct((keys, width), bf16)] * 4,
        [],
        40 * rows * keys * 512,
    )(
        query, upstream, mixed, lse.reshape(HEADS // 2, 2, rows), own, far, own, far,
        seg_q.reshape(1, rows), seg_own.reshape(keys, 1), seg_far.reshape(keys, 1),
    )


def vocab_body(info, a_ref, b_ref, ta_ref, tb_ref, w_ref, e_ref, top_ref, sum_ref, all_ref, tall_ref, logits):
    step = pl.program_id(0)
    chunk = 128

    @pl.when(step == 0)
    def _():
        all_ref[...] = jnp.zeros_like(all_ref)
        tall_ref[...] = jnp.zeros_like(tall_ref)
        for rel in range(GROUP):
            core, near = rel // 4, rel % 4
            block = (core | (near << 1)) ^ info[17]
            count, offset = info[block], info[8 + block]
            src, tsrc = (a_ref, ta_ref) if core == 0 else (b_ref, tb_ref)
            for start in range(0, src.shape[1], chunk):

                @pl.when(start < count)
                def _(src=src, tsrc=tsrc, near=near, start=start, offset=offset):
                    to = pl.ds(pl.multiple_of(offset + start, 16), chunk)
                    all_ref[to, :] += src[near, start : start + chunk, :]
                    tall_ref[to, :] += tsrc[near, start : start + chunk, :]

    @pl.when(step * TILE < info[16])
    def _():
        hidden = all_ref[pl.ds(pl.multiple_of(step * TILE, TILE), TILE), :]
        wide = w_ref.shape[1]
        piece = min(1024, wide)
        top = None
        for start in range(0, wide, piece):
            value = matmul(hidden, w_ref[:, start : start + piece])
            logits[:, start : start + piece] = value
            most = jnp.max(value, 1, keepdims=True)
            top = most if top is None else jnp.maximum(top, most)
        total = None
        for start in range(0, wide, piece):
            value = jnp.exp(logits[:, start : start + piece] - top)
            added = jnp.sum(value, 1, keepdims=True)
            total = added if total is None else total + added
            e_ref[:, start : start + piece] = value.astype(bf16)
        top_ref[...] = top
        sum_ref[...] = total


def last_active(i, info):
    return jnp.minimum(i, jnp.maximum((info[16] + TILE - 1) // TILE - 1, 0))


def vocab_forward(info, a, b, ta, tb, w_t):
    near, rows, width = a.shape
    total = GROUP * rows
    wide = w_t.shape[1]
    once = lambda *shape: pl.BlockSpec(
        shape, lambda i, info: (0,) * len(shape), pipeline_mode=pl.Buffered(1)
    )
    tile = lambda n: pl.BlockSpec((TILE, n), lambda i, info: (last_active(i, info), 0))
    return kernel_call(
        vocab_body,
        (total // TILE,),
        [once(near, rows, width), once(near, rows, width), once(near, rows, 1), once(near, rows, 1), once(width, wide)],
        [tile(wide), tile(1), tile(1), once(total, width), once(total, 1)],
        [
            jax.ShapeDtypeStruct((total, wide), bf16),
            jax.ShapeDtypeStruct((total, 1), f32),
            jax.ShapeDtypeStruct((total, 1), f32),
            jax.ShapeDtypeStruct((total, width), bf16),
            jax.ShapeDtypeStruct((total, 1), jnp.int32),
        ],
        [pltpu.VMEM((TILE, wide), f32)],
        1400 * wide * width * 2,
        prefetch=1,
    )(info, a, b, ta, tb, w_t)


def vocab_back_body(info, e_ref, w_ref, out_ref):
    @pl.when(pl.program_id(0) * TILE < info[16])
    def _():
        out_ref[...] = matmul(e_ref[...], w_ref[...]).astype(bf16)


def vocab_back(info, e, w):
    total, wide = e.shape
    width = w.shape[1]
    tile = lambda n: pl.BlockSpec((TILE, n), lambda i, info: (last_active(i, info), 0))
    return kernel_call(
        vocab_back_body,
        (total // TILE,),
        [tile(wide), pl.BlockSpec((wide, width), lambda i, info: (0, 0), pipeline_mode=pl.Buffered(1))],
        tile(width),
        jax.ShapeDtypeStruct((total, width), bf16),
        [],
        1400 * wide * width * 2,
        prefetch=1,
    )(info, e, w)


def spread_body(core, info, g_ref, f_ref, out_ref):
    near = pl.program_id(0)
    block = (core | (near << 1)) ^ info[17]
    rows = out_ref.shape[1]
    at = pl.multiple_of(info[8 + block], 16)
    row = lax.broadcasted_iota(jnp.int32, (rows, 1), 0)
    value = g_ref[pl.ds(at, rows), :].astype(f32) * f_ref[pl.ds(at, rows), :]
    out_ref[0] = jnp.where(row < info[block], value, 0.0).astype(bf16)


def spread(core, info, g, factor, rows):
    total, width = g.shape
    once = lambda *shape: pl.BlockSpec(
        shape, lambda i, info: (0,) * len(shape), pipeline_mode=pl.Buffered(1)
    )
    return kernel_call(
        functools.partial(spread_body, core),
        (GROUP // 2,),
        [once(total, width), once(total, 1)],
        pl.BlockSpec((1, rows, width), lambda i, info: (i, 0, 0)),
        jax.ShapeDtypeStruct((GROUP // 2, rows, width), bf16),
        [],
        total * width,
        prefetch=1,
    )(info, g, factor)


def vocab_grad_body(info, e_ref, h_ref, t_ref, f_ref, out_ref, total):
    step = pl.program_id(0)

    @pl.when(step == 0)
    def _():
        total[...] = jnp.zeros_like(total)

    @pl.when(step * TILE < info[16])
    def _():
        wide = e_ref.shape[1]
        piece = min(1024, wide)
        for start in range(0, wide, piece):
            column = start + 1 + lax.broadcasted_iota(jnp.int32, (TILE, piece), 1)
            weights = e_ref[:, start : start + piece].astype(f32) * f_ref[...]
            weights = (weights - jnp.where(column == t_ref[...], 1.0, 0.0)).astype(bf16)
            total[start : start + piece, :] += dot_tn(weights, h_ref[...])

    @pl.when(step == pl.num_programs(0) - 1)
    def _():
        out_ref[...] = total[...].astype(bf16)


def vocab_grad(info, e, hidden, target, factor):
    total, wide = e.shape
    width = hidden.shape[1]
    tile = lambda n: pl.BlockSpec((TILE, n), lambda i, info: (last_active(i, info), 0))
    return kernel_call(
        vocab_grad_body,
        (total // TILE,),
        [tile(wide), tile(width), tile(1), tile(1)],
        pl.BlockSpec((wide, width), lambda i, info: (0, 0)),
        jax.ShapeDtypeStruct((wide, width), bf16),
        [pltpu.VMEM((wide, width), f32)],
        1400 * wide * width * 2,
        prefetch=1,
    )(info, e, hidden, target, factor)


def line_summed(value):
    outer = lax.axis_size("dp") // 4
    mine = lax.axis_index("dp") // 4
    both = 2 * lax.axis_size("dp")
    step_size = GROUP

    def block(at):
        return lax.dynamic_index_in_dim(value, jnp.clip(at, 0, outer - 1), 0, keepdims=False).astype(f32)

    up = down = None
    for step in range(1, outer):
        left = outer - step
        send_up, send_down = block(mine + left), block(mine - left)
        if up is not None:
            send_up, send_down = send_up + up.astype(f32), send_down + down.astype(f32)
        up = lax.ppermute(
            send_up.astype(bf16),
            ("dp", "seq"),
            [(i, i + step_size) for i in range(both) if i // step_size <= min(step - 1, outer - 2)],
        )
        down = lax.ppermute(
            send_down.astype(bf16),
            ("dp", "seq"),
            [(i, i - step_size) for i in range(both) if i // step_size >= max(left, 1)],
        )
    return block(mine) + up.astype(f32) + down.astype(f32)


def per_device(
    hidden_in,
    enc_states,
    segment_ids,
    edit_pass,
    enc_segments,
    target_tokens,
    placeholder_counts,
    delete_labels,
    loss_mask,
    w_self_qkv,
    w_self_out,
    w_cross_q,
    w_cross_kv,
    w_cross_out,
    w_ffn_in,
    b_ffn_in,
    w_ffn_out,
    b_ffn_out,
    norm_gains,
    norm_shifts,
    w_vocab,
    w_pair,
    b_pair,
    w_delete,
):
    _, tokens, features = hidden_in.shape
    me = place()
    seq = lax.axis_index("seq")
    dp = lax.axis_index("dp")
    far = far_bits()
    hidden = hidden_in[0]
    source = enc_states[0]
    hidden_far = swapped(hidden, SEQ_BIT)
    source_far = swapped(source, SEQ_BIT)
    segment, passes, source_seg = segment_ids[0], edit_pass[0], enc_segments[0]
    segs_far = swapped(jnp.stack([segment, source_seg]), SEQ_BIT)
    segment_far, source_seg_far = segs_far[0], segs_far[1]

    keep_float = loss_mask[0].astype(f32)
    token_keep = keep_float * (passes == 2).astype(f32)
    row = lax.broadcasted_iota(jnp.int32, (tokens, tokens), 0)
    col = lax.broadcasted_iota(jnp.int32, (tokens, tokens), 1)
    rank = matmul(token_keep.astype(bf16)[None, :], (row <= col).astype(bf16)) - 1.0
    selects = (rank.astype(jnp.int32) == row) & (token_keep[None, :] > 0)
    chooser = selects.astype(bf16)
    targets = target_tokens[0]
    chosen = jnp.sum(jnp.where(selects, targets[None, :] + 1, 0), 1)
    near = lambda v: jnp.stack(
        [v, swapped(v, NEAR_BIT), swapped(v, SEQ_BIT), swapped(v, NEAR_BIT | SEQ_BIT)]
    )
    chosen_a = near(chosen)
    chosen_b = swapped(chosen_a, CORE_BIT)

    vocab = w_vocab.shape[0]
    outer = lax.axis_size("dp") // 4
    block = vocab // (outer * GROUP)
    inner = (dp % 4) * 2 + seq
    here = (dp % 4) + 4 * seq
    w_here = lax.dynamic_index_in_dim(
        w_vocab.reshape(outer, GROUP, block, features), inner, 1, keepdims=False
    ).reshape(outer * block, features)
    w_here_t = jnp.transpose(w_here)

    def local_target(value):
        index = value - 1
        mine = (value > 0) & ((index // block) % GROUP == inner)
        return jnp.where(mine, (index // (block * GROUP)) * block + index % block + 1, 0)[..., None]

    counts_rel = jnp.sum((jnp.concatenate([chosen_a, chosen_b]) > 0).astype(jnp.int32), 1)
    relative = jnp.array([c | (n << 1) for c in range(2) for n in range(4)], jnp.int32) ^ here
    counts = jnp.sum(
        jnp.where(relative[:, None] == jnp.arange(GROUP)[None, :], counts_rel[:, None], 0), 0
    )
    rounded = (counts + 15) // 16 * 16
    before = jnp.arange(GROUP)[:, None] < jnp.arange(GROUP)[None, :]
    offsets = jnp.sum(jnp.where(before, rounded[:, None], 0), 0)
    info = jnp.concatenate([counts, offsets, jnp.sum(rounded)[None], here[None]]).astype(jnp.int32)

    qkv = matmul(hidden, w_self_qkv).astype(bf16)
    kv_far = matmul(hidden_far, w_self_qkv[:, features:]).astype(bf16)
    ckv = matmul(source, w_cross_kv).astype(bf16)
    ckv_far = matmul(source_far, w_cross_kv).astype(bf16)
    self_mix, self_lse = attend(qkv, 0, qkv, 4, 8, kv_far, 0, 4, segment, segment, segment_far)
    layer_one, normed_one, invert_one = norm_forward(
        hidden.astype(f32) + matmul(self_mix, w_self_out), norm_gains[0], norm_shifts[0]
    )
    one_low = layer_one.astype(bf16)
    cross_query = matmul(one_low, w_cross_q).astype(bf16)
    cross_mix, cross_lse = attend(
        cross_query, 0, ckv, 0, 4, ckv_far, 0, 4, segment, source_seg, source_seg_far
    )
    layer_two, normed_two, invert_two = norm_forward(
        layer_one + matmul(cross_mix, w_cross_out), norm_gains[1], norm_shifts[1]
    )
    two_low = layer_two.astype(bf16)
    pre_act = matmul(two_low, w_ffn_in) + b_ffn_in
    activ, gate_back = jax.vjp(smooth_gate, pre_act)
    activ_low = activ.astype(bf16)
    layer_three, normed_three, invert_three = norm_forward(
        layer_two + (matmul(activ_low, w_ffn_out) + b_ffn_out), norm_gains[2], norm_shifts[2]
    )
    three_low = layer_three.astype(bf16)

    kept_a = near(matmul(chooser, three_low).astype(bf16))
    kept_b = swapped(kept_a, CORE_BIT)
    e, top, total, kept_all, target_all = vocab_forward(
        info, kept_a, kept_b, local_target(chosen_a), local_target(chosen_b), w_here_t
    )
    back_raw = vocab_back(info, e, w_here)
    stats = jnp.stack([top[:, 0], total[:, 0]])

    def merged(first, *others):
        most = functools.reduce(jnp.maximum, [o[0] for o in others], first[0])
        added = sum((o[1] * jnp.exp(o[0] - most) for o in others), first[1] * jnp.exp(first[0] - most))
        return jnp.stack([most, added])

    stats_pair = merged(stats, swapped(stats, CORE_BIT))
    stats_all = merged(
        stats_pair,
        swapped(stats_pair, NEAR_BIT),
        swapped(stats_pair, SEQ_BIT),
        swapped(stats_pair, NEAR_BIT | SEQ_BIT),
    )
    factor = jnp.exp(stats[0] - stats_all[0] - jnp.log(stats_all[1]))[:, None]
    back_b = spread(1, info, back_raw, factor, tokens)
    back_far = swapped(back_b, CORE_BIT)
    back_a = spread(0, info, back_raw, factor, tokens)
    back_sum = back_a.astype(f32) + back_far.astype(f32)
    back_low = back_sum.astype(bf16)
    head_back = (
        back_sum[0]
        + swapped(back_low[1], NEAR_BIT).astype(f32)
        + swapped(back_low[2], SEQ_BIT).astype(f32)
        + swapped(back_low[3], NEAR_BIT | SEQ_BIT).astype(f32)
    )
    vocab_part = vocab_grad(info, e, kept_all, target_all, factor)
    d_vocab = line_summed(vocab_part.reshape(outer, block, features))
    target_rows = jnp.take(w_vocab, targets, axis=0).astype(f32)

    position = seq * tokens + jnp.arange(tokens, dtype=jnp.int32)
    row_length = tokens * lax.axis_size("seq")
    next_row = passed_along(three_low[:1], "seq", -1)
    follow = jnp.concatenate([three_low[1:], next_row], 0)
    follow_seg = jnp.concatenate([segment[1:], segment_far[:1]], 0)
    pair_ok = (follow_seg == segment) & (position < row_length - 1)
    delete_keep = keep_float * (passes == 0).astype(f32)
    pair_keep = keep_float * (passes == 1).astype(f32) * pair_ok.astype(f32)
    pair_logits = matmul(three_low, w_pair[:features]) + matmul(follow, w_pair[features:]) + b_pair

    def label_grad(logits, labels, keep_mask):
        shifted = logits - jnp.max(logits, -1, keepdims=True)
        exponent = jnp.exp(shifted)
        weights = exponent / jnp.sum(exponent, -1, keepdims=True)
        onehot = labels[:, None] == lax.broadcasted_iota(jnp.int32, logits.shape, 1)
        return ((weights - onehot.astype(f32)) * keep_mask[:, None]).astype(bf16)

    pair_grad = label_grad(pair_logits, placeholder_counts[0], pair_keep)
    d_pair = jnp.concatenate([matmul_left(three_low, pair_grad), matmul_left(follow, pair_grad)], 1)
    d_b_pair = jnp.sum(pair_grad.astype(f32), 0)
    follow_grad = matmul_right(pair_grad, w_pair[features:])
    back_row = passed_along(follow_grad[-1:], "seq", 1)
    delete_grad = label_grad(matmul(three_low, w_delete), delete_labels[0], delete_keep)
    d_delete = matmul_left(delete_grad, three_low)
    grad_local = (
        matmul_right(pair_grad, w_pair[:features])
        + jnp.concatenate([back_row, follow_grad[:-1]], 0)
        + matmul_right(delete_grad, w_delete)
        - target_rows * token_keep[:, None]
    )

    grad_three = grad_local + matmul_left(chooser, head_back.astype(bf16))
    grad_sum3, gain_three, shift_three = norm_backward(
        grad_three, normed_three, invert_three, norm_gains[2]
    )
    branch_three = grad_sum3.astype(bf16)
    d_ffn_out = matmul_left(activ_low, branch_three).astype(bf16)
    d_b_ffn_out = jnp.sum(branch_three.astype(f32), 0)
    grad_pre = gate_back(matmul_right(branch_three, w_ffn_out))[0].astype(bf16)
    d_ffn_in = matmul_left(two_low, grad_pre).astype(bf16)
    d_b_ffn_in = jnp.sum(grad_pre.astype(f32), 0)
    grad_two = grad_sum3 + matmul_right(grad_pre, w_ffn_in)
    grad_sum2, gain_two, shift_two = norm_backward(grad_two, normed_two, invert_two, norm_gains[1])
    branch_two = grad_sum2.astype(bf16)
    d_cross_out = matmul_left(cross_mix, branch_two).astype(bf16)
    cross_up = matmul_right(branch_two, w_cross_out).astype(bf16)
    dcq, dck, dcv, dck_far, dcv_far = attend_back(
        cross_query, 0, cross_up, cross_mix, cross_lse, ckv, 0, 4, ckv_far, 0, 4,
        segment, source_seg, source_seg_far,
    )
    d_cross_q = matmul_left(one_low, dcq).astype(bf16)
    dckv = jnp.concatenate([dck, dcv], 1)
    dckv_far = jnp.concatenate([dck_far, dcv_far], 1)
    d_enc_far = swapped(matmul_right(dckv_far, w_cross_kv).astype(bf16), SEQ_BIT)
    d_enc = matmul_right(dckv, w_cross_kv) + d_enc_far.astype(f32)
    d_cross_kv = (matmul_left(source, dckv) + matmul_left(source_far, dckv_far)).astype(bf16)
    grad_one = grad_sum2 + matmul_right(dcq, w_cross_q)
    grad_sum1, gain_one, shift_one = norm_backward(grad_one, normed_one, invert_one, norm_gains[0])
    branch_one = grad_sum1.astype(bf16)
    d_self_out = matmul_left(self_mix, branch_one).astype(bf16)
    self_up = matmul_right(branch_one, w_self_out).astype(bf16)
    dq, dk, dv, dk_far, dv_far = attend_back(
        qkv, 0, self_up, self_mix, self_lse, qkv, 4, 8, kv_far, 0, 4, segment, segment, segment_far
    )
    dqkv = jnp.concatenate([dq, dk, dv], 1)
    dkv_far = jnp.concatenate([dk_far, dv_far], 1)
    d_hidden_far = swapped(matmul_right(dkv_far, w_self_qkv[:, features:]).astype(bf16), SEQ_BIT)
    d_hidden = grad_sum1 + matmul_right(dqkv, w_self_qkv) + d_hidden_far.astype(f32)
    d_self_qkv = jnp.concatenate(
        [
            matmul_left(hidden, dq),
            matmul_left(hidden, dqkv[:, features:]) + matmul_left(hidden_far, dkv_far),
        ],
        1,
    ).astype(bf16)

    small = jnp.concatenate(
        [
            d_b_ffn_in,
            d_b_ffn_out,
            gain_one,
            gain_two,
            gain_three,
            shift_one,
            shift_two,
            shift_three,
            d_b_pair,
            d_delete.reshape(-1),
        ]
    )
    small_size = small.shape[0]
    small_cols = -(-small_size // (features * LANES)) * LANES
    small = jnp.pad(small, (0, features * small_cols - small_size)).reshape(small_cols, features)
    small = jnp.transpose(small).astype(bf16)

    sum_out = summed_over_all(d_ffn_out, [CORE_BIT, NEAR_BIT, SEQ_BIT] + far)
    sum_in = summed_over_all(
        jnp.concatenate([d_ffn_in, d_pair.astype(bf16)], 1), [CORE_BIT, SEQ_BIT, NEAR_BIT] + far
    )
    sum_mid = summed_over_all(
        jnp.concatenate([d_cross_out, d_cross_q, d_cross_kv, d_self_out, small], 1),
        [CORE_BIT, NEAR_BIT, SEQ_BIT] + far,
    )
    sum_qkv = summed_over_all(d_self_qkv, [CORE_BIT, SEQ_BIT, NEAR_BIT] + far).astype(f32)
    hidden_units = w_ffn_in.shape[1]
    pair_count = w_pair.shape[1]
    sum_in = sum_in.astype(f32)
    sum_pair = sum_in[:, hidden_units:]
    sum_mid = sum_mid.astype(f32)
    flat = jnp.transpose(sum_mid[:, 5 * features :]).reshape(-1)
    at = [0]

    def taken(size):
        at[0] += size
        return flat[at[0] - size : at[0]]

    out_b_ffn_in = taken(hidden_units)
    out_b_ffn_out = taken(features)
    out_gains = taken(3 * features).reshape(3, features)
    out_shifts = taken(3 * features).reshape(3, features)
    out_b_pair = taken(pair_count)
    out_delete = jnp.transpose(taken(2 * features).reshape(2, features))
    return (
        three_low[None],
        d_hidden[None],
        d_enc[None],
        sum_qkv,
        sum_mid[:, 4 * features : 5 * features],
        sum_mid[:, features : 2 * features],
        sum_mid[:, 2 * features : 4 * features],
        sum_mid[:, :features],
        sum_in[:, :hidden_units],
        out_b_ffn_in,
        sum_out.astype(f32),
        out_b_ffn_out,
        out_gains,
        out_shifts,
        d_vocab,
        jnp.concatenate([sum_pair[:, :pair_count], sum_pair[:, pair_count:]], 0),
        out_b_pair,
        out_delete,
    )


def solution(mesh):
    split = P("dp", "seq", None)
    ids = P("dp", "seq")
    return jax.shard_map(
        per_device,
        mesh=mesh,
        in_specs=(split, split) + (ids,) * 7 + (P(),) * 15,
        out_specs=(split,) * 3 + (P(),) * 11 + (P(("dp", "seq"), None),) + (P(),) * 3,
        check_vma=False,
    )
```

```python
import functools

import jax
import jax.numpy as jnp
from jax import lax
from jax.experimental import pallas as pl
from jax.experimental.pallas import tpu as pltpu
from jax.sharding import Mesh
from jax.sharding import PartitionSpec as P

HEADS = 8
HEAD_DIM = 64
LANES = 128
SCALE = HEAD_DIM**-0.5
EPSILON = 1e-05
NEGATIVE = -1e30
TILE = 256

SEQ_BIT, CORE_BIT, NEAR_BIT = 1, 2, 4
GROUP = 8

bf16 = jnp.bfloat16
f32 = jnp.float32


def matmul(left, right):
    return jnp.dot(left, right, preferred_element_type=f32)


def matmul_left(left, right):
    return lax.dot_general(left, right, (((0,), (0,)), ((), ())), preferred_element_type=f32)


def matmul_right(left, right):
    return lax.dot_general(left, right, (((1,), (1,)), ((), ())), preferred_element_type=f32)


def smooth_gate(value):
    return jax.nn.gelu(value, approximate=True)


def norm_forward(summed, gain_row, shift_row):
    centered = summed - jnp.mean(summed, -1, keepdims=True)
    invert = lax.rsqrt(jnp.mean(centered * centered, -1, keepdims=True) + EPSILON)
    normed = centered * invert
    return (normed * gain_row + shift_row, normed, invert)


def norm_backward(upstream, normed, invert, gain_row):
    scaled = upstream * gain_row
    centered = (
        scaled
        - jnp.mean(scaled, -1, keepdims=True)
        - normed * jnp.mean(scaled * normed, -1, keepdims=True)
    )
    return (centered * invert, jnp.sum(upstream * normed, 0), jnp.sum(upstream, 0))


def passed_along(value, axis, steps):
    count = lax.axis_size(axis)
    leading, last = (max(0, -steps), min(count, count - steps))
    return lax.ppermute(value, axis, [(source, source + steps) for source in range(leading, last)])


AXES = ("far", "near", "core", "seq")


def place():
    return lax.axis_index(AXES)


def place_count():
    return lax.axis_size("far") * GROUP


def swapped(value, mask):
    return lax.ppermute(value, AXES, [(i, i ^ mask) for i in range(place_count())])


def after(value, *others):
    return lax.optimization_barrier((value,) + others)[0]


def group_index(bits):
    me = place()
    return sum(((me & bit) != 0).astype(jnp.int32) << n for n, bit in enumerate(bits))


def group_mask(bits, relative):
    return sum(bit for n, bit in enumerate(bits) if (relative >> n) & 1)


def scatter_sum(value, bits, *late):
    count = 1 << len(bits)
    rows = value.shape[0] // count
    index = group_index(bits)
    part = lambda relative: lax.dynamic_slice_in_dim(value, (index ^ relative) * rows, rows)
    total = part(0).astype(f32)
    others = [swapped(part(r), group_mask(bits, r)) for r in range(1, count)]
    if late:
        others = [after(other, *late) for other in others]
    for other in others:
        total = total + other.astype(f32)
    return total.astype(bf16)


def gathered(value, bits, *late):
    count = 1 << len(bits)
    index = group_index(bits)
    parts = [value] + [swapped(value, group_mask(bits, r)) for r in range(1, count)]
    if late:
        parts = [after(part, *late) for part in parts]
    for n in range(len(bits)):
        odd = ((index >> n) & 1) == 1
        parts = [
            jnp.where(odd, jnp.concatenate([second, first], 0), jnp.concatenate([first, second], 0))
            for first, second in zip(parts[::2], parts[1::2])
        ]
    return parts[0]


def doubled(value, bits, *late):
    for bit in bits:
        other = swapped(value, bit)
        if late:
            other = after(other, *late)
        value = (value.astype(f32) + other.astype(f32)).astype(bf16)
    return value


def far_bits():
    count = place_count()
    return [1 << n for n in range(3, count.bit_length() - 1)]


def kernel_call(body, grid, in_specs, out_specs, out_shape, scratch, flops, vmem, prefetch=0):
    return pl.pallas_call(
        body,
        grid_spec=pltpu.PrefetchScalarGridSpec(
            num_scalar_prefetch=prefetch,
            grid=grid,
            in_specs=in_specs,
            out_specs=out_specs,
            scratch_shapes=scratch,
        ),
        out_shape=out_shape,
        compiler_params=pltpu.CompilerParams(vmem_limit_bytes=vmem << 20),
        cost_estimate=pl.CostEstimate(flops=flops, bytes_accessed=8 << 20, transcendentals=0),
    )


def dot_nt(left, right):
    return lax.dot_general(left, right, (((1,), (1,)), ((), ())), preferred_element_type=f32)


def dot_tn(left, right):
    return lax.dot_general(left, right, (((0,), (0,)), ((), ())), preferred_element_type=f32)


def head_lanes(shape, head):
    lane = lax.broadcasted_iota(jnp.int32, shape, 1)
    return (lane >= HEAD_DIM) == (head == 1)


def attend_body(q_ref, ko_ref, kr_ref, vo_ref, vr_ref, sq_ref, so_ref, sr_ref, out_ref, lse_ref, stat):
    pair = pl.program_id(0)
    rows = q_ref.shape[0]

    @pl.when(pair == 0)
    def _():
        stat[...] = jnp.zeros_like(stat)

    for start in range(0, rows, TILE):
        part = pl.ds(start, TILE)
        queries = q_ref[part, :].astype(f32) * SCALE
        same_own = sq_ref[part, :] == so_ref[...]
        same_far = sq_ref[part, :] == sr_ref[...]
        lane = lax.broadcasted_iota(jnp.int32, (TILE, LANES), 1)
        mixed = None
        kept = stat[part, :]
        for head in range(2):
            masked = jnp.where(head_lanes((TILE, LANES), head), queries, 0.0).astype(bf16)
            s_own = jnp.where(same_own, dot_nt(masked, ko_ref[...]), NEGATIVE)
            s_far = jnp.where(same_far, dot_nt(masked, kr_ref[...]), NEGATIVE)
            top = jnp.maximum(
                jnp.max(s_own, 1, keepdims=True), jnp.max(s_far, 1, keepdims=True)
            )
            e_own = jnp.exp(s_own - top)
            e_far = jnp.exp(s_far - top)
            total = jnp.sum(e_own, 1, keepdims=True) + jnp.sum(e_far, 1, keepdims=True)
            mix = matmul(e_own.astype(bf16), vo_ref[...]) + matmul(e_far.astype(bf16), vr_ref[...])
            mix = mix / total
            kept = jnp.where(lane == 2 * pair + head, top + jnp.log(total), kept)
            mixed = mix if head == 0 else jnp.where(lane < HEAD_DIM, mixed, mix)
        out_ref[part, :] = mixed.astype(bf16)
        stat[part, :] = kept

    @pl.when(pair == HEADS // 2 - 1)
    def _():
        lse_ref[...] = jnp.transpose(stat[...])[:HEADS, :]


def attend(query, q_at, own, ko_at, vo_at, far, kr_at, vr_at, seg_q, seg_own, seg_far):
    rows, keys = query.shape[0], own.shape[0]
    pick = lambda n, at: pl.BlockSpec((n, LANES), lambda h, at=at: (0, at + h))
    whole = lambda *shape: pl.BlockSpec(shape, lambda h: (0, 0))
    return kernel_call(
        attend_body,
        (HEADS // 2,),
        [
            pick(rows, q_at),
            pick(keys, ko_at),
            pick(keys, kr_at),
            pick(keys, vo_at),
            pick(keys, vr_at),
            whole(rows, 1),
            whole(1, keys),
            whole(1, keys),
        ],
        [pick(rows, 0), whole(HEADS, rows)],
        [
            jax.ShapeDtypeStruct((rows, HEADS * HEAD_DIM), bf16),
            jax.ShapeDtypeStruct((HEADS, rows), f32),
        ],
        [pltpu.VMEM((rows, LANES), f32)],
        16 * rows * keys * 512,
        28,
    )(query, own, far, own, far, seg_q.reshape(rows, 1), seg_own.reshape(1, keys), seg_far.reshape(1, keys))


def attend_back_body(
    q_ref, g_ref, o_ref, lse_ref, ko_ref, kr_ref, vo_ref, vr_ref, sq_ref, so_ref, sr_ref,
    dq_ref, dko_ref, dvo_ref, dkr_ref, dvr_ref,
):
    rows = q_ref.shape[0]
    keys = ko_ref.shape[0]
    queries = q_ref[...].astype(f32) * SCALE
    upstream = g_ref[...].astype(f32)
    which = lax.broadcasted_iota(jnp.int32, (8, LANES), 0)
    lane = lax.broadcasted_iota(jnp.int32, (8, LANES), 1)
    chooser = jnp.where((lane >= HEAD_DIM) == (which == 1), 1.0, 0.0).astype(f32)
    along = lax.dot_general(
        chooser,
        upstream * o_ref[...].astype(f32),
        (((1,), (1,)), ((), ())),
        precision=lax.Precision.HIGHEST,
        preferred_element_type=f32,
    )
    q_of = [jnp.where(head_lanes((rows, LANES), h), queries, 0.0).astype(bf16) for h in range(2)]
    g_of = [jnp.where(head_lanes((rows, LANES), h), upstream, 0.0).astype(bf16) for h in range(2)]
    dq_of = [jnp.zeros((HEAD_DIM, rows), f32) for _ in range(2)]
    for k_ref, v_ref, s_ref, dk_ref, dv_ref in (
        (ko_ref, vo_ref, so_ref, dko_ref, dvo_ref),
        (kr_ref, vr_ref, sr_ref, dkr_ref, dvr_ref),
    ):
        for start in range(0, keys, TILE):
            part = pl.ds(start, TILE)
            key, value = k_ref[part, :], v_ref[part, :]
            same = s_ref[part, :] == sq_ref[...]
            key_t = jnp.transpose(key.astype(f32)).astype(bf16)
            dk = dv = None
            for h in range(2):
                scores = jnp.where(same, dot_nt(key, q_of[h]), NEGATIVE)
                weights = jnp.exp(scores - lse_ref[0, h : h + 1, :])
                back = dot_nt(value, g_of[h])
                grad = (weights * (back - along[h : h + 1, :])).astype(bf16)
                dv_h = matmul(weights.astype(bf16), g_of[h])
                dk_h = matmul(grad, q_of[h])
                dv = dv_h if dv is None else dv + dv_h
                dk = dk_h if dk is None else dk + dk_h
                dq_of[h] += matmul(key_t[h * HEAD_DIM : (h + 1) * HEAD_DIM, :], grad)
            dk_ref[part, :] = dk.astype(bf16)
            dv_ref[part, :] = dv.astype(bf16)
    dq = jnp.concatenate(dq_of, 0)
    dq_ref[...] = (jnp.transpose(dq) * SCALE).astype(bf16)


def attend_back(query, q_at, upstream, mixed, lse, own, ko_at, vo_at, far, kr_at, vr_at, seg_q, seg_own, seg_far):
    rows, keys = query.shape[0], own.shape[0]
    pick = lambda n, at: pl.BlockSpec((n, LANES), lambda h, at=at: (0, at + h))
    whole = lambda *shape: pl.BlockSpec(shape, lambda h: (0, 0))
    width = HEADS * HEAD_DIM
    return kernel_call(
        attend_back_body,
        (HEADS // 2,),
        [
            pick(rows, q_at),
            pick(rows, 0),
            pick(rows, 0),
            pl.BlockSpec((1, 2, rows), lambda h: (h, 0, 0)),
            pick(keys, ko_at),
            pick(keys, kr_at),
            pick(keys, vo_at),
            pick(keys, vr_at),
            whole(1, rows),
            whole(keys, 1),
            whole(keys, 1),
        ],
        [pick(rows, 0)] + [pick(keys, 0)] * 4,
        [jax.ShapeDtypeStruct((rows, width), bf16)] + [jax.ShapeDtypeStruct((keys, width), bf16)] * 4,
        [],
        40 * rows * keys * 512,
        28,
    )(
        query, upstream, mixed, lse.reshape(HEADS // 2, 2, rows), own, far, own, far,
        seg_q.reshape(1, rows), seg_own.reshape(keys, 1), seg_far.reshape(keys, 1),
    )


def columns_of(row):
    return jnp.transpose(jnp.broadcast_to(row, (LANES, row.shape[1])))


def vocab_body(info, *refs):
    blocks, (t_ref, w_ref, e_ref, stat_ref, all_ref, tall_ref, logits) = refs[:GROUP], refs[GROUP:]
    step = pl.program_id(0)
    chunk = 128

    @pl.when(step == 0)
    def _():
        all_ref[...] = jnp.zeros_like(all_ref)
        tall_ref[...] = jnp.zeros_like(tall_ref)
        for rel in range(GROUP):
            core, near = rel // 4, rel % 4
            block = (core | (near << 1)) ^ info[17]
            count, offset = info[block], info[8 + block]
            src = blocks[rel]
            for start in range(0, src.shape[0], chunk):

                @pl.when(start < count)
                def _(src=src, rel=rel, start=start, offset=offset):
                    to = pl.ds(pl.multiple_of(offset + start, 16), chunk)
                    all_ref[to, :] += src[start : start + chunk, :]
                    tall_ref[to, :] += columns_of(t_ref[rel : rel + 1, start : start + chunk])

    @pl.when(step * TILE < info[16])
    def _():
        hidden = all_ref[pl.ds(pl.multiple_of(step * TILE, TILE), TILE), :]
        wide = w_ref.shape[1]
        piece = min(1024, wide)
        top = None
        for start in range(0, wide, piece):
            value = matmul(hidden, w_ref[:, start : start + piece])
            logits[:, start : start + piece] = value
            most = jnp.max(value, 1, keepdims=True)
            top = most if top is None else jnp.maximum(top, most)
        total = None
        for start in range(0, wide, piece):
            value = jnp.exp(logits[:, start : start + piece] - top)
            added = jnp.sum(value, 1, keepdims=True)
            total = added if total is None else total + added
            e_ref[:, start : start + piece] = value.astype(bf16)
        lane = lax.broadcasted_iota(jnp.int32, (TILE, LANES), 1)
        stat_ref[...] = jnp.transpose(jnp.where(lane == 0, top, total))[:8, :]


def last_active(i, info):
    return jnp.minimum(i, jnp.maximum((info[16] + TILE - 1) // TILE - 1, 0))


def vocab_forward(info, blocks, targets, w_t):
    rows, width = blocks[0].shape
    total = GROUP * rows
    wide = w_t.shape[1]
    once = lambda *shape: pl.BlockSpec(
        shape, lambda i, info: (0,) * len(shape), pipeline_mode=pl.Buffered(1)
    )
    return kernel_call(
        vocab_body,
        (total // TILE,),
        [once(rows, width)] * GROUP + [once(GROUP, rows), once(width, wide)],
        [
            pl.BlockSpec((TILE, wide), lambda i, info: (last_active(i, info), 0)),
            pl.BlockSpec((8, TILE), lambda i, info: (0, last_active(i, info))),
            once(total, width),
            once(total, LANES),
        ],
        [
            jax.ShapeDtypeStruct((total, wide), bf16),
            jax.ShapeDtypeStruct((8, total), f32),
            jax.ShapeDtypeStruct((total, width), bf16),
            jax.ShapeDtypeStruct((total, LANES), f32),
        ],
        [pltpu.VMEM((TILE, wide), f32)],
        1400 * wide * width * 2,
        36,
        prefetch=1,
    )(info, *blocks, targets, w_t)


def vocab_back_body(info, e_ref, w_ref, out_ref):
    @pl.when(pl.program_id(0) * TILE < info[16])
    def _():
        out_ref[...] = matmul(e_ref[...], w_ref[...]).astype(bf16)


def vocab_back(info, e, w):
    total, wide = e.shape
    width = w.shape[1]
    tile = lambda n: pl.BlockSpec((TILE, n), lambda i, info: (last_active(i, info), 0))
    return kernel_call(
        vocab_back_body,
        (total // TILE,),
        [tile(wide), pl.BlockSpec((wide, width), lambda i, info: (0, 0), pipeline_mode=pl.Buffered(1))],
        tile(width),
        jax.ShapeDtypeStruct((total, width), bf16),
        [],
        1400 * wide * width * 2,
        24,
        prefetch=1,
    )(info, e, w)


def spread_body(info, g_ref, f_ref, near_ref, far_ref, columns):
    step = pl.program_id(0)
    total, width = g_ref.shape
    rows = near_ref.shape[1]

    @pl.when(step == 0)
    def _():
        for start in range(0, total, TILE):
            columns[start : start + TILE, :] = columns_of(f_ref[:, start : start + TILE])

    def block_of(core, near):
        block = (core | (near << 1)) ^ info[17]
        at = pl.ds(pl.multiple_of(info[8 + block], 16), rows)
        row = lax.broadcasted_iota(jnp.int32, (rows, LANES), 0)
        factor = jnp.where(row < info[block], columns[at, :], 0.0)
        live = row < info[block]
        pieces = [
            jnp.where(live, g_ref[at, start : start + LANES].astype(f32) * factor, 0.0)
            for start in range(0, width, LANES)
        ]
        return jnp.concatenate(pieces, 1).astype(bf16)

    @pl.when(step < GROUP // 2)
    def _():
        far_ref[0] = block_of(1, step)

    @pl.when(step >= GROUP // 2)
    def _():
        near_ref[0] = block_of(0, step - GROUP // 2)


def spread(info, g, factor, rows):
    total, width = g.shape
    half = GROUP // 2
    once = lambda *shape: pl.BlockSpec(
        shape, lambda i, info: (0,) * len(shape), pipeline_mode=pl.Buffered(1)
    )
    return kernel_call(
        spread_body,
        (GROUP,),
        [once(total, width), once(1, total)],
        [
            pl.BlockSpec((1, rows, width), lambda i, info: (jnp.maximum(i - half, 0), 0, 0)),
            pl.BlockSpec((1, rows, width), lambda i, info: (jnp.minimum(i, half - 1), 0, 0)),
        ],
        [jax.ShapeDtypeStruct((half, rows, width), bf16)] * 2,
        [pltpu.VMEM((total, LANES), f32)],
        total * width,
        24,
        prefetch=1,
    )(info, g, factor)


def vocab_grad_body(info, e_ref, h_ref, t_ref, f_ref, out_ref, total):
    step = pl.program_id(0)

    @pl.when(step == 0)
    def _():
        total[...] = jnp.zeros_like(total)

    @pl.when(step * TILE < info[16])
    def _():
        wide = e_ref.shape[1]
        piece = min(1024, wide)
        factor = columns_of(f_ref[...])[:, :1]
        target = t_ref[...][:, :1].astype(jnp.int32)
        for start in range(0, wide, piece):
            column = start + 1 + lax.broadcasted_iota(jnp.int32, (TILE, piece), 1)
            weights = e_ref[:, start : start + piece].astype(f32) * factor
            weights = (weights - jnp.where(column == target, 1.0, 0.0)).astype(bf16)
            total[start : start + piece, :] += dot_tn(weights, h_ref[...])

    @pl.when(step == pl.num_programs(0) - 1)
    def _():
        out_ref[...] = total[...].astype(bf16)


def vocab_grad(info, e, hidden, target, factor):
    total, wide = e.shape
    width = hidden.shape[1]
    tile = lambda n: pl.BlockSpec((TILE, n), lambda i, info: (last_active(i, info), 0))
    return kernel_call(
        vocab_grad_body,
        (total // TILE,),
        [
            tile(wide),
            tile(width),
            tile(LANES),
            pl.BlockSpec((1, TILE), lambda i, info: (0, last_active(i, info))),
        ],
        pl.BlockSpec((wide, width), lambda i, info: (0, 0)),
        jax.ShapeDtypeStruct((wide, width), bf16),
        [pltpu.VMEM((wide, width), f32)],
        1400 * wide * width * 2,
        40,
        prefetch=1,
    )(info, e, hidden, target, factor)


def halves_body(plan, info, *refs):
    operands, out_ref = refs[:-1], refs[-1]
    rows = out_ref.shape[0]
    half = info[0] * rows
    at = 0
    for terms, width in plan:
        total = None
        for left, left_at, right, right_at in terms:
            if right is None:
                value = operands[left][pl.ds(pl.multiple_of(half, rows), rows), :].astype(f32)
            else:
                lanes = pl.ds(pl.multiple_of(left_at + half, rows), rows)
                value = dot_tn(operands[left][:, lanes], operands[right][:, right_at : right_at + width])
            total = value if total is None else total + value
        out_ref[:, at : at + width] = total.astype(bf16)
        at += width


def weight_sums(columns, rows):
    operands, plan = [], []

    def index_of(array):
        for n, known in enumerate(operands):
            if known is array:
                return n
        operands.append(array)
        return len(operands) - 1

    for width, terms in columns:
        plan.append(
            (
                [
                    (index_of(left), left_at, None if right is None else index_of(right), right_at)
                    for left, left_at, right, right_at in terms
                ],
                width,
            )
        )
    total = sum(width for width, _ in columns)
    whole = lambda array: pl.BlockSpec(
        array.shape, lambda i, info: (0, 0), pipeline_mode=pl.Buffered(1)
    )

    def half(index):
        return kernel_call(
            functools.partial(halves_body, plan),
            (1,),
            [whole(o) for o in operands],
            pl.BlockSpec((rows // 2, total), lambda i, info: (0, 0), pipeline_mode=pl.Buffered(1)),
            jax.ShapeDtypeStruct((rows // 2, total), bf16),
            [],
            rows * total * 512,
            36,
            prefetch=1,
        )(index[None], *operands)

    mine = group_index([CORE_BIT])
    send = swapped(half(1 - mine), CORE_BIT)
    return (half(mine).astype(f32) + send.astype(f32)).astype(bf16)


def joined_body(plan, info, own_ref, other_ref, *outs):
    rows = own_ref.shape[0]
    mine, far = pl.multiple_of(info[0] * rows, rows), pl.multiple_of((1 - info[0]) * rows, rows)
    for (starts, width, turned), out_ref in zip(plan, outs):
        for n, start in enumerate(starts):
            for ref, at in ((own_ref, mine), (other_ref, far)):
                value = ref[:, start : start + width].astype(f32)
                if turned:
                    out_ref[:, pl.ds(at, rows)] = jnp.transpose(value)
                else:
                    out_ref[pl.ds(n * 2 * rows + at, rows), :] = value


def joined(own, other, plan):
    rows = own.shape[0]
    shapes = [
        (width, 2 * rows) if turned else (2 * rows * len(starts), width)
        for starts, width, turned in plan
    ]
    once = lambda shape: pl.BlockSpec(shape, lambda i, info: (0, 0), pipeline_mode=pl.Buffered(1))
    return kernel_call(
        functools.partial(joined_body, plan),
        (1,),
        [once(own.shape)] * 2,
        [once(shape) for shape in shapes],
        [jax.ShapeDtypeStruct(shape, f32) for shape in shapes],
        [],
        own.size,
        36,
        prefetch=1,
    )(group_index([CORE_BIT])[None], own, other)


def per_device(
    hidden_in,
    enc_states,
    segment_ids,
    edit_pass,
    enc_segments,
    target_tokens,
    placeholder_counts,
    delete_labels,
    loss_mask,
    w_self_qkv,
    w_self_out,
    w_cross_q,
    w_cross_kv,
    w_cross_out,
    w_ffn_in,
    b_ffn_in,
    w_ffn_out,
    b_ffn_out,
    norm_gains,
    norm_shifts,
    w_vocab,
    w_pair,
    b_pair,
    w_delete,
):
    _, tokens, features = hidden_in.shape
    seq = lax.axis_index("seq")
    chip = [NEAR_BIT, SEQ_BIT]
    far = far_bits()
    hidden = hidden_in[0]
    source = enc_states[0]
    hidden_far = swapped(hidden, SEQ_BIT)
    qkv = matmul(hidden, w_self_qkv).astype(bf16)
    segment, passes, source_seg = segment_ids[0], edit_pass[0], enc_segments[0]

    keep_float = loss_mask[0].astype(f32)
    token_keep = keep_float * (passes == 2).astype(f32)
    row = lax.broadcasted_iota(jnp.int32, (tokens, tokens), 0)
    col = lax.broadcasted_iota(jnp.int32, (tokens, tokens), 1)
    rank = matmul(token_keep.astype(bf16)[None, :], (row <= col).astype(bf16)) - 1.0
    selects = (rank.astype(jnp.int32) == row) & (token_keep[None, :] > 0)
    chooser = selects.astype(bf16)
    targets = target_tokens[0]
    chosen = jnp.sum(jnp.where(selects, targets[None, :] + 1, 0), 1)
    ids_far = swapped(jnp.stack([segment, source_seg, chosen]), SEQ_BIT)
    segment_far, source_seg_far = ids_far[0], ids_far[1]

    vocab = w_vocab.shape[0]
    outer = lax.axis_size("far")
    block = vocab // (outer * GROUP)
    inner = lax.axis_index(("near", "core", "seq"))
    here = group_index([CORE_BIT, NEAR_BIT, SEQ_BIT])
    ckv = matmul(source, w_cross_kv).astype(bf16)
    kv_far = matmul(hidden_far, w_self_qkv[:, features:]).astype(bf16)
    source_far = swapped(after(source, hidden_far), SEQ_BIT)
    self_mix, self_lse = attend(qkv, 0, qkv, 4, 8, kv_far, 0, 4, segment, segment, segment_far)
    layer_one, normed_one, invert_one = norm_forward(
        hidden.astype(f32) + matmul(self_mix, w_self_out), norm_gains[0], norm_shifts[0]
    )

    chosen_row = after(jnp.stack([chosen, ids_far[2]]), self_mix)
    chosen_near = swapped(chosen_row, NEAR_BIT)
    chosen_chip = jnp.stack([chosen_row[0], chosen_near[0], chosen_row[1], chosen_near[1]])
    chosen_all = jnp.concatenate([chosen_chip, swapped(chosen_chip, CORE_BIT)])
    index = chosen_all - 1
    local = (index // (block * GROUP)) * block + index % block + 1
    mine = (chosen_all > 0) & ((index // block) % GROUP == inner)
    local_targets = jnp.where(mine, local, 0).astype(f32)
    counts_rel = jnp.sum((chosen_all > 0).astype(jnp.int32), 1)
    relative = jnp.array([c | (n << 1) for c in range(2) for n in range(4)], jnp.int32) ^ here
    counts = jnp.sum(
        jnp.where(relative[:, None] == jnp.arange(GROUP)[None, :], counts_rel[:, None], 0), 0
    )
    rounded = (counts + 15) // 16 * 16
    before = jnp.arange(GROUP)[:, None] < jnp.arange(GROUP)[None, :]
    offsets = jnp.sum(jnp.where(before, rounded[:, None], 0), 0)
    info = jnp.concatenate([counts, offsets, jnp.sum(rounded)[None], here[None]]).astype(jnp.int32)

    one_low = layer_one.astype(bf16)
    cross_query = matmul(one_low, w_cross_q).astype(bf16)
    ckv_far = matmul(source_far, w_cross_kv).astype(bf16)
    cross_mix, cross_lse = attend(
        cross_query, 0, ckv, 0, 4, ckv_far, 0, 4, segment, source_seg, source_seg_far
    )
    layer_two, normed_two, invert_two = norm_forward(
        layer_one + matmul(cross_mix, w_cross_out), norm_gains[1], norm_shifts[1]
    )
    two_low = layer_two.astype(bf16)
    pre_act = matmul(two_low, w_ffn_in) + b_ffn_in
    activ, gate_back = jax.vjp(smooth_gate, pre_act)
    activ_low = activ.astype(bf16)
    layer_three, normed_three, invert_three = norm_forward(
        layer_two + (matmul(activ_low, w_ffn_out) + b_ffn_out), norm_gains[2], norm_shifts[2]
    )
    three_low = layer_three.astype(bf16)

    kept = matmul(chooser, three_low).astype(bf16)
    kept_core = swapped(kept, CORE_BIT)
    kept_chip = [swapped(kept, NEAR_BIT), swapped(kept, SEQ_BIT), swapped(kept, NEAR_BIT | SEQ_BIT)]
    next_row = passed_along(three_low[:1], "seq", -1)
    w_here = lax.dynamic_index_in_dim(
        w_vocab.reshape(outer, GROUP, block, features), after(inner, kept), 1, keepdims=False
    ).reshape(outer * block, features)
    w_here_t = jnp.transpose(w_here)
    target_rows = jnp.take(w_vocab, after(targets, kept), axis=0).astype(f32)
    kept_chip = [after(k, w_here_t, target_rows) for k in kept_chip]
    kept_other = [swapped(k, CORE_BIT) for k in kept_chip]

    delete_keep = keep_float * (passes == 0).astype(f32)

    def label_grad(logits, labels, keep_mask):
        shifted = logits - jnp.max(logits, -1, keepdims=True)
        exponent = jnp.exp(shifted)
        weights = exponent / jnp.sum(exponent, -1, keepdims=True)
        onehot = labels[:, None] == lax.broadcasted_iota(jnp.int32, logits.shape, 1)
        return ((weights - onehot.astype(f32)) * keep_mask[:, None]).astype(bf16)

    delete_grad = label_grad(matmul(three_low, w_delete), delete_labels[0], delete_keep)

    delete_back = matmul_right(delete_grad, w_delete) - target_rows * token_keep[:, None]
    d_delete = matmul_left(delete_grad, three_low)
    info = after(info, delete_back, d_delete)
    e, stats, kept_all, target_all = vocab_forward(
        info, [kept] + kept_chip + [kept_core] + kept_other, local_targets, w_here_t
    )
    stats = stats[:2]

    def merged(first, *others):
        most = functools.reduce(jnp.maximum, [o[0] for o in others], first[0])
        added = sum((o[1] * jnp.exp(o[0] - most) for o in others), first[1] * jnp.exp(first[0] - most))
        return jnp.stack([most, added])

    stats_pair = merged(stats, swapped(stats, CORE_BIT))
    stats_all = merged(stats_pair, *[swapped(stats_pair, group_mask(chip, r)) for r in (1, 2, 3)])
    factor = jnp.exp(stats[0] - stats_all[0] - jnp.log(stats_all[1]))[None, :]
    back_raw = vocab_back(info, e, w_here)
    back_near, back_core = spread(info, back_raw, factor, tokens)
    back_core = swapped(back_core, CORE_BIT)
    back_low = [(back_near[r].astype(f32) + back_core[r].astype(f32)).astype(bf16) for r in (1, 2, 3)]
    position = seq * tokens + jnp.arange(tokens, dtype=jnp.int32)
    row_length = tokens * lax.axis_size("seq")
    follow = jnp.concatenate([three_low[1:], after(next_row, *back_low)], 0)
    follow_seg = jnp.concatenate([segment[1:], segment_far[:1]], 0)
    pair_ok = (follow_seg == segment) & (position < row_length - 1)
    pair_keep = keep_float * (passes == 1).astype(f32) * pair_ok.astype(f32)
    pair_logits = matmul(three_low, w_pair[:features]) + matmul(follow, w_pair[features:]) + b_pair
    pair_grad = label_grad(pair_logits, placeholder_counts[0], pair_keep)
    follow_grad = matmul_right(pair_grad, w_pair[features:])
    back_row = passed_along(follow_grad[-1:], "seq", 1)
    d_b_pair = jnp.sum(pair_grad.astype(f32), 0)
    head_back = [swapped(back_low[r - 1], group_mask(chip, r)).astype(f32) for r in (1, 2, 3)]
    head_back = sum(head_back, back_near[0].astype(f32) + back_core[0].astype(f32))
    vocab_part = vocab_grad(info, e, kept_all, target_all, after(factor, *back_low))
    d_vocab = lax.psum_scatter(vocab_part, "far", scatter_dimension=0, tiled=True).astype(f32)
    grad_local = (
        delete_back
        + matmul_right(pair_grad, w_pair[:features])
        + jnp.concatenate([back_row, follow_grad[:-1]], 0)
    )
    grad_local = after(grad_local, vocab_part)

    grad_three = grad_local + matmul_left(chooser, head_back.astype(bf16))
    grad_sum3, gain_three, shift_three = norm_backward(
        grad_three, normed_three, invert_three, norm_gains[2]
    )
    branch_three = grad_sum3.astype(bf16)
    d_b_ffn_out = jnp.sum(branch_three.astype(f32), 0)
    grad_pre = gate_back(matmul_right(branch_three, w_ffn_out))[0].astype(bf16)
    d_b_ffn_in = jnp.sum(grad_pre.astype(f32), 0)
    hidden_units = w_ffn_in.shape[1]
    pair_count = w_pair.shape[1]
    sum_ffn = weight_sums(
        [(hidden_units, [(two_low, 0, grad_pre, 0)])]
        + [(features, [(activ_low, at, branch_three, 0)]) for at in range(0, hidden_units, features)],
        features,
    )
    grad_two = grad_sum3 + matmul_right(grad_pre, w_ffn_in)
    grad_sum2, gain_two, shift_two = norm_backward(grad_two, normed_two, invert_two, norm_gains[1])
    branch_two = grad_sum2.astype(bf16)
    cross_up = matmul_right(branch_two, w_cross_out).astype(bf16)
    cross_up = after(cross_up, sum_ffn)
    sum_in = scatter_sum(sum_ffn[:, :hidden_units], chip)
    dcq, dck, dcv, dck_far, dcv_far = attend_back(
        cross_query, 0, cross_up, cross_mix, cross_lse, ckv, 0, 4, ckv_far, 0, 4,
        segment, source_seg, source_seg_far,
    )
    sum_in = after(sum_in, dck)
    dcq = after(dcq, sum_in)
    sum_out = scatter_sum(after(sum_ffn[:, hidden_units:], sum_in), chip)
    grad_one = grad_sum2 + matmul_right(dcq, w_cross_q)
    grad_sum1, gain_one, shift_one = norm_backward(grad_one, normed_one, invert_one, norm_gains[0])
    branch_one = grad_sum1.astype(bf16)
    self_up = matmul_right(branch_one, w_self_out).astype(bf16)
    small = jnp.concatenate(
        [
            d_b_ffn_in,
            d_b_ffn_out,
            gain_one,
            gain_two,
            gain_three,
            shift_one,
            shift_two,
            shift_three,
            d_b_pair,
            d_delete.reshape(-1),
        ]
    )
    small_size = small.shape[0]
    small_cols = -(-small_size // (features * LANES)) * LANES
    small = jnp.pad(small, (0, features * small_cols - small_size)).reshape(small_cols, features)
    small = jnp.transpose(small)
    sum_mid = weight_sums(
        [
            (features, [(cross_mix, 0, branch_two, 0)]),
            (features, [(one_low, 0, dcq, 0)]),
            (features, [(source, 0, dck, 0), (source_far, 0, dck_far, 0)]),
            (features, [(source, 0, dcv, 0), (source_far, 0, dcv_far, 0)]),
            (features, [(self_mix, 0, branch_one, 0)]),
            (pair_count, [(three_low, 0, pair_grad, 0)]),
            (pair_count, [(follow, 0, pair_grad, 0)]),
            (small_cols, [(small, 0, None, 0)]),
        ],
        features,
    )
    w_ckey, w_cvalue = w_cross_kv[:, :features], w_cross_kv[:, features:]
    d_enc_low = (matmul_right(dck_far, w_ckey) + matmul_right(dcv_far, w_cvalue)).astype(bf16)
    self_up = after(self_up, sum_out, sum_mid, d_enc_low)
    dq, dk, dv, dk_far, dv_far = attend_back(
        qkv, 0, self_up, self_mix, self_lse, qkv, 4, 8, kv_far, 0, 4, segment, segment, segment_far
    )
    sum_mid = scatter_sum(sum_mid, chip)
    dq = after(dq, sum_mid)
    sum_ffn = after(jnp.concatenate([sum_in, sum_out], 1), dq)
    sum_qkv = weight_sums(
        [
            (features, [(hidden, 0, dq, 0)]),
            (features, [(hidden, 0, dk, 0), (hidden_far, 0, dk_far, 0)]),
            (features, [(hidden, 0, dv, 0), (hidden_far, 0, dv_far, 0)]),
        ],
        features,
    )
    w_key, w_value = w_self_qkv[:, features : 2 * features], w_self_qkv[:, 2 * features :]
    d_hidden_low = (matmul_right(dk_far, w_key) + matmul_right(dv_far, w_value)).astype(bf16)
    sum_ffn = scatter_sum(sum_ffn, far[:1], sum_qkv)
    for bit in far[1:]:
        sum_ffn = scatter_sum(sum_ffn, [bit])
    sum_qkv = scatter_sum(sum_qkv, chip)
    d_hidden_far = swapped(after(d_hidden_low, sum_qkv), SEQ_BIT)

    def from_far(value, *late):
        for bit in reversed(far):
            value = gathered(value, [bit], *late)
        return value

    sum_ffn = after(sum_ffn, sum_qkv)
    sum_rest = jnp.concatenate([sum_mid, sum_qkv], 1)
    sum_ffn = from_far(sum_ffn)
    for bit in far:
        sum_rest = scatter_sum(sum_rest, [bit])
    d_enc_far = swapped(after(d_enc_low, d_hidden_far), SEQ_BIT)
    sum_rest = from_far(sum_rest)
    sum_ffn = gathered(after(sum_ffn, d_hidden_far, d_enc_far), chip, sum_rest)
    ffn_other = swapped(sum_ffn, CORE_BIT)
    out_ffn_in, out_ffn_out = joined(
        sum_ffn,
        ffn_other,
        [
            ([0], hidden_units, False),
            (list(range(hidden_units, 2 * hidden_units, features)), features, False),
        ],
    )
    mid_columns = sum_mid.shape[1]
    sum_mid = after(sum_rest[:, :mid_columns], sum_ffn)
    sum_qkv = sum_rest[:, mid_columns:]
    d_hidden = (
        grad_sum1
        + matmul_right(dq, w_self_qkv[:, :features])
        + matmul_right(dk, w_key)
        + matmul_right(dv, w_value)
        + d_hidden_far.astype(f32)
    )
    d_enc = matmul_right(dck, w_ckey) + matmul_right(dcv, w_cvalue) + d_enc_far.astype(f32)

    sum_mid = gathered(sum_mid, chip, out_ffn_in, out_ffn_out, d_hidden, d_enc)
    mid_other = swapped(sum_mid, CORE_BIT)
    pair_at = 5 * features
    small_at = pair_at + 2 * pair_count
    out_cross_out, out_cross_q, out_cross_kv, out_self_out, out_pair, flat = joined(
        sum_mid,
        mid_other,
        [
            ([0], features, False),
            ([features], features, False),
            ([2 * features], 2 * features, False),
            ([4 * features], features, False),
            ([pair_at, pair_at + pair_count], pair_count, False),
            ([small_at], small_cols, True),
        ],
    )
    sum_qkv = gathered(after(sum_qkv, sum_mid), chip, out_cross_out)
    (out_self_qkv,) = joined(sum_qkv, swapped(sum_qkv, CORE_BIT), [([0], 3 * features, False)])
    flat = flat.reshape(-1)
    at = [0]

    def taken(size):
        at[0] += size
        return flat[at[0] - size : at[0]]

    out_b_ffn_in = taken(hidden_units)
    out_b_ffn_out = taken(features)
    out_gains = taken(3 * features).reshape(3, features)
    out_shifts = taken(3 * features).reshape(3, features)
    out_b_pair = taken(pair_count)
    out_delete = jnp.transpose(taken(2 * features).reshape(2, features))
    return (
        three_low[None],
        d_hidden[None],
        d_enc[None],
        out_self_qkv,
        out_self_out,
        out_cross_q,
        out_cross_kv,
        out_cross_out,
        out_ffn_in,
        out_b_ffn_in,
        out_ffn_out,
        out_b_ffn_out,
        out_gains,
        out_shifts,
        d_vocab,
        out_pair,
        out_b_pair,
        out_delete,
    )


def solution(mesh):
    split_mesh = Mesh(mesh.devices.reshape(-1, 2, 2, mesh.shape["seq"]), AXES)
    rows = ("far", "near", "core")
    split = P(rows, "seq", None)
    ids = P(rows, "seq")
    return jax.shard_map(
        per_device,
        mesh=split_mesh,
        in_specs=(split, split) + (ids,) * 7 + (P(),) * 15,
        out_specs=(split,) * 3 + (P(),) * 11 + (P(AXES, None),) + (P(),) * 3,
        check_vma=False,
    )
```

```python
import functools

import jax
import jax.numpy as jnp
from jax import lax
from jax.experimental import pallas as pl
from jax.experimental.pallas import tpu as pltpu
from jax.sharding import Mesh
from jax.sharding import PartitionSpec as P

HEADS = 8
HEAD_DIM = 64
LANES = 128
SCALE = HEAD_DIM**-0.5
EPSILON = 1e-05
NEGATIVE = -1e30
TILE = 256
ATTEND_TILE = 512

SEQ_BIT, CORE_BIT, NEAR_BIT = 1, 2, 4
GROUP = 8

bf16 = jnp.bfloat16
f32 = jnp.float32


def matmul(left, right):
    return jnp.dot(left, right, preferred_element_type=f32)


def matmul_left(left, right):
    return lax.dot_general(left, right, (((0,), (0,)), ((), ())), preferred_element_type=f32)


def matmul_right(left, right):
    return lax.dot_general(left, right, (((1,), (1,)), ((), ())), preferred_element_type=f32)


def smooth_gate(value):
    return jax.nn.gelu(value, approximate=True)


def norm_forward(summed, gain_row, shift_row):
    centered = summed - jnp.mean(summed, -1, keepdims=True)
    invert = lax.rsqrt(jnp.mean(centered * centered, -1, keepdims=True) + EPSILON)
    normed = centered * invert
    return (normed * gain_row + shift_row, normed, invert)


def norm_backward(upstream, normed, invert, gain_row):
    scaled = upstream * gain_row
    centered = (
        scaled
        - jnp.mean(scaled, -1, keepdims=True)
        - normed * jnp.mean(scaled * normed, -1, keepdims=True)
    )
    return (
        centered * invert,
        jnp.sum(upstream * normed, 0, keepdims=True),
        jnp.sum(upstream, 0, keepdims=True),
    )


def passed_along(value, axis, steps):
    count = lax.axis_size(axis)
    leading, last = (max(0, -steps), min(count, count - steps))
    return lax.ppermute(value, axis, [(source, source + steps) for source in range(leading, last)])


AXES = ("far", "near", "core", "seq")


def place():
    return lax.axis_index(AXES)


def place_count():
    return lax.axis_size("far") * GROUP


def swapped(value, mask):
    return lax.ppermute(value, AXES, [(i, i ^ mask) for i in range(place_count())])


def after(value, *others):
    return lax.optimization_barrier((value,) + others)[0]


def group_index(bits):
    me = place()
    return sum(((me & bit) != 0).astype(jnp.int32) << n for n, bit in enumerate(bits))


def group_mask(bits, relative):
    return sum(bit for n, bit in enumerate(bits) if (relative >> n) & 1)


def scatter_sum(value, bits, *late):
    count = 1 << len(bits)
    rows = value.shape[0] // count
    index = group_index(bits)
    part = lambda relative: lax.dynamic_slice_in_dim(value, (index ^ relative) * rows, rows)
    total = part(0).astype(f32)
    others = [swapped(part(r), group_mask(bits, r)) for r in range(1, count)]
    if late:
        others = [after(other, *late) for other in others]
    for other in others:
        total = total + other.astype(f32)
    return total.astype(bf16)


def gathered(value, bits, *late):
    count = 1 << len(bits)
    index = group_index(bits)
    parts = [value] + [swapped(value, group_mask(bits, r)) for r in range(1, count)]
    if late:
        parts = [after(part, *late) for part in parts]
    for n in range(len(bits)):
        odd = ((index >> n) & 1) == 1
        parts = [
            jnp.where(odd, jnp.concatenate([second, first], 0), jnp.concatenate([first, second], 0))
            for first, second in zip(parts[::2], parts[1::2])
        ]
    return parts[0]


def doubled(value, bits, *late):
    for bit in bits:
        other = swapped(value, bit)
        if late:
            other = after(other, *late)
        value = (value.astype(f32) + other.astype(f32)).astype(bf16)
    return value


def far_bits():
    count = place_count()
    return [1 << n for n in range(3, count.bit_length() - 1)]


def kernel_call(body, grid, in_specs, out_specs, out_shape, scratch, flops, vmem, prefetch=0):
    return pl.pallas_call(
        body,
        grid_spec=pltpu.PrefetchScalarGridSpec(
            num_scalar_prefetch=prefetch,
            grid=grid,
            in_specs=in_specs,
            out_specs=out_specs,
            scratch_shapes=scratch,
        ),
        out_shape=out_shape,
        compiler_params=pltpu.CompilerParams(vmem_limit_bytes=vmem << 20),
        cost_estimate=pl.CostEstimate(flops=flops, bytes_accessed=8 << 20, transcendentals=0),
    )


def dot_nt(left, right):
    return lax.dot_general(left, right, (((1,), (1,)), ((), ())), preferred_element_type=f32)


def dot_tn(left, right):
    return lax.dot_general(left, right, (((0,), (0,)), ((), ())), preferred_element_type=f32)


def head_lanes(shape, head):
    lane = lax.broadcasted_iota(jnp.int32, shape, 1)
    return (lane >= HEAD_DIM) == (head == 1)


def attend_body(q_ref, ko_ref, kr_ref, vo_ref, vr_ref, sq_ref, so_ref, sr_ref, out_ref, lse_ref, stat):
    pair = pl.program_id(0)
    rows = q_ref.shape[0]

    @pl.when(pair == 0)
    def _():
        stat[...] = jnp.zeros_like(stat)

    for start in range(0, rows, ATTEND_TILE):
        part = pl.ds(start, ATTEND_TILE)
        queries = q_ref[part, :].astype(f32) * SCALE
        same_own = sq_ref[part, :] == so_ref[...]
        same_far = sq_ref[part, :] == sr_ref[...]
        lane = lax.broadcasted_iota(jnp.int32, (ATTEND_TILE, LANES), 1)
        mixed = None
        kept = stat[part, :]
        for head in range(2):
            masked = jnp.where(head_lanes((ATTEND_TILE, LANES), head), queries, 0.0).astype(bf16)
            s_own = jnp.where(same_own, dot_nt(masked, ko_ref[...]), NEGATIVE)
            s_far = jnp.where(same_far, dot_nt(masked, kr_ref[...]), NEGATIVE)
            top = jnp.maximum(
                jnp.max(s_own, 1, keepdims=True), jnp.max(s_far, 1, keepdims=True)
            )
            e_own = jnp.exp(s_own - top)
            e_far = jnp.exp(s_far - top)
            total = jnp.sum(e_own, 1, keepdims=True) + jnp.sum(e_far, 1, keepdims=True)
            mix = matmul(e_own.astype(bf16), vo_ref[...]) + matmul(e_far.astype(bf16), vr_ref[...])
            mix = mix / total
            kept = jnp.where(lane == 2 * pair + head, top + jnp.log(total), kept)
            mixed = mix if head == 0 else jnp.where(lane < HEAD_DIM, mixed, mix)
        out_ref[part, :] = mixed.astype(bf16)
        stat[part, :] = kept

    @pl.when(pair == HEADS // 2 - 1)
    def _():
        lse_ref[...] = jnp.transpose(stat[...])[:HEADS, :]


def attend(query, q_at, own, ko_at, vo_at, far, kr_at, vr_at, seg_q, seg_own, seg_far):
    rows, keys = query.shape[0], own.shape[0]
    pick = lambda n, at: pl.BlockSpec((n, LANES), lambda h, at=at: (0, at + h))
    whole = lambda *shape: pl.BlockSpec(shape, lambda h: (0, 0))
    return kernel_call(
        attend_body,
        (HEADS // 2,),
        [
            pick(rows, q_at),
            pick(keys, ko_at),
            pick(keys, kr_at),
            pick(keys, vo_at),
            pick(keys, vr_at),
            whole(rows, 1),
            whole(1, keys),
            whole(1, keys),
        ],
        [pick(rows, 0), whole(HEADS, rows)],
        [
            jax.ShapeDtypeStruct((rows, HEADS * HEAD_DIM), bf16),
            jax.ShapeDtypeStruct((HEADS, rows), f32),
        ],
        [pltpu.VMEM((rows, LANES), f32)],
        16 * rows * keys * 512,
        28,
    )(query, own, far, own, far, seg_q.reshape(rows, 1), seg_own.reshape(1, keys), seg_far.reshape(1, keys))


def attend_back_body(
    q_ref, g_ref, o_ref, lse_ref, ko_ref, kr_ref, vo_ref, vr_ref, sq_ref, so_ref, sr_ref, *refs
):
    dq_ref, dko_ref, dvo_ref, dkr_ref, dvr_ref = refs[-5:]
    rows = q_ref.shape[0]
    keys = ko_ref.shape[0]
    queries = q_ref[...].astype(f32) * SCALE
    upstream = g_ref[...].astype(f32)
    which = lax.broadcasted_iota(jnp.int32, (8, LANES), 0)
    lane = lax.broadcasted_iota(jnp.int32, (8, LANES), 1)
    chooser = jnp.where((lane >= HEAD_DIM) == (which == 1), 1.0, 0.0).astype(f32)
    along = lax.dot_general(
        chooser,
        upstream * o_ref[...].astype(f32),
        (((1,), (1,)), ((), ())),
        precision=lax.Precision.HIGHEST,
        preferred_element_type=f32,
    )
    q_of = [jnp.where(head_lanes((rows, LANES), h), queries, 0.0).astype(bf16) for h in range(2)]
    g_of = [jnp.where(head_lanes((rows, LANES), h), upstream, 0.0).astype(bf16) for h in range(2)]
    dq_of = [jnp.zeros((HEAD_DIM, rows), f32) for _ in range(2)]
    for k_ref, v_ref, s_ref, dk_ref, dv_ref in (
        (ko_ref, vo_ref, so_ref, dko_ref, dvo_ref),
        (kr_ref, vr_ref, sr_ref, dkr_ref, dvr_ref),
    ):
        for start in range(0, keys, ATTEND_TILE):
            part = pl.ds(start, ATTEND_TILE)
            key, value = k_ref[part, :], v_ref[part, :]
            same = s_ref[part, :] == sq_ref[...]
            key_t = jnp.transpose(key.astype(f32)).astype(bf16)
            dk = dv = None
            for h in range(2):
                scores = jnp.where(same, dot_nt(key, q_of[h]), NEGATIVE)
                weights = jnp.exp(scores - lse_ref[0, h : h + 1, :])
                back = dot_nt(value, g_of[h])
                grad = (weights * (back - along[h : h + 1, :])).astype(bf16)
                dv_h = matmul(weights.astype(bf16), g_of[h])
                dk_h = matmul(grad, q_of[h])
                dv = dv_h if dv is None else dv + dv_h
                dk = dk_h if dk is None else dk + dk_h
                dq_of[h] += matmul(key_t[h * HEAD_DIM : (h + 1) * HEAD_DIM, :], grad)
            dk_ref[part, :] = dk.astype(bf16)
            dv_ref[part, :] = dv.astype(bf16)
    dq = jnp.concatenate(dq_of, 0)
    dq_ref[...] = (jnp.transpose(dq) * SCALE).astype(bf16)


def attend_back(
    query, q_at, upstream, mixed, lse, own, ko_at, vo_at, far, kr_at, vr_at, seg_q, seg_own, seg_far,
    pairs=(0, HEADS // 2), begun=(),
):
    rows, keys = query.shape[0], own.shape[0]
    first, last = pairs
    pick = lambda n, at: pl.BlockSpec((n, LANES), lambda h, at=at: (0, at + first + h))
    whole = lambda *shape: pl.BlockSpec(shape, lambda h: (0, 0))
    width = HEADS * HEAD_DIM
    in_specs = [
        pick(rows, q_at),
        pick(rows, 0),
        pick(rows, 0),
        pl.BlockSpec((1, 2, rows), lambda h: (first + h, 0, 0)),
        pick(keys, ko_at),
        pick(keys, kr_at),
        pick(keys, vo_at),
        pick(keys, vr_at),
        whole(1, rows),
        whole(keys, 1),
        whole(keys, 1),
    ] + [pl.BlockSpec(memory_space=pl.ANY)] * len(begun)
    return pl.pallas_call(
        attend_back_body,
        grid=(last - first,),
        in_specs=in_specs,
        out_specs=[pick(rows, 0)] + [pick(keys, 0)] * 4,
        out_shape=[jax.ShapeDtypeStruct((rows, width), bf16)] + [jax.ShapeDtypeStruct((keys, width), bf16)] * 4,
        input_output_aliases={11 + n: n for n in range(len(begun))},
        compiler_params=pltpu.CompilerParams(vmem_limit_bytes=28 << 20),
        cost_estimate=pl.CostEstimate(
            flops=10 * rows * keys * LANES * 8 * (last - first), bytes_accessed=8 << 20, transcendentals=0
        ),
    )(
        query, upstream, mixed, lse.reshape(HEADS // 2, 2, rows), own, far, own, far,
        seg_q.reshape(1, rows), seg_own.reshape(keys, 1), seg_far.reshape(keys, 1), *begun,
    )


def columns_of(row):
    return jnp.transpose(jnp.broadcast_to(row, (LANES, row.shape[1])))


def vocab_body(info, *refs):
    blocks, (t_ref, w_ref, e_ref, stat_ref, all_ref, tall_ref, logits) = refs[:GROUP], refs[GROUP:]
    step = pl.program_id(0)
    chunk = 128

    @pl.when(step == 0)
    def _():
        all_ref[...] = jnp.zeros_like(all_ref)
        tall_ref[...] = jnp.zeros_like(tall_ref)
        for rel in range(GROUP):
            core, near = rel // 4, rel % 4
            block = (core | (near << 1)) ^ info[17]
            count, offset = info[block], info[8 + block]
            src = blocks[rel]
            for start in range(0, src.shape[0], chunk):

                @pl.when(start < count)
                def _(src=src, rel=rel, start=start, offset=offset):
                    to = pl.ds(pl.multiple_of(offset + start, 16), chunk)
                    all_ref[to, :] += src[start : start + chunk, :]
                    tall_ref[to, :] += columns_of(t_ref[rel : rel + 1, start : start + chunk])

    @pl.when(step * TILE < info[16])
    def _():
        hidden = all_ref[pl.ds(pl.multiple_of(step * TILE, TILE), TILE), :]
        outer, _, piece, _ = w_ref.shape
        wide = outer * piece
        top = None
        for n, start in enumerate(range(0, wide, piece)):
            value = dot_nt(hidden, w_ref[n, 0])
            logits[:, start : start + piece] = value
            most = jnp.max(value, 1, keepdims=True)
            top = most if top is None else jnp.maximum(top, most)
        total = None
        for start in range(0, wide, piece):
            value = jnp.exp(logits[:, start : start + piece] - top)
            added = jnp.sum(value, 1, keepdims=True)
            total = added if total is None else total + added
            e_ref[:, start : start + piece] = value.astype(bf16)
        lane = lax.broadcasted_iota(jnp.int32, (TILE, LANES), 1)
        stat_ref[...] = jnp.transpose(jnp.where(lane == 0, top, total))[:8, :]


def last_active(i, info):
    return jnp.minimum(i, jnp.maximum((info[16] + TILE - 1) // TILE - 1, 0))


def vocab_slice(w):
    outer, _, block, width = w.shape
    return pl.BlockSpec(
        (outer, 1, block, width), lambda i, info: (0, info[18], 0, 0), pipeline_mode=pl.Buffered(1)
    )


def vocab_forward(info, blocks, targets, w):
    rows, width = blocks[0].shape
    total = GROUP * rows
    wide = w.shape[0] * w.shape[2]
    once = lambda *shape: pl.BlockSpec(
        shape, lambda i, info: (0,) * len(shape), pipeline_mode=pl.Buffered(1)
    )
    return kernel_call(
        vocab_body,
        (total // TILE,),
        [once(rows, width)] * GROUP + [once(GROUP, rows), vocab_slice(w)],
        [
            pl.BlockSpec((TILE, wide), lambda i, info: (last_active(i, info), 0)),
            pl.BlockSpec((8, TILE), lambda i, info: (0, last_active(i, info))),
            once(total, width),
            once(total, LANES),
        ],
        [
            jax.ShapeDtypeStruct((total, wide), bf16),
            jax.ShapeDtypeStruct((8, total), f32),
            jax.ShapeDtypeStruct((total, width), bf16),
            jax.ShapeDtypeStruct((total, LANES), f32),
        ],
        [pltpu.VMEM((TILE, wide), f32)],
        1400 * wide * width * 2,
        36,
        prefetch=1,
    )(info, *blocks, targets, w)


def vocab_back_body(info, e_ref, w_ref, out_ref):
    @pl.when(pl.program_id(0) * TILE < info[16])
    def _():
        outer, _, piece, _ = w_ref.shape
        back = matmul(e_ref[:, :piece], w_ref[0, 0])
        for n in range(1, outer):
            back = back + matmul(e_ref[:, n * piece : (n + 1) * piece], w_ref[n, 0])
        out_ref[...] = back.astype(bf16)


def vocab_back(info, e, w):
    total, wide = e.shape
    width = w.shape[3]
    tile = lambda n: pl.BlockSpec((TILE, n), lambda i, info: (last_active(i, info), 0))
    return kernel_call(
        vocab_back_body,
        (total // TILE,),
        [tile(wide), vocab_slice(w)],
        tile(width),
        jax.ShapeDtypeStruct((total, width), bf16),
        [],
        1400 * wide * width * 2,
        24,
        prefetch=1,
    )(info, e, w)


def spread_body(info, g_ref, f_ref, *refs):
    outs, columns = refs[:-1], refs[-1]
    step = pl.program_id(0)
    total, width = g_ref.shape
    rows = outs[0].shape[0]

    @pl.when(step == 0)
    def _():
        for start in range(0, total, TILE):
            columns[start : start + TILE, :] = columns_of(f_ref[:, start : start + TILE])

    def block_of(core, near):
        block = (core | (near << 1)) ^ info[17]
        at = pl.ds(pl.multiple_of(info[8 + block], 16), rows)
        row = lax.broadcasted_iota(jnp.int32, (rows, LANES), 0)
        factor = jnp.where(row < info[block], columns[at, :], 0.0)
        live = row < info[block]
        pieces = [
            jnp.where(live, g_ref[at, start : start + LANES].astype(f32) * factor, 0.0)
            for start in range(0, width, LANES)
        ]
        return jnp.concatenate(pieces, 1).astype(bf16)

    for n, out_ref in enumerate(outs):

        @pl.when(step == n)
        def _(n=n, out_ref=out_ref):
            out_ref[...] = block_of(1 - n // 4, n % 4)


def spread(info, g, factor, rows):
    total, width = g.shape
    once = lambda *shape: pl.BlockSpec(
        shape, lambda i, info: (0,) * len(shape), pipeline_mode=pl.Buffered(1)
    )
    return kernel_call(
        spread_body,
        (GROUP,),
        [once(total, width), once(1, total)],
        [once(rows, width)] * GROUP,
        [jax.ShapeDtypeStruct((rows, width), bf16)] * GROUP,
        [pltpu.VMEM((total, LANES), f32)],
        total * width,
        24,
        prefetch=1,
    )(info, g, factor)


def vocab_grad_body(info, e_ref, h_ref, t_ref, f_ref, out_ref, total):
    step = pl.program_id(0)

    @pl.when(step == 0)
    def _():
        total[...] = jnp.zeros_like(total)

    @pl.when(step * TILE < info[16])
    def _():
        wide = e_ref.shape[1]
        piece = min(1024, wide)
        factor = columns_of(f_ref[...])[:, :1]
        target = t_ref[...][:, :1].astype(jnp.int32)
        for start in range(0, wide, piece):
            column = start + 1 + lax.broadcasted_iota(jnp.int32, (TILE, piece), 1)
            weights = e_ref[:, start : start + piece].astype(f32) * factor
            weights = (weights - jnp.where(column == target, 1.0, 0.0)).astype(bf16)
            total[start : start + piece, :] += dot_tn(weights, h_ref[...])

    @pl.when(step == pl.num_programs(0) - 1)
    def _():
        out_ref[...] = total[...].astype(bf16)


def vocab_grad(info, e, hidden, target, factor):
    total, wide = e.shape
    width = hidden.shape[1]
    tile = lambda n: pl.BlockSpec((TILE, n), lambda i, info: (last_active(i, info), 0))
    return kernel_call(
        vocab_grad_body,
        (total // TILE,),
        [
            tile(wide),
            tile(width),
            tile(LANES),
            pl.BlockSpec((1, TILE), lambda i, info: (0, last_active(i, info))),
        ],
        pl.BlockSpec((wide, width), lambda i, info: (0, 0)),
        jax.ShapeDtypeStruct((wide, width), bf16),
        [pltpu.VMEM((wide, width), f32)],
        1400 * wide * width * 2,
        40,
        prefetch=1,
    )(info, e, hidden, target, factor)


def halves_body(plan, info, *refs):
    operands, outs = refs[:-2], refs[-2:]
    rows = outs[0].shape[0]

    def fill(half, out_ref):
        at = 0
        for terms, width in plan:
            total = None
            for left, left_at, right, right_at in terms:
                if right is None:
                    lines = [operands[n][:, start : start + 2 * rows] for n, start in left]
                    blank = width - sum(line.shape[0] for line in lines)
                    lines.append(jnp.zeros((blank, 2 * rows), f32))
                    turned = jnp.transpose(jnp.concatenate(lines, 0))
                    value = jnp.where(half == 0, turned[:rows], turned[rows:])
                else:
                    lanes = pl.ds(pl.multiple_of(left_at + half * rows, rows), rows)
                    value = dot_tn(
                        operands[left][:, lanes], operands[right][:, right_at : right_at + width]
                    )
                total = value if total is None else total + value
            out_ref[:, at : at + width] = total.astype(bf16)
            at += width

    @pl.when(pl.program_id(0) == 0)
    def _():
        fill(1 - info[0], outs[0])

    @pl.when(pl.program_id(0) == 1)
    def _():
        fill(info[0], outs[1])


def weight_halves(columns, rows, vmem=36):
    operands, plan = [], []

    def index_of(array):
        for n, known in enumerate(operands):
            if known is array:
                return n
        operands.append(array)
        return len(operands) - 1

    for width, terms in columns:
        taken = []
        for left, left_at, right, right_at in terms:
            if right is None:
                taken.append(([(index_of(row), start) for row, start in left], 0, None, 0))
            else:
                taken.append((index_of(left), left_at, index_of(right), right_at))
        plan.append((taken, width))
    total = sum(width for width, _ in columns)
    whole = lambda shape: pl.BlockSpec(shape, lambda i, info: (0, 0), pipeline_mode=pl.Buffered(1))
    return kernel_call(
        functools.partial(halves_body, plan),
        (2,),
        [whole(o.shape) for o in operands],
        [whole((rows // 2, total))] * 2,
        [jax.ShapeDtypeStruct((rows // 2, total), bf16)] * 2,
        [],
        rows * total * 1024,
        vmem,
        prefetch=1,
    )(group_index([CORE_BIT])[None], *operands)


def core_summed(send, keep):
    return (keep.astype(f32) + swapped(send, CORE_BIT).astype(f32)).astype(bf16)


def joined_body(plan, info, own_ref, other_ref, *outs):
    rows = own_ref.shape[0]
    mine, far = pl.multiple_of(info[0] * rows, rows), pl.multiple_of((1 - info[0]) * rows, rows)
    for (starts, width, turned), out_ref in zip(plan, outs):
        for n, start in enumerate(starts):
            for ref, at in ((own_ref, mine), (other_ref, far)):
                value = ref[:, start : start + width].astype(f32)
                if turned:
                    out_ref[:, pl.ds(at, rows)] = jnp.transpose(value)
                else:
                    out_ref[pl.ds(n * 2 * rows + at, rows), :] = value


def joined(own, other, plan):
    rows = own.shape[0]
    shapes = [
        (width, 2 * rows) if turned else (2 * rows * len(starts), width)
        for starts, width, turned in plan
    ]
    once = lambda shape: pl.BlockSpec(shape, lambda i, info: (0, 0), pipeline_mode=pl.Buffered(1))
    return kernel_call(
        functools.partial(joined_body, plan),
        (1,),
        [once(own.shape)] * 2,
        [once(shape) for shape in shapes],
        [jax.ShapeDtypeStruct(shape, f32) for shape in shapes],
        [],
        own.size,
        36,
        prefetch=1,
    )(group_index([CORE_BIT])[None], own, other)


def per_device(
    hidden_in,
    enc_states,
    segment_ids,
    edit_pass,
    enc_segments,
    target_tokens,
    placeholder_counts,
    delete_labels,
    loss_mask,
    w_self_qkv,
    w_self_out,
    w_cross_q,
    w_cross_kv,
    w_cross_out,
    w_ffn_in,
    b_ffn_in,
    w_ffn_out,
    b_ffn_out,
    norm_gains,
    norm_shifts,
    w_vocab,
    w_pair,
    b_pair,
    w_delete,
):
    _, tokens, features = hidden_in.shape
    seq = lax.axis_index("seq")
    chip = [NEAR_BIT, SEQ_BIT]
    far = far_bits()
    hidden = hidden_in[0]
    source = enc_states[0]
    hidden_far = swapped(hidden, SEQ_BIT)
    qkv = matmul(hidden, w_self_qkv).astype(bf16)
    segment, passes, source_seg = segment_ids[0], edit_pass[0], enc_segments[0]

    keep_float = loss_mask[0].astype(f32)
    token_keep = keep_float * (passes == 2).astype(f32)
    row = lax.broadcasted_iota(jnp.int32, (tokens, tokens), 0)
    col = lax.broadcasted_iota(jnp.int32, (tokens, tokens), 1)
    rank = matmul(token_keep.astype(bf16)[None, :], (row <= col).astype(bf16)) - 1.0
    selects = (rank.astype(jnp.int32) == row) & (token_keep[None, :] > 0)
    chooser = selects.astype(bf16)
    targets = target_tokens[0]
    chosen = jnp.sum(jnp.where(selects, targets[None, :] + 1, 0), 1)
    ids_far = swapped(jnp.stack([segment, source_seg, chosen]), SEQ_BIT)
    segment_far, source_seg_far = ids_far[0], ids_far[1]

    vocab = w_vocab.shape[0]
    outer = lax.axis_size("far")
    block = vocab // (outer * GROUP)
    inner = lax.axis_index(("near", "core", "seq"))
    here = group_index([CORE_BIT, NEAR_BIT, SEQ_BIT])
    ckv = matmul(source, w_cross_kv).astype(bf16)
    kv_far = matmul(hidden_far, w_self_qkv[:, features:]).astype(bf16)
    source_far = swapped(after(source, hidden_far), SEQ_BIT)
    self_mix, self_lse = attend(qkv, 0, qkv, 4, 8, kv_far, 0, 4, segment, segment, segment_far)
    layer_one, normed_one, invert_one = norm_forward(
        hidden.astype(f32) + matmul(self_mix, w_self_out), norm_gains[0], norm_shifts[0]
    )

    chosen_row = after(jnp.stack([chosen, ids_far[2]]), self_mix)
    chosen_near = swapped(chosen_row, NEAR_BIT)
    chosen_chip = jnp.stack([chosen_row[0], chosen_near[0], chosen_row[1], chosen_near[1]])
    chosen_all = jnp.concatenate([chosen_chip, swapped(chosen_chip, CORE_BIT)])
    index = chosen_all - 1
    local = (index // (block * GROUP)) * block + index % block + 1
    mine = (chosen_all > 0) & ((index // block) % GROUP == inner)
    local_targets = jnp.where(mine, local, 0).astype(f32)
    counts_rel = jnp.sum((chosen_all > 0).astype(jnp.int32), 1)
    relative = jnp.array([c | (n << 1) for c in range(2) for n in range(4)], jnp.int32) ^ here
    counts = jnp.sum(
        jnp.where(relative[:, None] == jnp.arange(GROUP)[None, :], counts_rel[:, None], 0), 0
    )
    rounded = (counts + 15) // 16 * 16
    before = jnp.arange(GROUP)[:, None] < jnp.arange(GROUP)[None, :]
    offsets = jnp.sum(jnp.where(before, rounded[:, None], 0), 0)
    info = jnp.concatenate([counts, offsets, jnp.sum(rounded)[None], here[None], inner[None]]).astype(jnp.int32)

    one_low = layer_one.astype(bf16)
    cross_query = matmul(one_low, w_cross_q).astype(bf16)
    ckv_far = matmul(source_far, w_cross_kv).astype(bf16)
    cross_mix, cross_lse = attend(
        cross_query, 0, ckv, 0, 4, ckv_far, 0, 4, segment, source_seg, source_seg_far
    )
    layer_two, normed_two, invert_two = norm_forward(
        layer_one + matmul(cross_mix, w_cross_out), norm_gains[1], norm_shifts[1]
    )
    two_low = layer_two.astype(bf16)
    pre_act = matmul(two_low, w_ffn_in) + b_ffn_in
    activ, gate_back = jax.vjp(smooth_gate, pre_act)
    activ_low = activ.astype(bf16)
    layer_three, normed_three, invert_three = norm_forward(
        layer_two + (matmul(activ_low, w_ffn_out) + b_ffn_out), norm_gains[2], norm_shifts[2]
    )
    three_low = layer_three.astype(bf16)

    kept = matmul(chooser, three_low).astype(bf16)
    kept_core = swapped(kept, CORE_BIT)
    kept_chip = [swapped(kept, NEAR_BIT), swapped(kept, SEQ_BIT), swapped(kept, NEAR_BIT | SEQ_BIT)]
    next_row = passed_along(three_low[:1], "seq", -1)
    w_parts = w_vocab.reshape(outer, GROUP, block, features)
    target_rows = jnp.take(w_vocab, after(targets, kept), axis=0).astype(f32)
    kept_chip = [after(k, target_rows) for k in kept_chip]
    kept_other = [swapped(k, CORE_BIT) for k in kept_chip]

    delete_keep = keep_float * (passes == 0).astype(f32)

    def label_grad(logits, labels, keep_mask):
        shifted = logits - jnp.max(logits, -1, keepdims=True)
        exponent = jnp.exp(shifted)
        weights = exponent / jnp.sum(exponent, -1, keepdims=True)
        onehot = labels[:, None] == lax.broadcasted_iota(jnp.int32, logits.shape, 1)
        return ((weights - onehot.astype(f32)) * keep_mask[:, None]).astype(bf16)

    delete_grad = label_grad(matmul(three_low, w_delete), delete_labels[0], delete_keep)

    delete_back = matmul_right(delete_grad, w_delete) - target_rows * token_keep[:, None]
    d_delete = matmul_left(delete_grad, three_low)
    info = after(info, delete_back, d_delete)
    e, stats, kept_all, target_all = vocab_forward(
        info, [kept] + kept_chip + [kept_core] + kept_other, local_targets, w_parts
    )
    stats = stats[:2]

    def merged(first, *others):
        most = functools.reduce(jnp.maximum, [o[0] for o in others], first[0])
        added = sum((o[1] * jnp.exp(o[0] - most) for o in others), first[1] * jnp.exp(first[0] - most))
        return jnp.stack([most, added])

    stats_pair = merged(stats, swapped(stats, CORE_BIT))
    stats_all = merged(stats_pair, *[swapped(stats_pair, group_mask(chip, r)) for r in (1, 2, 3)])
    factor = jnp.exp(stats[0] - stats_all[0] - jnp.log(stats_all[1]))[None, :]
    back_raw = vocab_back(info, e, w_parts)
    back = spread(info, back_raw, factor, tokens)
    back_core = [swapped(b, CORE_BIT) for b in back[:4]]
    back_near = back[4:]
    back_low = [(back_near[r].astype(f32) + back_core[r].astype(f32)).astype(bf16) for r in (1, 2, 3)]
    position = seq * tokens + jnp.arange(tokens, dtype=jnp.int32)
    row_length = tokens * lax.axis_size("seq")
    follow = jnp.concatenate([three_low[1:], after(next_row, *back_low)], 0)
    follow_seg = jnp.concatenate([segment[1:], segment_far[:1]], 0)
    pair_ok = (follow_seg == segment) & (position < row_length - 1)
    pair_keep = keep_float * (passes == 1).astype(f32) * pair_ok.astype(f32)
    pair_logits = matmul(three_low, w_pair[:features]) + matmul(follow, w_pair[features:]) + b_pair
    pair_grad = label_grad(pair_logits, placeholder_counts[0], pair_keep)
    follow_grad = matmul_right(pair_grad, w_pair[features:])
    back_row = passed_along(follow_grad[-1:], "seq", 1)
    d_b_pair = jnp.sum(pair_grad.astype(f32), 0, keepdims=True)
    d_b_pair = jnp.pad(d_b_pair, ((0, 0), (0, features - d_b_pair.shape[1])))
    head_back = [swapped(back_low[r - 1], group_mask(chip, r)).astype(f32) for r in (1, 2, 3)]
    head_back = sum(head_back, back_near[0].astype(f32) + back_core[0].astype(f32))
    vocab_part = vocab_grad(info, e, kept_all, target_all, after(factor, *back_low))
    d_vocab = lax.psum_scatter(vocab_part, "far", scatter_dimension=0, tiled=True)
    grad_local = (
        delete_back
        + matmul_right(pair_grad, w_pair[:features])
        + jnp.concatenate([back_row, follow_grad[:-1]], 0)
    )
    grad_local = after(grad_local, vocab_part)

    grad_three = grad_local + matmul_left(chooser, head_back.astype(bf16))
    grad_sum3, gain_three, shift_three = norm_backward(
        grad_three, normed_three, invert_three, norm_gains[2]
    )
    branch_three = grad_sum3.astype(bf16)
    row_sum = lambda value: jnp.sum(value.astype(f32), 0, keepdims=True)
    d_b_ffn_out = row_sum(branch_three)
    grad_pre = gate_back(matmul_right(branch_three, w_ffn_out))[0].astype(bf16)
    d_b_ffn_in = row_sum(grad_pre)
    hidden_units = w_ffn_in.shape[1]
    pair_count = w_pair.shape[1]
    send_ffn, keep_ffn = weight_halves(
        [(hidden_units, [(two_low, 0, grad_pre, 0)])]
        + [(features, [(activ_low, at, branch_three, 0)]) for at in range(0, hidden_units, features)],
        features,
    )
    sum_ffn = core_summed(send_ffn, keep_ffn)
    grad_two = grad_sum3 + matmul_right(grad_pre, w_ffn_in)
    grad_sum2, gain_two, shift_two = norm_backward(grad_two, normed_two, invert_two, norm_gains[1])
    branch_two = grad_sum2.astype(bf16)
    cross_up = matmul_right(branch_two, w_cross_out).astype(bf16)
    cross_up = after(cross_up, sum_ffn)
    sum_ffn = scatter_sum(sum_ffn, chip)
    dcq, dck, dcv, dck_far, dcv_far = attend_back(
        cross_query, 0, cross_up, cross_mix, cross_lse, ckv, 0, 4, ckv_far, 0, 4,
        segment, source_seg, source_seg_far,
    )
    dcq = after(dcq, sum_ffn)
    w_ckey, w_cvalue = w_cross_kv[:, :features], w_cross_kv[:, features:]
    d_enc_low = (matmul_right(dck_far, w_ckey) + matmul_right(dcv_far, w_cvalue)).astype(bf16)
    d_enc_far = swapped(d_enc_low, SEQ_BIT)
    dcq = after(dcq, d_enc_low)
    send_mid, keep_mid = weight_halves(
        [
            (features, [(cross_mix, 0, branch_two, 0)]),
            (features, [(one_low, 0, dcq, 0)]),
            (features, [(source, 0, dck, 0), (source_far, 0, dck_far, 0)]),
            (features, [(source, 0, dcv, 0), (source_far, 0, dcv_far, 0)]),
            (pair_count, [(three_low, 0, pair_grad, 0)]),
            (pair_count, [(follow, 0, pair_grad, 0)]),
        ],
        features,
    )
    sum_mid = core_summed(send_mid, keep_mid)
    grad_one = grad_sum2 + matmul_right(after(dcq, keep_mid), w_cross_q)
    grad_sum1, gain_one, shift_one = norm_backward(grad_one, normed_one, invert_one, norm_gains[0])
    branch_one = grad_sum1.astype(bf16)
    self_up = matmul_right(branch_one, w_self_out).astype(bf16)
    self_up = after(self_up, sum_mid, d_enc_far)
    sum_mid = scatter_sum(after(sum_mid, self_up), chip)
    sum_ffn = scatter_sum(after(sum_ffn, self_up), far[:1])
    self_back = functools.partial(
        attend_back, qkv, 0, self_up, self_mix, self_lse, qkv, 4, 8, kv_far, 0, 4, segment, segment, segment_far
    )
    dq, dk, dv, dk_far, dv_far = self_back()
    dq, dk, dv, dk_far, dv_far, sum_mid, sum_ffn = lax.optimization_barrier(
        (dq, dk, dv, dk_far, dv_far, sum_mid, sum_ffn)
    )

    def from_far(value, *late):
        for bit in reversed(far):
            value = gathered(value, [bit], *late)
        return value

    w_key, w_value = w_self_qkv[:, features : 2 * features], w_self_qkv[:, 2 * features :]
    d_hidden_low = (matmul_right(dk_far, w_key) + matmul_right(dv_far, w_value)).astype(bf16)
    dq = after(dq, d_hidden_low)
    send_qkv, keep_qkv = weight_halves(
        [
            (features, [(hidden, 0, dq, 0)]),
            (features, [(hidden, 0, dk, 0), (hidden_far, 0, dk_far, 0)]),
            (features, [(hidden, 0, dv, 0), (hidden_far, 0, dv_far, 0)]),
            (features, [(self_mix, 0, branch_one, 0)]),
            (
                LANES,
                [
                    (
                        [(d_b_ffn_in, at) for at in range(0, hidden_units, features)]
                        + [(row, 0) for row in (d_b_ffn_out, gain_one, gain_two, gain_three)]
                        + [(row, 0) for row in (shift_one, shift_two, shift_three, d_b_pair)]
                        + [(d_delete, 0)],
                        0,
                        None,
                        0,
                    )
                ],
            ),
        ],
        features,
        58,
    )
    sum_qkv = after(core_summed(send_qkv, keep_qkv), d_vocab)
    d_hidden_far = swapped(d_hidden_low, SEQ_BIT)
    for bit in far[1:]:
        sum_ffn = scatter_sum(sum_ffn, [bit], keep_qkv)
    for bit in reversed(far[1:]):
        sum_ffn = gathered(sum_ffn, [bit], sum_qkv)
    sum_qkv = scatter_sum(sum_qkv, chip)
    sum_ffn = gathered(sum_ffn, far[:1], sum_qkv)
    sum_ffn = after(sum_ffn, d_hidden_far)
    sum_mid = scatter_sum(after(sum_mid, sum_qkv), far[:1])
    for bit in far[1:]:
        sum_mid = scatter_sum(sum_mid, [bit])
    sum_mid = from_far(sum_mid)
    sum_qkv = doubled(sum_qkv, far)
    sum_ffn = gathered(sum_ffn, chip, sum_mid, sum_qkv)
    ffn_other = swapped(sum_ffn, CORE_BIT)
    out_ffn_in, out_ffn_out = joined(
        sum_ffn,
        ffn_other,
        [
            ([0], hidden_units, False),
            (list(range(hidden_units, 2 * hidden_units, features)), features, False),
        ],
    )
    sum_mid = gathered(after(sum_mid, sum_ffn), chip, out_ffn_in, out_ffn_out)
    d_hidden = (
        grad_sum1
        + matmul_right(dq, w_self_qkv[:, :features])
        + matmul_right(dk, w_key)
        + matmul_right(dv, w_value)
        + d_hidden_far.astype(f32)
    )
    d_enc = matmul_right(dck, w_ckey) + matmul_right(dcv, w_cvalue) + d_enc_far.astype(f32)

    mid_other = swapped(sum_mid, CORE_BIT)
    pair_at = 4 * features
    out_cross_out, out_cross_q, out_cross_kv, out_pair = joined(
        sum_mid,
        mid_other,
        [
            ([0], features, False),
            ([features], features, False),
            ([2 * features], 2 * features, False),
            ([pair_at, pair_at + pair_count], pair_count, False),
        ],
    )
    sum_qkv = gathered(after(sum_qkv, sum_mid), chip, out_cross_out, d_hidden, d_enc)
    out_self_qkv, out_self_out, small = joined(
        sum_qkv,
        swapped(sum_qkv, CORE_BIT),
        [
            ([0], 3 * features, False),
            ([3 * features], features, False),
            ([4 * features], LANES, True),
        ],
    )
    d_vocab = after(d_vocab, small).astype(f32)
    units = hidden_units // features
    out_b_ffn_in = small[:units].reshape(-1)
    out_b_ffn_out = small[units]
    out_gains = small[units + 1 : units + 4]
    out_shifts = small[units + 4 : units + 7]
    out_b_pair = small[units + 7, :pair_count]
    out_delete = jnp.transpose(small[units + 8 : units + 10])
    return (
        three_low[None],
        d_hidden[None],
        d_enc[None],
        out_self_qkv,
        out_self_out,
        out_cross_q,
        out_cross_kv,
        out_cross_out,
        out_ffn_in,
        out_b_ffn_in,
        out_ffn_out,
        out_b_ffn_out,
        out_gains,
        out_shifts,
        d_vocab,
        out_pair,
        out_b_pair,
        out_delete,
    )


def solution(mesh):
    split_mesh = Mesh(mesh.devices.reshape(-1, 2, 2, mesh.shape["seq"]), AXES)
    rows = ("far", "near", "core")
    split = P(rows, "seq", None)
    ids = P(rows, "seq")
    return jax.shard_map(
        per_device,
        mesh=split_mesh,
        in_specs=(split, split) + (ids,) * 7 + (P(),) * 15,
        out_specs=(split,) * 3 + (P(),) * 11 + (P(AXES, None),) + (P(),) * 3,
        check_vma=False,
    )
```

```python
import functools

import jax
import jax.numpy as jnp
from jax import lax
from jax.experimental import pallas as pl
from jax.experimental.pallas import tpu as pltpu
from jax.sharding import Mesh
from jax.sharding import PartitionSpec as P

HEADS = 8
HEAD_DIM = 64
LANES = 128
SCALE = HEAD_DIM**-0.5
EPSILON = 1e-05
NEGATIVE = -1e30
TILE = 256
STEP_PAIRS = 2

SEQ_BIT, CORE_BIT, NEAR_BIT = 1, 2, 4
GROUP = 8

bf16 = jnp.bfloat16
f32 = jnp.float32


def matmul(left, right):
    return jnp.dot(left, right, preferred_element_type=f32)


def matmul_left(left, right):
    return lax.dot_general(left, right, (((0,), (0,)), ((), ())), preferred_element_type=f32)


def matmul_right(left, right):
    return lax.dot_general(left, right, (((1,), (1,)), ((), ())), preferred_element_type=f32)


def smooth_gate(value):
    return jax.nn.gelu(value, approximate=True)


def norm_forward(summed, gain_row, shift_row):
    centered = summed - jnp.mean(summed, -1, keepdims=True)
    invert = lax.rsqrt(jnp.mean(centered * centered, -1, keepdims=True) + EPSILON)
    normed = centered * invert
    return (normed * gain_row + shift_row, normed, invert)


def norm_backward(upstream, normed, invert, gain_row):
    scaled = upstream * gain_row
    centered = (
        scaled
        - jnp.mean(scaled, -1, keepdims=True)
        - normed * jnp.mean(scaled * normed, -1, keepdims=True)
    )
    return (
        centered * invert,
        jnp.sum(upstream * normed, 0, keepdims=True),
        jnp.sum(upstream, 0, keepdims=True),
    )


def passed_along(value, axis, steps):
    count = lax.axis_size(axis)
    leading, last = (max(0, -steps), min(count, count - steps))
    return lax.ppermute(value, axis, [(source, source + steps) for source in range(leading, last)])


AXES = ("far", "near", "core", "seq")


def place():
    return lax.axis_index(AXES)


def place_count():
    return lax.axis_size("far") * GROUP


def swapped(value, mask):
    return lax.ppermute(value, AXES, [(i, i ^ mask) for i in range(place_count())])


def after(value, *others):
    return lax.optimization_barrier((value,) + others)[0]


def group_index(bits):
    me = place()
    return sum(((me & bit) != 0).astype(jnp.int32) << n for n, bit in enumerate(bits))


def group_mask(bits, relative):
    return sum(bit for n, bit in enumerate(bits) if (relative >> n) & 1)


def scatter_sum(value, bits, *late):
    count = 1 << len(bits)
    rows = value.shape[0] // count
    index = group_index(bits)
    part = lambda relative: lax.dynamic_slice_in_dim(value, (index ^ relative) * rows, rows)
    total = part(0).astype(f32)
    others = [swapped(part(r), group_mask(bits, r)) for r in range(1, count)]
    if late:
        others = [after(other, *late) for other in others]
    for other in others:
        total = total + other.astype(f32)
    return total.astype(bf16)


def gathered(value, bits, *late):
    count = 1 << len(bits)
    index = group_index(bits)
    parts = [value] + [swapped(value, group_mask(bits, r)) for r in range(1, count)]
    if late:
        parts = [after(part, *late) for part in parts]
    for n in range(len(bits)):
        odd = ((index >> n) & 1) == 1
        parts = [
            jnp.where(odd, jnp.concatenate([second, first], 0), jnp.concatenate([first, second], 0))
            for first, second in zip(parts[::2], parts[1::2])
        ]
    return parts[0]


def doubled(value, bits, *late):
    for bit in bits:
        other = swapped(value, bit)
        if late:
            other = after(other, *late)
        value = (value.astype(f32) + other.astype(f32)).astype(bf16)
    return value


def far_bits():
    count = place_count()
    return [1 << n for n in range(3, count.bit_length() - 1)]


def kernel_call(body, grid, in_specs, out_specs, out_shape, scratch, flops, vmem, prefetch=0):
    return pl.pallas_call(
        body,
        grid_spec=pltpu.PrefetchScalarGridSpec(
            num_scalar_prefetch=prefetch,
            grid=grid,
            in_specs=in_specs,
            out_specs=out_specs,
            scratch_shapes=scratch,
        ),
        out_shape=out_shape,
        compiler_params=pltpu.CompilerParams(vmem_limit_bytes=vmem << 20),
        cost_estimate=pl.CostEstimate(flops=flops, bytes_accessed=8 << 20, transcendentals=0),
    )


def dot_nt(left, right):
    return lax.dot_general(left, right, (((1,), (1,)), ((), ())), preferred_element_type=f32)


def dot_tn(left, right):
    return lax.dot_general(left, right, (((0,), (0,)), ((), ())), preferred_element_type=f32)


def head_lanes(shape, head):
    lane = lax.broadcasted_iota(jnp.int32, shape, 1)
    return (lane >= HEAD_DIM) == (head == 1)


def attend_body(q_ref, ko_ref, kr_ref, vo_ref, vr_ref, sq_ref, so_ref, sr_ref, out_ref, lse_ref, stat):
    step = pl.program_id(0)
    rows = q_ref.shape[0]
    heads = 2 * STEP_PAIRS

    @pl.when(step == 0)
    def _():
        stat[...] = jnp.zeros_like(stat)

    lane = lax.broadcasted_iota(jnp.int32, (rows, LANES), 1)
    same_own = sq_ref[...] == so_ref[...]
    same_far = sq_ref[...] == sr_ref[...]

    def scores(head):
        at = slice(head // 2 * LANES, (head // 2 + 1) * LANES)
        queries = q_ref[:, at].astype(f32) * SCALE
        queries = jnp.where(head_lanes((rows, LANES), head % 2), queries, 0.0).astype(bf16)
        return (
            jnp.where(same_own, dot_nt(queries, ko_ref[:, at]), NEGATIVE),
            jnp.where(same_far, dot_nt(queries, kr_ref[:, at]), NEGATIVE),
        )

    kept = stat[...]
    mixed = []
    ahead = scores(0)
    for head in range(heads):
        s_own, s_far = ahead
        if head + 1 < heads:
            ahead = scores(head + 1)
        top = jnp.maximum(jnp.max(s_own, 1, keepdims=True), jnp.max(s_far, 1, keepdims=True))
        e_own = jnp.exp(s_own - top)
        e_far = jnp.exp(s_far - top)
        total = jnp.sum(e_own, 1, keepdims=True) + jnp.sum(e_far, 1, keepdims=True)
        at = slice(head // 2 * LANES, (head // 2 + 1) * LANES)
        mix = matmul(e_own.astype(bf16), vo_ref[:, at]) + matmul(e_far.astype(bf16), vr_ref[:, at])
        mixed.append(mix / total)
        kept = jnp.where(lane == heads * step + head, top + jnp.log(total), kept)
    for pair in range(STEP_PAIRS):
        at = slice(pair * LANES, (pair + 1) * LANES)
        out_ref[:, at] = jnp.where(lane < HEAD_DIM, mixed[2 * pair], mixed[2 * pair + 1]).astype(bf16)
    stat[...] = kept

    @pl.when(step == pl.num_programs(0) - 1)
    def _():
        lse_ref[...] = jnp.transpose(stat[...])[:HEADS, :]


def attend(query, q_at, own, ko_at, vo_at, far, kr_at, vr_at, seg_q, seg_own, seg_far):
    rows, keys = query.shape[0], own.shape[0]
    pick = lambda n, at: pl.BlockSpec(
        (n, STEP_PAIRS * LANES), lambda h, at=at: (0, at // STEP_PAIRS + h)
    )
    whole = lambda *shape: pl.BlockSpec(shape, lambda h: (0, 0))
    return kernel_call(
        attend_body,
        (HEADS // 2 // STEP_PAIRS,),
        [
            pick(rows, q_at),
            pick(keys, ko_at),
            pick(keys, kr_at),
            pick(keys, vo_at),
            pick(keys, vr_at),
            whole(rows, 1),
            whole(1, keys),
            whole(1, keys),
        ],
        [pick(rows, 0), whole(HEADS, rows)],
        [
            jax.ShapeDtypeStruct((rows, HEADS * HEAD_DIM), bf16),
            jax.ShapeDtypeStruct((HEADS, rows), f32),
        ],
        [pltpu.VMEM((rows, LANES), f32)],
        16 * rows * keys * 512,
        40,
    )(query, own, far, own, far, seg_q.reshape(rows, 1), seg_own.reshape(1, keys), seg_far.reshape(1, keys))


def attend_back_body(
    q_ref, g_ref, o_ref, lse_ref, ko_ref, kr_ref, vo_ref, vr_ref, sq_ref, so_ref, sr_ref,
    dq_ref, dko_ref, dvo_ref, dkr_ref, dvr_ref,
):
    rows = q_ref.shape[0]
    which = lax.broadcasted_iota(jnp.int32, (8, LANES), 0)
    lane = lax.broadcasted_iota(jnp.int32, (8, LANES), 1)
    chooser = jnp.where((lane >= HEAD_DIM) == (which == 1), 1.0, 0.0).astype(f32)
    along, q_of, g_of = [], [], []
    for pair in range(STEP_PAIRS):
        at = slice(pair * LANES, (pair + 1) * LANES)
        queries = q_ref[:, at].astype(f32) * SCALE
        upstream = g_ref[:, at].astype(f32)
        rows_along = lax.dot_general(
            chooser,
            upstream * o_ref[:, at].astype(f32),
            (((1,), (1,)), ((), ())),
            precision=lax.Precision.HIGHEST,
            preferred_element_type=f32,
        )
        for head in range(2):
            mine = head_lanes((rows, LANES), head)
            along.append(rows_along[head : head + 1, :])
            q_of.append(jnp.where(mine, queries, 0.0).astype(bf16))
            g_of.append(jnp.where(mine, upstream, 0.0).astype(bf16))
    halves = (
        (ko_ref, vo_ref, so_ref, dko_ref, dvo_ref),
        (kr_ref, vr_ref, sr_ref, dkr_ref, dvr_ref),
    )
    units = [
        (pair, head, half) for pair in range(STEP_PAIRS) for half in range(2) for head in range(2)
    ]

    def products(unit):
        pair, head, half = unit
        at = slice(pair * LANES, (pair + 1) * LANES)
        k_ref, v_ref = halves[half][:2]
        return dot_nt(k_ref[:, at], q_of[2 * pair + head]), dot_nt(v_ref[:, at], g_of[2 * pair + head])

    dq_of = [None] * (2 * STEP_PAIRS)
    ahead = products(units[0])
    for n, unit in enumerate(units):
        pair, head, half = unit
        index = 2 * pair + head
        at = slice(pair * LANES, (pair + 1) * LANES)
        k_ref, _, s_ref, dk_ref, dv_ref = halves[half]
        scores, back = ahead
        if n + 1 < len(units):
            ahead = products(units[n + 1])
        same = s_ref[...] == sq_ref[...]
        weights = jnp.exp(jnp.where(same, scores, NEGATIVE) - lse_ref[pair, head : head + 1, :])
        grad = (weights * (back - along[index])).astype(bf16)
        dv = matmul(weights.astype(bf16), g_of[index])
        dk = matmul(grad, q_of[index])
        if head == 0:
            key_t = jnp.transpose(k_ref[:, at].astype(f32)).astype(bf16)
            first = (dk, dv)
        else:
            dk_ref[:, at] = (first[0] + dk).astype(bf16)
            dv_ref[:, at] = (first[1] + dv).astype(bf16)
        dq = matmul(key_t[head * HEAD_DIM : (head + 1) * HEAD_DIM, :], grad)
        dq_of[index] = dq if dq_of[index] is None else dq_of[index] + dq
    for pair in range(STEP_PAIRS):
        at = slice(pair * LANES, (pair + 1) * LANES)
        dq = jnp.concatenate(dq_of[2 * pair : 2 * pair + 2], 0)
        dq_ref[:, at] = (jnp.transpose(dq) * SCALE).astype(bf16)


def attend_back(query, q_at, upstream, mixed, lse, own, ko_at, vo_at, far, kr_at, vr_at, seg_q, seg_own, seg_far):
    rows, keys = query.shape[0], own.shape[0]
    pick = lambda n, at: pl.BlockSpec(
        (n, STEP_PAIRS * LANES), lambda h, at=at: (0, at // STEP_PAIRS + h)
    )
    whole = lambda *shape: pl.BlockSpec(shape, lambda h: (0, 0))
    width = HEADS * HEAD_DIM
    return kernel_call(
        attend_back_body,
        (HEADS // 2 // STEP_PAIRS,),
        [
            pick(rows, q_at),
            pick(rows, 0),
            pick(rows, 0),
            pl.BlockSpec((STEP_PAIRS, 2, rows), lambda h: (h, 0, 0)),
            pick(keys, ko_at),
            pick(keys, kr_at),
            pick(keys, vo_at),
            pick(keys, vr_at),
            whole(1, rows),
            whole(keys, 1),
            whole(keys, 1),
        ],
        [pick(rows, 0)] + [pick(keys, 0)] * 4,
        [jax.ShapeDtypeStruct((rows, width), bf16)] + [jax.ShapeDtypeStruct((keys, width), bf16)] * 4,
        [],
        40 * rows * keys * 512,
        40,
    )(
        query, upstream, mixed, lse.reshape(HEADS // 2, 2, rows), own, far, own, far,
        seg_q.reshape(1, rows), seg_own.reshape(keys, 1), seg_far.reshape(keys, 1),
    )


def columns_of(row):
    return jnp.transpose(jnp.broadcast_to(row, (LANES, row.shape[1])))


def vocab_body(info, *refs):
    blocks, (t_ref, w_ref, e_ref, stat_ref, hidden_ref, kept, targets, logits) = refs[:GROUP], refs[GROUP:]
    step = pl.program_id(0)
    chunk = 128

    @pl.when(step == 0)
    def _():
        for start in range(0, kept.shape[0], TILE):

            @pl.when(start < info[16])
            def _(start=start):
                kept[start : start + TILE, :] = jnp.zeros((TILE, kept.shape[1]), kept.dtype)
                targets[start : start + TILE, :] = jnp.zeros((TILE, LANES), f32)

        for rel in range(GROUP):
            core, near = rel // 4, rel % 4
            block = (core | (near << 1)) ^ info[17]
            count, offset = info[block], info[8 + block]
            src = blocks[rel]
            for start in range(0, src.shape[0], chunk):

                @pl.when(start < count)
                def _(src=src, rel=rel, start=start, offset=offset):
                    for piece in range(start, start + chunk, 16):

                        @pl.when(piece < count)
                        def _(piece=piece):
                            to = pl.ds(pl.multiple_of(offset + piece, 16), 16)
                            kept[to, :] = src[piece : piece + 16, :]

                    value = columns_of(t_ref[rel : rel + 1, start : start + chunk])
                    for piece in range(start, start + chunk, 16):

                        @pl.when(piece < count)
                        def _(piece=piece):
                            to = pl.ds(pl.multiple_of(offset + piece, 16), 16)
                            targets[to, :] = value[piece - start : piece - start + 16, :]

    @pl.when(step * TILE < info[16])
    def _():
        rows = pl.ds(pl.multiple_of(step * TILE, TILE), TILE)
        hidden = kept[rows, :]
        hidden_ref[...] = hidden
        outer, _, piece, _ = w_ref.shape
        wide = outer * piece
        top = None
        for n, start in enumerate(range(0, wide, piece)):
            value = dot_nt(hidden, w_ref[n, 0])
            logits[:, start : start + piece] = value
            most = jnp.max(value, 1, keepdims=True)
            top = most if top is None else jnp.maximum(top, most)
        total = None
        for start in range(0, wide, piece):
            value = jnp.exp(logits[:, start : start + piece] - top)
            added = jnp.sum(value, 1, keepdims=True)
            total = added if total is None else total + added
            e_ref[:, start : start + piece] = value.astype(bf16)
        lane = lax.broadcasted_iota(jnp.int32, (TILE, LANES), 1)
        kind = jnp.where(lane == 0, top, jnp.where(lane == 1, total, targets[rows, :]))
        stat_ref[...] = jnp.transpose(kind)[:8, :]


def last_active(i, info):
    return jnp.minimum(i, jnp.maximum((info[16] + TILE - 1) // TILE - 1, 0))


def vocab_slice(w):
    outer, _, block, width = w.shape
    return pl.BlockSpec(
        (outer, 1, block, width), lambda i, info: (0, info[18], 0, 0), pipeline_mode=pl.Buffered(1)
    )


def vocab_forward(info, blocks, targets, w):
    rows, width = blocks[0].shape
    total = GROUP * rows
    wide = w.shape[0] * w.shape[2]
    once = lambda *shape: pl.BlockSpec(
        shape, lambda i, info: (0,) * len(shape), pipeline_mode=pl.Buffered(1)
    )
    return kernel_call(
        vocab_body,
        (total // TILE,),
        [once(rows, width)] * GROUP + [once(GROUP, rows), vocab_slice(w)],
        [
            pl.BlockSpec((TILE, wide), lambda i, info: (last_active(i, info), 0)),
            pl.BlockSpec((8, TILE), lambda i, info: (0, last_active(i, info))),
            pl.BlockSpec((TILE, width), lambda i, info: (last_active(i, info), 0)),
        ],
        [
            jax.ShapeDtypeStruct((total, wide), bf16),
            jax.ShapeDtypeStruct((8, total), f32),
            jax.ShapeDtypeStruct((total, width), bf16),
        ],
        [
            pltpu.VMEM((total, width), bf16),
            pltpu.VMEM((total, LANES), f32),
            pltpu.VMEM((TILE, wide), f32),
        ],
        1400 * wide * width * 2,
        36,
        prefetch=1,
    )(info, *blocks, targets, w)


def vocab_back_body(info, e_ref, w_ref, out_ref):
    @pl.when(pl.program_id(0) * TILE < info[16])
    def _():
        outer, _, piece, _ = w_ref.shape
        back = matmul(e_ref[:, :piece], w_ref[0, 0])
        for n in range(1, outer):
            back = back + matmul(e_ref[:, n * piece : (n + 1) * piece], w_ref[n, 0])
        out_ref[...] = back.astype(bf16)


def vocab_back(info, e, w):
    total, wide = e.shape
    width = w.shape[3]
    tile = lambda n: pl.BlockSpec((TILE, n), lambda i, info: (last_active(i, info), 0))
    return kernel_call(
        vocab_back_body,
        (total // TILE,),
        [tile(wide), vocab_slice(w)],
        tile(width),
        jax.ShapeDtypeStruct((total, width), bf16),
        [],
        1400 * wide * width * 2,
        24,
        prefetch=1,
    )(info, e, w)


def spread_body(info, g_ref, f_ref, *refs):
    outs, columns = refs[:-1], refs[-1]
    step = pl.program_id(0)
    total, width = g_ref.shape
    rows = outs[0].shape[0]

    @pl.when(step == 0)
    def _():
        for start in range(0, total, TILE):
            columns[start : start + TILE, :] = columns_of(f_ref[:, start : start + TILE])

    def block_of(core, near):
        block = (core | (near << 1)) ^ info[17]
        at = pl.ds(pl.multiple_of(info[8 + block], 16), rows)
        row = lax.broadcasted_iota(jnp.int32, (rows, LANES), 0)
        factor = jnp.where(row < info[block], columns[at, :], 0.0)
        live = row < info[block]
        pieces = [
            jnp.where(live, g_ref[at, start : start + LANES].astype(f32) * factor, 0.0)
            for start in range(0, width, LANES)
        ]
        return jnp.concatenate(pieces, 1).astype(bf16)

    for n, out_ref in enumerate(outs):

        @pl.when(step == n)
        def _(n=n, out_ref=out_ref):
            out_ref[...] = block_of(1 - n // 4, n % 4)


def spread(info, g, factor, rows):
    total, width = g.shape
    once = lambda *shape: pl.BlockSpec(
        shape, lambda i, info: (0,) * len(shape), pipeline_mode=pl.Buffered(1)
    )
    return kernel_call(
        spread_body,
        (GROUP,),
        [once(total, width), once(1, total)],
        [once(rows, width)] * GROUP,
        [jax.ShapeDtypeStruct((rows, width), bf16)] * GROUP,
        [pltpu.VMEM((total, LANES), f32)],
        total * width,
        24,
        prefetch=1,
    )(info, g, factor)


def vocab_grad_body(info, e_ref, h_ref, s_ref, f_ref, out_ref, total):
    step = pl.program_id(0)

    @pl.when(step == 0)
    def _():
        total[...] = jnp.zeros_like(total)

    @pl.when(step * TILE < info[16])
    def _():
        wide = e_ref.shape[1]
        piece = min(1024, wide)
        factor = columns_of(f_ref[...])[:, :1]
        target = columns_of(s_ref[2:3, :])[:, :1].astype(jnp.int32)
        for start in range(0, wide, piece):
            column = start + 1 + lax.broadcasted_iota(jnp.int32, (TILE, piece), 1)
            weights = e_ref[:, start : start + piece].astype(f32) * factor
            weights = (weights - jnp.where(column == target, 1.0, 0.0)).astype(bf16)
            total[start : start + piece, :] += dot_tn(weights, h_ref[...])

    @pl.when(step == pl.num_programs(0) - 1)
    def _():
        out_ref[...] = total[...].astype(bf16)


def vocab_grad(info, e, hidden, stats, factor):
    total, wide = e.shape
    width = hidden.shape[1]
    tile = lambda n: pl.BlockSpec((TILE, n), lambda i, info: (last_active(i, info), 0))
    return kernel_call(
        vocab_grad_body,
        (total // TILE,),
        [
            tile(wide),
            tile(width),
            pl.BlockSpec((8, TILE), lambda i, info: (0, last_active(i, info))),
            pl.BlockSpec((1, TILE), lambda i, info: (0, last_active(i, info))),
        ],
        pl.BlockSpec((wide, width), lambda i, info: (0, 0)),
        jax.ShapeDtypeStruct((wide, width), bf16),
        [pltpu.VMEM((wide, width), f32)],
        1400 * wide * width * 2,
        40,
        prefetch=1,
    )(info, e, hidden, stats, factor)


def halves_body(plan, info, *refs):
    operands, outs = refs[:-2], refs[-2:]
    rows = outs[0].shape[0]

    def fill(half, out_ref):
        at = 0
        for terms, width in plan:
            total = None
            for left, left_at, right, right_at in terms:
                if right is None:
                    lines = [operands[n][:, start : start + 2 * rows] for n, start in left]
                    blank = width - sum(line.shape[0] for line in lines)
                    lines.append(jnp.zeros((blank, 2 * rows), f32))
                    turned = jnp.transpose(jnp.concatenate(lines, 0))
                    value = jnp.where(half == 0, turned[:rows], turned[rows:])
                else:
                    lanes = pl.ds(pl.multiple_of(left_at + half * rows, rows), rows)
                    value = dot_tn(
                        operands[left][:, lanes], operands[right][:, right_at : right_at + width]
                    )
                total = value if total is None else total + value
            out_ref[:, at : at + width] = total.astype(bf16)
            at += width

    @pl.when(pl.program_id(0) == 0)
    def _():
        fill(1 - info[0], outs[0])

    @pl.when(pl.program_id(0) == 1)
    def _():
        fill(info[0], outs[1])


def weight_halves(columns, rows, vmem=36):
    operands, plan = [], []

    def index_of(array):
        for n, known in enumerate(operands):
            if known is array:
                return n
        operands.append(array)
        return len(operands) - 1

    for width, terms in columns:
        taken = []
        for left, left_at, right, right_at in terms:
            if right is None:
                taken.append(([(index_of(row), start) for row, start in left], 0, None, 0))
            else:
                taken.append((index_of(left), left_at, index_of(right), right_at))
        plan.append((taken, width))
    total = sum(width for width, _ in columns)
    whole = lambda shape: pl.BlockSpec(shape, lambda i, info: (0, 0), pipeline_mode=pl.Buffered(1))
    return kernel_call(
        functools.partial(halves_body, plan),
        (2,),
        [whole(o.shape) for o in operands],
        [whole((rows // 2, total))] * 2,
        [jax.ShapeDtypeStruct((rows // 2, total), bf16)] * 2,
        [],
        rows * total * 1024,
        vmem,
        prefetch=1,
    )(group_index([CORE_BIT])[None], *operands)


def core_summed(send, keep):
    return (keep.astype(f32) + swapped(send, CORE_BIT).astype(f32)).astype(bf16)


def joined_body(plan, info, own_ref, other_ref, *outs):
    rows = own_ref.shape[0]
    mine, far = pl.multiple_of(info[0] * rows, rows), pl.multiple_of((1 - info[0]) * rows, rows)
    for (starts, width, turned), out_ref in zip(plan, outs):
        for n, start in enumerate(starts):
            for ref, at in ((own_ref, mine), (other_ref, far)):
                value = ref[:, start : start + width].astype(f32)
                if turned:
                    out_ref[:, pl.ds(at, rows)] = jnp.transpose(value)
                else:
                    out_ref[pl.ds(n * 2 * rows + at, rows), :] = value


def joined(own, other, plan):
    rows = own.shape[0]
    shapes = [
        (width, 2 * rows) if turned else (2 * rows * len(starts), width)
        for starts, width, turned in plan
    ]
    once = lambda shape: pl.BlockSpec(shape, lambda i, info: (0, 0), pipeline_mode=pl.Buffered(1))
    return kernel_call(
        functools.partial(joined_body, plan),
        (1,),
        [once(own.shape)] * 2,
        [once(shape) for shape in shapes],
        [jax.ShapeDtypeStruct(shape, f32) for shape in shapes],
        [],
        own.size,
        36,
        prefetch=1,
    )(group_index([CORE_BIT])[None], own, other)


def as_columns_body(rows_ref, *outs):
    for n, out_ref in enumerate(outs):
        out_ref[...] = columns_of(rows_ref[n : n + 1, :])[:, :1].astype(jnp.int32)


def as_columns(*rows):
    count = rows[0].shape[0]
    whole = lambda *shape: pl.BlockSpec(shape, lambda i, info: (0, 0))
    return kernel_call(
        as_columns_body_with_info,
        (1,),
        [whole(len(rows), count)],
        [whole(count, 1)] * len(rows),
        [jax.ShapeDtypeStruct((count, 1), jnp.int32)] * len(rows),
        [],
        count,
        16,
        prefetch=1,
    )(jnp.zeros((1,), jnp.int32), jnp.stack(rows).astype(f32))


def as_columns_body_with_info(info, *refs):
    as_columns_body(*refs)


def added_body(info, *refs):
    count = len(refs) // 3
    for n in range(count):
        total = refs[n][...].astype(f32) + refs[count + n][...].astype(f32)
        refs[2 * count + n][...] = total.astype(bf16)


def added(firsts, seconds):
    rows, width = firsts[0].shape
    piece = pl.BlockSpec((rows // 4, width), lambda i, info: (i, 0))
    return kernel_call(
        added_body,
        (4,),
        [piece] * (2 * len(firsts)),
        [piece] * len(firsts),
        [jax.ShapeDtypeStruct((rows, width), bf16)] * len(firsts),
        [],
        rows * width,
        58,
        prefetch=1,
    )(jnp.zeros((1,), jnp.int32), *firsts, *seconds)


def per_device(
    hidden_in,
    enc_states,
    segment_ids,
    edit_pass,
    enc_segments,
    target_tokens,
    placeholder_counts,
    delete_labels,
    loss_mask,
    w_self_qkv,
    w_self_out,
    w_cross_q,
    w_cross_kv,
    w_cross_out,
    w_ffn_in,
    b_ffn_in,
    w_ffn_out,
    b_ffn_out,
    norm_gains,
    norm_shifts,
    w_vocab,
    w_pair,
    b_pair,
    w_delete,
):
    _, tokens, features = hidden_in.shape
    seq = lax.axis_index("seq")
    chip = [NEAR_BIT, SEQ_BIT]
    far = far_bits()
    hidden = hidden_in[0]
    source = enc_states[0]
    hidden_far = swapped(hidden, SEQ_BIT)
    qkv = matmul(hidden, w_self_qkv).astype(bf16)
    segment, passes, source_seg = segment_ids[0], edit_pass[0], enc_segments[0]

    keep_float = loss_mask[0].astype(f32)
    token_keep = keep_float * (passes == 2).astype(f32)
    row = lax.broadcasted_iota(jnp.int32, (tokens, tokens), 0)
    col = lax.broadcasted_iota(jnp.int32, (tokens, tokens), 1)
    rank = matmul(token_keep.astype(bf16)[None, :], (row <= col).astype(bf16)) - 1.0
    selects = (rank.astype(jnp.int32) == row) & (token_keep[None, :] > 0)
    chooser = selects.astype(bf16)
    targets = target_tokens[0]
    chosen = jnp.sum(jnp.where(selects, targets[None, :] + 1, 0), 1)
    ids_far = swapped(jnp.stack([segment, source_seg, chosen]), SEQ_BIT)
    segment_far, source_seg_far = ids_far[0], ids_far[1]

    vocab = w_vocab.shape[0]
    outer = lax.axis_size("far")
    block = vocab // (outer * GROUP)
    inner = lax.axis_index(("near", "core", "seq"))
    here = group_index([CORE_BIT, NEAR_BIT, SEQ_BIT])
    ckv = matmul(source, w_cross_kv).astype(bf16)
    hidden_far = after(hidden_far, ckv, qkv, chosen)
    kv_far = matmul(hidden_far, w_self_qkv[:, features:]).astype(bf16)
    source_far = swapped(after(source, hidden_far), SEQ_BIT)
    self_mix, self_lse = attend(qkv, 0, qkv, 4, 8, kv_far, 0, 4, segment, segment, segment_far)
    chosen_row = jnp.stack([chosen, ids_far[2]])
    chosen_near = swapped(chosen_row, NEAR_BIT)
    self_mix, self_lse, source_far, chosen_near = lax.optimization_barrier(
        (self_mix, self_lse, source_far, chosen_near)
    )
    layer_one, normed_one, invert_one = norm_forward(
        hidden.astype(f32) + matmul(self_mix, w_self_out), norm_gains[0], norm_shifts[0]
    )

    chosen_chip = jnp.stack([chosen_row[0], chosen_near[0], chosen_row[1], chosen_near[1]])
    chosen_core = swapped(chosen_chip, CORE_BIT)
    one_low = layer_one.astype(bf16)
    cross_query = matmul(one_low, w_cross_q).astype(bf16)
    ckv_far = matmul(source_far, w_cross_kv).astype(bf16)
    cross_mix, cross_lse = attend(
        cross_query, 0, ckv, 0, 4, ckv_far, 0, 4, segment, source_seg, source_seg_far
    )
    cross_mix, cross_lse, chosen_core = lax.optimization_barrier((cross_mix, cross_lse, chosen_core))
    chosen_all = jnp.concatenate([chosen_chip, chosen_core])
    index = chosen_all - 1
    local = (index // (block * GROUP)) * block + index % block + 1
    mine = (chosen_all > 0) & ((index // block) % GROUP == inner)
    local_targets = jnp.where(mine, local, 0).astype(f32)
    counts_rel = jnp.sum((chosen_all > 0).astype(jnp.int32), 1)
    relative = jnp.array([c | (n << 1) for c in range(2) for n in range(4)], jnp.int32) ^ here
    counts = jnp.sum(
        jnp.where(relative[:, None] == jnp.arange(GROUP)[None, :], counts_rel[:, None], 0), 0
    )
    rounded = (counts + 15) // 16 * 16
    before = jnp.arange(GROUP)[:, None] < jnp.arange(GROUP)[None, :]
    offsets = jnp.sum(jnp.where(before, rounded[:, None], 0), 0)
    info = jnp.concatenate([counts, offsets, jnp.sum(rounded)[None], here[None], inner[None]]).astype(jnp.int32)

    layer_two, normed_two, invert_two = norm_forward(
        layer_one + matmul(cross_mix, w_cross_out), norm_gains[1], norm_shifts[1]
    )
    two_low = layer_two.astype(bf16)
    pre_act = matmul(two_low, w_ffn_in) + b_ffn_in
    activ, gate_back = jax.vjp(smooth_gate, pre_act)
    activ_low = activ.astype(bf16)
    layer_three, normed_three, invert_three = norm_forward(
        layer_two + (matmul(activ_low, w_ffn_out) + b_ffn_out), norm_gains[2], norm_shifts[2]
    )
    three_low = layer_three.astype(bf16)

    kept = matmul(chooser, three_low).astype(bf16)
    kept_core = swapped(kept, CORE_BIT)
    kept_chip = [swapped(kept, NEAR_BIT), swapped(kept, SEQ_BIT), swapped(kept, NEAR_BIT | SEQ_BIT)]
    next_row = passed_along(three_low[:1], "seq", -1)
    w_parts = w_vocab.reshape(outer, GROUP, block, features)
    target_rows = jnp.take(w_vocab, after(targets, kept), axis=0).astype(f32)
    kept_chip = [after(k, target_rows) for k in kept_chip]
    kept_other = [swapped(k, CORE_BIT) for k in kept_chip]

    delete_keep = keep_float * (passes == 0).astype(f32)

    def label_grad(logits, labels, keep_mask):
        shifted = logits - jnp.max(logits, -1, keepdims=True)
        exponent = jnp.exp(shifted)
        weights = exponent / jnp.sum(exponent, -1, keepdims=True)
        onehot = labels[:, None] == lax.broadcasted_iota(jnp.int32, logits.shape, 1)
        return ((weights - onehot.astype(f32)) * keep_mask[:, None]).astype(bf16)

    delete_grad = label_grad(matmul(three_low, w_delete), delete_labels[0], delete_keep)

    delete_back = matmul_right(delete_grad, w_delete) - target_rows * token_keep[:, None]
    d_delete = matmul_left(delete_grad, three_low)
    segment_col, segment_far_col, source_col, source_far_col = as_columns(
        segment, segment_far, source_seg, source_seg_far
    )
    info, segment_col, segment_far_col, source_col, source_far_col = lax.optimization_barrier(
        (info, segment_col, segment_far_col, source_col, source_far_col)
    )
    info = after(info, delete_back, d_delete)
    e, stat_rows, kept_all = vocab_forward(
        info, [kept] + kept_chip + [kept_core] + kept_other, local_targets, w_parts
    )
    stats = stat_rows[:2]

    def merged(first, *others):
        most = functools.reduce(jnp.maximum, [o[0] for o in others], first[0])
        added = sum((o[1] * jnp.exp(o[0] - most) for o in others), first[1] * jnp.exp(first[0] - most))
        return jnp.stack([most, added])

    stats_pair = merged(stats, swapped(stats, CORE_BIT))
    stats_all = merged(stats_pair, *[swapped(stats_pair, group_mask(chip, r)) for r in (1, 2, 3)])
    factor = jnp.exp(stats[0] - stats_all[0] - jnp.log(stats_all[1]))[None, :]
    back_raw = vocab_back(info, e, w_parts)
    back = spread(info, back_raw, factor, tokens)
    back_core = [swapped(b, CORE_BIT) for b in back[:4]]
    back_near = back[4:]
    back_low = added(back_near[1:], back_core[1:])
    position = seq * tokens + jnp.arange(tokens, dtype=jnp.int32)
    row_length = tokens * lax.axis_size("seq")
    follow = jnp.concatenate([three_low[1:], after(next_row, *back_low)], 0)
    follow_seg = jnp.concatenate([segment[1:], segment_far[:1]], 0)
    pair_ok = (follow_seg == segment) & (position < row_length - 1)
    pair_keep = keep_float * (passes == 1).astype(f32) * pair_ok.astype(f32)
    pair_logits = matmul(three_low, w_pair[:features]) + matmul(follow, w_pair[features:]) + b_pair
    pair_grad = label_grad(pair_logits, placeholder_counts[0], pair_keep)
    follow_grad = matmul_right(pair_grad, w_pair[features:])
    back_row = passed_along(follow_grad[-1:], "seq", 1)
    d_b_pair = jnp.sum(pair_grad.astype(f32), 0, keepdims=True)
    d_b_pair = jnp.pad(d_b_pair, ((0, 0), (0, features - d_b_pair.shape[1])))
    head_back = [swapped(back_low[r - 1], group_mask(chip, r)).astype(f32) for r in (1, 2, 3)]
    head_back = sum(head_back, back_near[0].astype(f32) + back_core[0].astype(f32))
    vocab_part = vocab_grad(info, e, kept_all, stat_rows, after(factor, *back_low))
    d_vocab = lax.psum_scatter(vocab_part, "far", scatter_dimension=0, tiled=True)
    grad_local = (
        delete_back
        + matmul_right(pair_grad, w_pair[:features])
        + jnp.concatenate([back_row, follow_grad[:-1]], 0)
    )
    grad_local = after(grad_local, vocab_part)

    grad_three = grad_local + matmul_left(chooser, head_back.astype(bf16))
    grad_sum3, gain_three, shift_three = norm_backward(
        grad_three, normed_three, invert_three, norm_gains[2]
    )
    branch_three = grad_sum3.astype(bf16)
    row_sum = lambda value: jnp.sum(value.astype(f32), 0, keepdims=True)
    d_b_ffn_out = row_sum(branch_three)
    grad_pre = gate_back(matmul_right(branch_three, w_ffn_out))[0].astype(bf16)
    d_b_ffn_in = row_sum(grad_pre)
    hidden_units = w_ffn_in.shape[1]
    pair_count = w_pair.shape[1]
    send_ffn, keep_ffn = weight_halves(
        [(hidden_units, [(two_low, 0, grad_pre, 0)])]
        + [(features, [(activ_low, at, branch_three, 0)]) for at in range(0, hidden_units, features)],
        features,
    )
    sum_ffn = core_summed(send_ffn, keep_ffn)
    grad_two = grad_sum3 + matmul_right(grad_pre, w_ffn_in)
    grad_sum2, gain_two, shift_two = norm_backward(grad_two, normed_two, invert_two, norm_gains[1])
    branch_two = grad_sum2.astype(bf16)
    cross_up = matmul_right(branch_two, w_cross_out).astype(bf16)
    cross_up = after(cross_up, sum_ffn)
    sum_ffn = scatter_sum(sum_ffn, chip)
    dcq, dck, dcv, dck_far, dcv_far = attend_back(
        cross_query, 0, cross_up, cross_mix, cross_lse, ckv, 0, 4, ckv_far, 0, 4,
        segment, source_col, source_far_col,
    )
    w_ckey, w_cvalue = w_cross_kv[:, :features], w_cross_kv[:, features:]
    d_enc_low = (matmul_right(dck_far, w_ckey) + matmul_right(dcv_far, w_cvalue)).astype(bf16)
    d_enc_far = swapped(d_enc_low, SEQ_BIT)
    dcq = after(dcq, d_enc_low)
    send_mid, keep_mid = weight_halves(
        [
            (features, [(cross_mix, 0, branch_two, 0)]),
            (features, [(one_low, 0, dcq, 0)]),
            (features, [(source, 0, dck, 0), (source_far, 0, dck_far, 0)]),
            (features, [(source, 0, dcv, 0), (source_far, 0, dcv_far, 0)]),
            (pair_count, [(three_low, 0, pair_grad, 0)]),
            (pair_count, [(follow, 0, pair_grad, 0)]),
        ],
        features,
    )
    keep_mid, send_mid, sum_ffn = lax.optimization_barrier((keep_mid, send_mid, sum_ffn))
    sum_mid = core_summed(send_mid, keep_mid)
    grad_one = grad_sum2 + matmul_right(after(dcq, keep_mid), w_cross_q)
    grad_sum1, gain_one, shift_one = norm_backward(grad_one, normed_one, invert_one, norm_gains[0])
    branch_one = grad_sum1.astype(bf16)
    self_up = matmul_right(branch_one, w_self_out).astype(bf16)
    self_up = after(self_up, sum_mid)
    sum_mid = scatter_sum(after(sum_mid, self_up), chip)
    sum_ffn = scatter_sum(after(sum_ffn, self_up), far[:1])
    dq, dk, dv, dk_far, dv_far = attend_back(
        qkv, 0, self_up, self_mix, self_lse, qkv, 4, 8, kv_far, 0, 4, segment, segment_col, segment_far_col
    )
    dq, dk, dv, dk_far, dv_far, sum_mid, sum_ffn, d_enc_far = lax.optimization_barrier(
        (dq, dk, dv, dk_far, dv_far, sum_mid, sum_ffn, d_enc_far)
    )

    w_key, w_value = w_self_qkv[:, features : 2 * features], w_self_qkv[:, 2 * features :]
    d_hidden_low = (matmul_right(dk_far, w_key) + matmul_right(dv_far, w_value)).astype(bf16)
    dq = after(dq, d_hidden_low)
    send_qkv, keep_qkv = weight_halves(
        [
            (features, [(hidden, 0, dq, 0)]),
            (features, [(hidden, 0, dk, 0), (hidden_far, 0, dk_far, 0)]),
            (features, [(hidden, 0, dv, 0), (hidden_far, 0, dv_far, 0)]),
            (features, [(self_mix, 0, branch_one, 0)]),
            (
                LANES,
                [
                    (
                        [(d_b_ffn_in, at) for at in range(0, hidden_units, features)]
                        + [(row, 0) for row in (d_b_ffn_out, gain_one, gain_two, gain_three)]
                        + [(row, 0) for row in (shift_one, shift_two, shift_three, d_b_pair)]
                        + [(d_delete, 0)],
                        0,
                        None,
                        0,
                    )
                ],
            ),
        ],
        features,
        58,
    )
    d_hidden_far = swapped(d_hidden_low, SEQ_BIT)
    sum_ffn = doubled(sum_ffn, far[1:], keep_qkv)
    sum_qkv, d_hidden_far, d_vocab, sum_ffn = lax.optimization_barrier((core_summed(send_qkv, keep_qkv), d_hidden_far, d_vocab, sum_ffn))
    sum_qkv = scatter_sum(sum_qkv, chip)
    sum_mid = scatter_sum(after(sum_mid, sum_ffn), far[:1], sum_qkv)
    sum_ffn = gathered(sum_ffn, far[:1], sum_qkv)
    sum_mid = doubled(sum_mid, far[1:])
    sum_mid = gathered(sum_mid, far[:1])
    sum_qkv = doubled(sum_qkv, far)
    sum_rest = jnp.concatenate([sum_mid, sum_qkv], 1)
    sum_ffn = gathered(sum_ffn, chip, sum_rest)
    ffn_other = swapped(sum_ffn, CORE_BIT)
    out_ffn_in, out_ffn_out = joined(
        sum_ffn,
        ffn_other,
        [
            ([0], hidden_units, False),
            (list(range(hidden_units, 2 * hidden_units, features)), features, False),
        ],
    )
    rest_at = sum_mid.shape[1]
    sum_rest = gathered(after(sum_rest, sum_ffn), chip, out_ffn_in, out_ffn_out)
    d_hidden = (
        grad_sum1
        + matmul_right(dq, w_self_qkv[:, :features])
        + matmul_right(dk, w_key)
        + matmul_right(dv, w_value)
        + d_hidden_far.astype(f32)
    )
    d_enc = matmul_right(dck, w_ckey) + matmul_right(dcv, w_cvalue) + d_enc_far.astype(f32)

    rest_other = after(swapped(sum_rest, CORE_BIT), d_hidden, d_enc)
    pair_at = 4 * features
    out_cross_out, out_cross_q, out_cross_kv, out_pair, out_self_qkv, out_self_out, small = joined(
        sum_rest,
        rest_other,
        [
            ([0], features, False),
            ([features], features, False),
            ([2 * features], 2 * features, False),
            ([pair_at, pair_at + pair_count], pair_count, False),
            ([rest_at], 3 * features, False),
            ([rest_at + 3 * features], features, False),
            ([rest_at + 4 * features], LANES, True),
        ],
    )
    d_vocab = after(d_vocab, small).astype(f32)
    units = hidden_units // features
    out_b_ffn_in = small[:units].reshape(-1)
    out_b_ffn_out = small[units]
    out_gains = small[units + 1 : units + 4]
    out_shifts = small[units + 4 : units + 7]
    out_b_pair = small[units + 7, :pair_count]
    out_delete = jnp.transpose(small[units + 8 : units + 10])
    return (
        three_low[None],
        d_hidden[None],
        d_enc[None],
        out_self_qkv,
        out_self_out,
        out_cross_q,
        out_cross_kv,
        out_cross_out,
        out_ffn_in,
        out_b_ffn_in,
        out_ffn_out,
        out_b_ffn_out,
        out_gains,
        out_shifts,
        d_vocab,
        out_pair,
        out_b_pair,
        out_delete,
    )


def solution(mesh):
    split_mesh = Mesh(mesh.devices.reshape(-1, 2, 2, mesh.shape["seq"]), AXES)
    rows = ("far", "near", "core")
    split = P(rows, "seq", None)
    ids = P(rows, "seq")
    return jax.shard_map(
        per_device,
        mesh=split_mesh,
        in_specs=(split, split) + (ids,) * 7 + (P(),) * 15,
        out_specs=(split,) * 3 + (P(),) * 11 + (P(AXES, None),) + (P(),) * 3,
        check_vma=False,
    )
```

```python
import functools

import jax
import jax.numpy as jnp
from jax import lax
from jax.experimental import pallas as pl
from jax.experimental.pallas import tpu as pltpu
from jax.sharding import Mesh
from jax.sharding import PartitionSpec as P

HEADS = 8
HEAD_DIM = 64
LANES = 128
SCALE = HEAD_DIM**-0.5
EPSILON = 1e-05
NEGATIVE = -1e30
TILE = 256
STEP_PAIRS = 2

SEQ_BIT, CORE_BIT, NEAR_BIT = 1, 2, 4
GROUP = 8

bf16 = jnp.bfloat16
f32 = jnp.float32


def matmul(left, right):
    return jnp.dot(left, right, preferred_element_type=f32)


def matmul_left(left, right):
    return lax.dot_general(left, right, (((0,), (0,)), ((), ())), preferred_element_type=f32)


def matmul_right(left, right):
    return lax.dot_general(left, right, (((1,), (1,)), ((), ())), preferred_element_type=f32)


def smooth_gate(value):
    return jax.nn.gelu(value, approximate=True)


def norm_forward(summed, gain_row, shift_row):
    centered = summed - jnp.mean(summed, -1, keepdims=True)
    invert = lax.rsqrt(jnp.mean(centered * centered, -1, keepdims=True) + EPSILON)
    normed = centered * invert
    return (normed * gain_row + shift_row, normed, invert)


def norm_backward(upstream, normed, invert, gain_row):
    scaled = upstream * gain_row
    centered = (
        scaled
        - jnp.mean(scaled, -1, keepdims=True)
        - normed * jnp.mean(scaled * normed, -1, keepdims=True)
    )
    return (
        centered * invert,
        jnp.sum(upstream * normed, 0, keepdims=True),
        jnp.sum(upstream, 0, keepdims=True),
    )


def passed_along(value, axis, steps):
    count = lax.axis_size(axis)
    leading, last = (max(0, -steps), min(count, count - steps))
    return lax.ppermute(value, axis, [(source, source + steps) for source in range(leading, last)])


AXES = ("far", "near", "core", "seq")


def place():
    return lax.axis_index(AXES)


def place_count():
    return lax.axis_size("far") * GROUP


def swapped(value, mask):
    return lax.ppermute(value, AXES, [(i, i ^ mask) for i in range(place_count())])


def after(value, *others):
    return lax.optimization_barrier((value,) + others)[0]


def group_index(bits):
    me = place()
    return sum(((me & bit) != 0).astype(jnp.int32) << n for n, bit in enumerate(bits))


def group_mask(bits, relative):
    return sum(bit for n, bit in enumerate(bits) if (relative >> n) & 1)


def scatter_sum(value, bits, *late):
    count = 1 << len(bits)
    rows = value.shape[0] // count
    index = group_index(bits)
    part = lambda relative: lax.dynamic_slice_in_dim(value, (index ^ relative) * rows, rows)
    total = part(0).astype(f32)
    others = [swapped(part(r), group_mask(bits, r)) for r in range(1, count)]
    if late:
        others = [after(other, *late) for other in others]
    for other in others:
        total = total + other.astype(f32)
    return total.astype(bf16)


def gathered(value, bits, *late):
    count = 1 << len(bits)
    index = group_index(bits)
    parts = [value] + [swapped(value, group_mask(bits, r)) for r in range(1, count)]
    if late:
        parts = [after(part, *late) for part in parts]
    for n in range(len(bits)):
        odd = ((index >> n) & 1) == 1
        parts = [
            jnp.where(odd, jnp.concatenate([second, first], 0), jnp.concatenate([first, second], 0))
            for first, second in zip(parts[::2], parts[1::2])
        ]
    return parts[0]


def doubled(value, bits, *late):
    for bit in bits:
        other = swapped(value, bit)
        if late:
            other = after(other, *late)
        value = (value.astype(f32) + other.astype(f32)).astype(bf16)
    return value


def far_bits():
    count = place_count()
    return [1 << n for n in range(3, count.bit_length() - 1)]


def kernel_call(body, grid, in_specs, out_specs, out_shape, scratch, flops, vmem, prefetch=0):
    return pl.pallas_call(
        body,
        grid_spec=pltpu.PrefetchScalarGridSpec(
            num_scalar_prefetch=prefetch,
            grid=grid,
            in_specs=in_specs,
            out_specs=out_specs,
            scratch_shapes=scratch,
        ),
        out_shape=out_shape,
        compiler_params=pltpu.CompilerParams(vmem_limit_bytes=vmem << 20),
        cost_estimate=pl.CostEstimate(flops=flops, bytes_accessed=8 << 20, transcendentals=0),
    )


def dot_nt(left, right):
    return lax.dot_general(left, right, (((1,), (1,)), ((), ())), preferred_element_type=f32)


def dot_tn(left, right):
    return lax.dot_general(left, right, (((0,), (0,)), ((), ())), preferred_element_type=f32)


def head_lanes(shape, head):
    lane = lax.broadcasted_iota(jnp.int32, shape, 1)
    return (lane >= HEAD_DIM) == (head == 1)


def attend_body(q_ref, ko_ref, kr_ref, vo_ref, vr_ref, sq_ref, so_ref, sr_ref, out_ref, lse_ref, stat):
    step = pl.program_id(0)
    rows = q_ref.shape[0]
    heads = 2 * STEP_PAIRS

    @pl.when(step == 0)
    def _():
        stat[...] = jnp.zeros_like(stat)

    lane = lax.broadcasted_iota(jnp.int32, (rows, LANES), 1)
    same_own = sq_ref[...] == so_ref[...]
    same_far = sq_ref[...] == sr_ref[...]

    def scores(head):
        at = slice(head // 2 * LANES, (head // 2 + 1) * LANES)
        queries = q_ref[:, at].astype(f32) * SCALE
        queries = jnp.where(head_lanes((rows, LANES), head % 2), queries, 0.0).astype(bf16)
        return (
            jnp.where(same_own, dot_nt(queries, ko_ref[:, at]), NEGATIVE),
            jnp.where(same_far, dot_nt(queries, kr_ref[:, at]), NEGATIVE),
        )

    kept = stat[...]
    mixed = []
    ahead = scores(0)
    for head in range(heads):
        s_own, s_far = ahead
        if head + 1 < heads:
            ahead = scores(head + 1)
        top = jnp.maximum(jnp.max(s_own, 1, keepdims=True), jnp.max(s_far, 1, keepdims=True))
        e_own = jnp.exp(s_own - top)
        e_far = jnp.exp(s_far - top)
        total = jnp.sum(e_own, 1, keepdims=True) + jnp.sum(e_far, 1, keepdims=True)
        at = slice(head // 2 * LANES, (head // 2 + 1) * LANES)
        mix = matmul(e_own.astype(bf16), vo_ref[:, at]) + matmul(e_far.astype(bf16), vr_ref[:, at])
        mixed.append(mix / total)
        kept = jnp.where(lane == heads * step + head, top + jnp.log(total), kept)
    for pair in range(STEP_PAIRS):
        at = slice(pair * LANES, (pair + 1) * LANES)
        out_ref[:, at] = jnp.where(lane < HEAD_DIM, mixed[2 * pair], mixed[2 * pair + 1]).astype(bf16)
    stat[...] = kept

    @pl.when(step == pl.num_programs(0) - 1)
    def _():
        lse_ref[...] = jnp.transpose(stat[...])[:HEADS, :]


def attend(query, q_at, own, ko_at, vo_at, far, kr_at, vr_at, seg_q, seg_own, seg_far):
    rows, keys = query.shape[0], own.shape[0]
    pick = lambda n, at: pl.BlockSpec(
        (n, STEP_PAIRS * LANES), lambda h, at=at: (0, at // STEP_PAIRS + h)
    )
    whole = lambda *shape: pl.BlockSpec(shape, lambda h: (0, 0))
    return kernel_call(
        attend_body,
        (HEADS // 2 // STEP_PAIRS,),
        [
            pick(rows, q_at),
            pick(keys, ko_at),
            pick(keys, kr_at),
            pick(keys, vo_at),
            pick(keys, vr_at),
            whole(rows, 1),
            whole(1, keys),
            whole(1, keys),
        ],
        [pick(rows, 0), whole(HEADS, rows)],
        [
            jax.ShapeDtypeStruct((rows, HEADS * HEAD_DIM), bf16),
            jax.ShapeDtypeStruct((HEADS, rows), f32),
        ],
        [pltpu.VMEM((rows, LANES), f32)],
        16 * rows * keys * 512,
        40,
    )(query, own, far, own, far, seg_q.reshape(rows, 1), seg_own.reshape(1, keys), seg_far.reshape(1, keys))


def attend_back_body(
    q_ref, g_ref, o_ref, lse_ref, ko_ref, kr_ref, vo_ref, vr_ref, sq_ref, so_ref, sr_ref,
    dq_ref, dko_ref, dvo_ref, dkr_ref, dvr_ref,
):
    rows = q_ref.shape[0]
    which = lax.broadcasted_iota(jnp.int32, (8, LANES), 0)
    lane = lax.broadcasted_iota(jnp.int32, (8, LANES), 1)
    chooser = jnp.where((lane >= HEAD_DIM) == (which == 1), 1.0, 0.0).astype(f32)
    along, q_of, g_of = [], [], []
    for pair in range(STEP_PAIRS):
        at = slice(pair * LANES, (pair + 1) * LANES)
        queries = q_ref[:, at].astype(f32) * SCALE
        upstream = g_ref[:, at].astype(f32)
        rows_along = lax.dot_general(
            chooser,
            upstream * o_ref[:, at].astype(f32),
            (((1,), (1,)), ((), ())),
            precision=lax.Precision.HIGHEST,
            preferred_element_type=f32,
        )
        for head in range(2):
            mine = head_lanes((rows, LANES), head)
            along.append(rows_along[head : head + 1, :])
            q_of.append(jnp.where(mine, queries, 0.0).astype(bf16))
            g_of.append(jnp.where(mine, upstream, 0.0).astype(bf16))
    halves = (
        (ko_ref, vo_ref, so_ref, dko_ref, dvo_ref),
        (kr_ref, vr_ref, sr_ref, dkr_ref, dvr_ref),
    )
    units = [
        (pair, head, half) for pair in range(STEP_PAIRS) for half in range(2) for head in range(2)
    ]

    def products(unit):
        pair, head, half = unit
        at = slice(pair * LANES, (pair + 1) * LANES)
        k_ref, v_ref = halves[half][:2]
        return dot_nt(k_ref[:, at], q_of[2 * pair + head]), dot_nt(v_ref[:, at], g_of[2 * pair + head])

    dq_of = [None] * (2 * STEP_PAIRS)
    ahead = products(units[0])
    for n, unit in enumerate(units):
        pair, head, half = unit
        index = 2 * pair + head
        at = slice(pair * LANES, (pair + 1) * LANES)
        k_ref, _, s_ref, dk_ref, dv_ref = halves[half]
        scores, back = ahead
        if n + 1 < len(units):
            ahead = products(units[n + 1])
        same = s_ref[...] == sq_ref[...]
        weights = jnp.exp(jnp.where(same, scores, NEGATIVE) - lse_ref[pair, head : head + 1, :])
        grad = (weights * (back - along[index])).astype(bf16)
        dv = matmul(weights.astype(bf16), g_of[index])
        dk = matmul(grad, q_of[index])
        if head == 0:
            key_t = jnp.transpose(k_ref[:, at].astype(f32)).astype(bf16)
            first = (dk, dv)
        else:
            dk_ref[:, at] = (first[0] + dk).astype(bf16)
            dv_ref[:, at] = (first[1] + dv).astype(bf16)
        dq = matmul(key_t[head * HEAD_DIM : (head + 1) * HEAD_DIM, :], grad)
        dq_of[index] = dq if dq_of[index] is None else dq_of[index] + dq
    for pair in range(STEP_PAIRS):
        at = slice(pair * LANES, (pair + 1) * LANES)
        dq = jnp.concatenate(dq_of[2 * pair : 2 * pair + 2], 0)
        dq_ref[:, at] = (jnp.transpose(dq) * SCALE).astype(bf16)


def attend_back(query, q_at, upstream, mixed, lse, own, ko_at, vo_at, far, kr_at, vr_at, seg_q, seg_own, seg_far):
    rows, keys = query.shape[0], own.shape[0]
    pick = lambda n, at: pl.BlockSpec(
        (n, STEP_PAIRS * LANES), lambda h, at=at: (0, at // STEP_PAIRS + h)
    )
    whole = lambda *shape: pl.BlockSpec(shape, lambda h: (0, 0))
    width = HEADS * HEAD_DIM
    return kernel_call(
        attend_back_body,
        (HEADS // 2 // STEP_PAIRS,),
        [
            pick(rows, q_at),
            pick(rows, 0),
            pick(rows, 0),
            pl.BlockSpec((STEP_PAIRS, 2, rows), lambda h: (h, 0, 0)),
            pick(keys, ko_at),
            pick(keys, kr_at),
            pick(keys, vo_at),
            pick(keys, vr_at),
            whole(1, rows),
            whole(keys, 1),
            whole(keys, 1),
        ],
        [pick(rows, 0)] + [pick(keys, 0)] * 4,
        [jax.ShapeDtypeStruct((rows, width), bf16)] + [jax.ShapeDtypeStruct((keys, width), bf16)] * 4,
        [],
        40 * rows * keys * 512,
        40,
    )(
        query, upstream, mixed, lse.reshape(HEADS // 2, 2, rows), own, far, own, far,
        seg_q.reshape(1, rows), seg_own.reshape(keys, 1), seg_far.reshape(keys, 1),
    )


def columns_of(row):
    return jnp.transpose(jnp.broadcast_to(row, (LANES, row.shape[1])))


def vocab_body(info, *refs):
    blocks, (t_ref, w_ref, e_ref, stat_ref, hidden_ref, kept, targets) = refs[:GROUP], refs[GROUP:]
    step = pl.program_id(0)
    chunk = 128

    @pl.when(step == 0)
    def _():
        for start in range(0, kept.shape[0], TILE):

            @pl.when(start < info[16])
            def _(start=start):
                kept[start : start + TILE, :] = jnp.zeros((TILE, kept.shape[1]), kept.dtype)
                targets[start : start + TILE, :] = jnp.zeros((TILE, LANES), f32)

        for rel in range(GROUP):
            core, near = rel // 4, rel % 4
            block = (core | (near << 1)) ^ info[17]
            count, offset = info[block], info[8 + block]
            src = blocks[rel]
            for start in range(0, src.shape[0], chunk):

                @pl.when(start < count)
                def _(src=src, rel=rel, start=start, offset=offset):
                    for piece in range(start, start + chunk, 16):

                        @pl.when(piece < count)
                        def _(piece=piece):
                            to = pl.ds(pl.multiple_of(offset + piece, 16), 16)
                            kept[to, :] = src[piece : piece + 16, :]

                    value = columns_of(t_ref[rel : rel + 1, start : start + chunk])
                    for piece in range(start, start + chunk, 16):

                        @pl.when(piece < count)
                        def _(piece=piece):
                            to = pl.ds(pl.multiple_of(offset + piece, 16), 16)
                            targets[to, :] = value[piece - start : piece - start + 16, :]

    @pl.when(step * TILE < info[16])
    def _():
        rows = pl.ds(pl.multiple_of(step * TILE, TILE), TILE)
        hidden = kept[rows, :]
        hidden_ref[...] = hidden
        outer, _, piece, _ = w_ref.shape
        tops, totals = [], []
        ahead = dot_nt(w_ref[0, 0], hidden)
        for n in range(outer):
            value = ahead
            if n + 1 < outer:
                ahead = dot_nt(w_ref[n + 1, 0], hidden)
            top = jnp.max(value, 0, keepdims=True)
            value = jnp.exp(value - top)
            tops.append(top)
            totals.append(jnp.sum(value, 0, keepdims=True))
            e_ref[0, n * piece : (n + 1) * piece, :] = value.astype(bf16)
        top = functools.reduce(jnp.maximum, tops)
        shares = [jnp.exp(part - top) for part in tops]
        total = sum(part * share for part, share in zip(totals, shares))
        target = jnp.transpose(targets[rows, :])[:1, :]
        lines = [top, total, target] + shares
        lines.append(jnp.zeros((stat_ref.shape[0] - len(lines), TILE), f32))
        stat_ref[...] = jnp.concatenate(lines, 0)


def stat_lines(outer):
    return -(-(3 + outer + 1) // 8) * 8


def last_active(i, info):
    return jnp.minimum(i, jnp.maximum((info[16] + TILE - 1) // TILE - 1, 0))


def vocab_slice(w):
    outer, _, block, width = w.shape
    return pl.BlockSpec(
        (outer, 1, block, width), lambda i, info: (0, info[18], 0, 0), pipeline_mode=pl.Buffered(1)
    )


def vocab_forward(info, blocks, targets, w):
    rows, width = blocks[0].shape
    total = GROUP * rows
    wide = w.shape[0] * w.shape[2]
    once = lambda *shape: pl.BlockSpec(
        shape, lambda i, info: (0,) * len(shape), pipeline_mode=pl.Buffered(1)
    )
    return kernel_call(
        vocab_body,
        (total // TILE,),
        [once(rows, width)] * GROUP + [once(GROUP, rows), vocab_slice(w)],
        [
            pl.BlockSpec((1, wide, TILE), lambda i, info: (last_active(i, info), 0, 0)),
            pl.BlockSpec((stat_lines(w.shape[0]), TILE), lambda i, info: (0, last_active(i, info))),
            pl.BlockSpec((TILE, width), lambda i, info: (last_active(i, info), 0)),
        ],
        [
            jax.ShapeDtypeStruct((total // TILE, wide, TILE), bf16),
            jax.ShapeDtypeStruct((stat_lines(w.shape[0]), total), f32),
            jax.ShapeDtypeStruct((total, width), bf16),
        ],
        [
            pltpu.VMEM((total, width), bf16),
            pltpu.VMEM((total, LANES), f32),
        ],
        1400 * wide * width * 2,
        34,
        prefetch=1,
    )(info, *blocks, targets, w)


def vocab_back_body(info, e_ref, s_ref, w_ref, out_ref):
    @pl.when(pl.program_id(0) * out_ref.shape[0] < info[16])
    def _():
        outer, _, piece, width = w_ref.shape
        back = None
        for n in range(outer):
            at = slice(n * piece, (n + 1) * piece)
            weights = jnp.concatenate([e_ref[t, at, :] for t in range(e_ref.shape[0])], 1)
            share = columns_of(s_ref[3 + n : 4 + n, :])
            share = jnp.concatenate([share] * (width // LANES), 1)
            value = dot_tn(weights, w_ref[n, 0]) * share
            back = value if back is None else back + value
        out_ref[...] = back.astype(bf16)


def vocab_back(info, e, stats, w):
    tiles, wide, _ = e.shape
    width = w.shape[3]
    both = 2 * TILE
    at = lambda i, info: jnp.minimum(i, jnp.maximum((info[16] + both - 1) // both - 1, 0))
    return kernel_call(
        vocab_back_body,
        (tiles // 2,),
        [
            pl.BlockSpec((2, wide, TILE), lambda i, info: (at(i, info), 0, 0)),
            pl.BlockSpec((stats.shape[0], both), lambda i, info: (0, at(i, info))),
            vocab_slice(w),
        ],
        pl.BlockSpec((both, width), lambda i, info: (at(i, info), 0)),
        jax.ShapeDtypeStruct((tiles * TILE, width), bf16),
        [],
        1400 * wide * width * 2,
        26,
        prefetch=1,
    )(info, e, stats, w)


def spread_body(info, g_ref, f_ref, *refs):
    outs, columns = refs[:-1], refs[-1]
    step = pl.program_id(0)
    total, width = g_ref.shape
    rows = outs[0].shape[0]

    @pl.when(step == 0)
    def _():
        for start in range(0, total, TILE):
            columns[start : start + TILE, :] = columns_of(f_ref[:, start : start + TILE])

    def block_of(core, near):
        block = (core | (near << 1)) ^ info[17]
        at = pl.ds(pl.multiple_of(info[8 + block], 16), rows)
        row = lax.broadcasted_iota(jnp.int32, (rows, LANES), 0)
        factor = jnp.where(row < info[block], columns[at, :], 0.0)
        live = row < info[block]
        pieces = [
            jnp.where(live, g_ref[at, start : start + LANES].astype(f32) * factor, 0.0)
            for start in range(0, width, LANES)
        ]
        return jnp.concatenate(pieces, 1).astype(bf16)

    for n, out_ref in enumerate(outs):

        @pl.when(step == n)
        def _(n=n, out_ref=out_ref):
            out_ref[...] = block_of(1 - n // 4, n % 4)


def spread(info, g, factor, rows):
    total, width = g.shape
    once = lambda *shape: pl.BlockSpec(
        shape, lambda i, info: (0,) * len(shape), pipeline_mode=pl.Buffered(1)
    )
    return kernel_call(
        spread_body,
        (GROUP,),
        [once(total, width), once(1, total)],
        [once(rows, width)] * GROUP,
        [jax.ShapeDtypeStruct((rows, width), bf16)] * GROUP,
        [pltpu.VMEM((total, LANES), f32)],
        total * width,
        24,
        prefetch=1,
    )(info, g, factor)


def vocab_grad_body(piece, info, e_ref, h_ref, s_ref, f_ref, out_ref, total):
    step = pl.program_id(0)

    @pl.when(step == 0)
    def _():
        total[...] = jnp.zeros_like(total)

    @pl.when(step * TILE < info[16])
    def _():
        wide = e_ref.shape[1]
        factor = f_ref[...]
        target = s_ref[2:3, :].astype(jnp.int32)
        row = 1 + lax.broadcasted_iota(jnp.int32, (piece, TILE), 0)
        for start in range(0, wide, piece):
            at = slice(start, start + piece)
            share = 3 + start // piece
            weights = e_ref[0, at, :].astype(f32) * (factor * s_ref[share : share + 1, :])
            weights = (weights - jnp.where(row == target - start, 1.0, 0.0)).astype(bf16)
            total[at, :] += matmul(weights, h_ref[...])

    @pl.when(step == pl.num_programs(0) - 1)
    def _():
        out_ref[...] = total[...].astype(bf16)


def vocab_grad(info, e, hidden, stats, factor, piece):
    tiles, wide, _ = e.shape
    width = hidden.shape[1]
    tile = lambda n: pl.BlockSpec((TILE, n), lambda i, info: (last_active(i, info), 0))
    return kernel_call(
        functools.partial(vocab_grad_body, piece),
        (tiles,),
        [
            pl.BlockSpec((1, wide, TILE), lambda i, info: (last_active(i, info), 0, 0)),
            tile(width),
            pl.BlockSpec((stats.shape[0], TILE), lambda i, info: (0, last_active(i, info))),
            pl.BlockSpec((1, TILE), lambda i, info: (0, last_active(i, info))),
        ],
        pl.BlockSpec((wide, width), lambda i, info: (0, 0)),
        jax.ShapeDtypeStruct((wide, width), bf16),
        [pltpu.VMEM((wide, width), f32)],
        1400 * wide * width * 2,
        40,
        prefetch=1,
    )(info, e, hidden, stats, factor)


def halves_body(plan, info, *refs):
    operands, outs = refs[:-2], refs[-2:]
    rows = outs[0].shape[0]

    def fill(half, out_ref):
        at = 0
        for terms, width in plan:
            total = None
            for left, left_at, right, right_at in terms:
                if right is None:
                    lines = [operands[n][:, start : start + 2 * rows] for n, start in left]
                    blank = width - sum(line.shape[0] for line in lines)
                    lines.append(jnp.zeros((blank, 2 * rows), f32))
                    turned = jnp.transpose(jnp.concatenate(lines, 0))
                    value = jnp.where(half == 0, turned[:rows], turned[rows:])
                else:
                    lanes = pl.ds(pl.multiple_of(left_at + half * rows, rows), rows)
                    value = dot_tn(
                        operands[left][:, lanes], operands[right][:, right_at : right_at + width]
                    )
                total = value if total is None else total + value
            out_ref[:, at : at + width] = total.astype(bf16)
            at += width

    @pl.when(pl.program_id(0) == 0)
    def _():
        fill(1 - info[0], outs[0])

    @pl.when(pl.program_id(0) == 1)
    def _():
        fill(info[0], outs[1])


def weight_halves(columns, rows, vmem=36):
    operands, plan = [], []

    def index_of(array):
        for n, known in enumerate(operands):
            if known is array:
                return n
        operands.append(array)
        return len(operands) - 1

    for width, terms in columns:
        taken = []
        for left, left_at, right, right_at in terms:
            if right is None:
                taken.append(([(index_of(row), start) for row, start in left], 0, None, 0))
            else:
                taken.append((index_of(left), left_at, index_of(right), right_at))
        plan.append((taken, width))
    total = sum(width for width, _ in columns)
    whole = lambda shape: pl.BlockSpec(shape, lambda i, info: (0, 0), pipeline_mode=pl.Buffered(1))
    return kernel_call(
        functools.partial(halves_body, plan),
        (2,),
        [whole(o.shape) for o in operands],
        [whole((rows // 2, total))] * 2,
        [jax.ShapeDtypeStruct((rows // 2, total), bf16)] * 2,
        [],
        rows * total * 1024,
        vmem,
        prefetch=1,
    )(group_index([CORE_BIT])[None], *operands)


def core_summed(send, keep):
    return (keep.astype(f32) + swapped(send, CORE_BIT).astype(f32)).astype(bf16)


def joined_body(plan, info, own_ref, other_ref, *outs):
    rows = own_ref.shape[0]
    mine, far = pl.multiple_of(info[0] * rows, rows), pl.multiple_of((1 - info[0]) * rows, rows)
    for (starts, width, turned), out_ref in zip(plan, outs):
        for n, start in enumerate(starts):
            for ref, at in ((own_ref, mine), (other_ref, far)):
                value = ref[:, start : start + width].astype(f32)
                if turned:
                    out_ref[:, pl.ds(at, rows)] = jnp.transpose(value)
                else:
                    out_ref[pl.ds(n * 2 * rows + at, rows), :] = value


def joined(own, other, plan):
    rows = own.shape[0]
    shapes = [
        (width, 2 * rows) if turned else (2 * rows * len(starts), width)
        for starts, width, turned in plan
    ]
    once = lambda shape: pl.BlockSpec(shape, lambda i, info: (0, 0), pipeline_mode=pl.Buffered(1))
    return kernel_call(
        functools.partial(joined_body, plan),
        (1,),
        [once(own.shape)] * 2,
        [once(shape) for shape in shapes],
        [jax.ShapeDtypeStruct(shape, f32) for shape in shapes],
        [],
        own.size,
        36,
        prefetch=1,
    )(group_index([CORE_BIT])[None], own, other)


def as_columns_body(rows_ref, *outs):
    for n, out_ref in enumerate(outs):
        out_ref[...] = columns_of(rows_ref[n : n + 1, :])[:, :1].astype(jnp.int32)


def as_columns(*rows):
    count = rows[0].shape[0]
    whole = lambda *shape: pl.BlockSpec(shape, lambda i, info: (0, 0))
    return kernel_call(
        as_columns_body_with_info,
        (1,),
        [whole(len(rows), count)],
        [whole(count, 1)] * len(rows),
        [jax.ShapeDtypeStruct((count, 1), jnp.int32)] * len(rows),
        [],
        count,
        16,
        prefetch=1,
    )(jnp.zeros((1,), jnp.int32), jnp.stack(rows).astype(f32))


def as_columns_body_with_info(info, *refs):
    as_columns_body(*refs)


def added_body(info, *refs):
    count = len(refs) // 3
    for n in range(count):
        total = refs[n][...].astype(f32) + refs[count + n][...].astype(f32)
        refs[2 * count + n][...] = total.astype(bf16)


def added(firsts, seconds):
    rows, width = firsts[0].shape
    piece = pl.BlockSpec((rows // 4, width), lambda i, info: (i, 0))
    return kernel_call(
        added_body,
        (4,),
        [piece] * (2 * len(firsts)),
        [piece] * len(firsts),
        [jax.ShapeDtypeStruct((rows, width), bf16)] * len(firsts),
        [],
        rows * width,
        24,
        prefetch=1,
    )(jnp.zeros((1,), jnp.int32), *firsts, *seconds)


def per_device(
    hidden_in,
    enc_states,
    segment_ids,
    edit_pass,
    enc_segments,
    target_tokens,
    placeholder_counts,
    delete_labels,
    loss_mask,
    w_self_qkv,
    w_self_out,
    w_cross_q,
    w_cross_kv,
    w_cross_out,
    w_ffn_in,
    b_ffn_in,
    w_ffn_out,
    b_ffn_out,
    norm_gains,
    norm_shifts,
    w_vocab,
    w_pair,
    b_pair,
    w_delete,
):
    _, tokens, features = hidden_in.shape
    seq = lax.axis_index("seq")
    chip = [NEAR_BIT, SEQ_BIT]
    far = far_bits()
    hidden = hidden_in[0]
    source = enc_states[0]
    hidden_far = swapped(hidden, SEQ_BIT)
    qkv = matmul(hidden, w_self_qkv).astype(bf16)
    segment, passes, source_seg = segment_ids[0], edit_pass[0], enc_segments[0]

    keep_float = loss_mask[0].astype(f32)
    token_keep = keep_float * (passes == 2).astype(f32)
    row = lax.broadcasted_iota(jnp.int32, (tokens, tokens), 0)
    col = lax.broadcasted_iota(jnp.int32, (tokens, tokens), 1)
    rank = matmul(token_keep.astype(bf16)[None, :], (row <= col).astype(bf16)) - 1.0
    selects = (rank.astype(jnp.int32) == row) & (token_keep[None, :] > 0)
    chooser = selects.astype(bf16)
    targets = target_tokens[0]
    chosen = jnp.sum(jnp.where(selects, targets[None, :] + 1, 0), 1)
    ids_far = swapped(jnp.stack([segment, source_seg, chosen]), SEQ_BIT)
    segment_far, source_seg_far = ids_far[0], ids_far[1]

    vocab = w_vocab.shape[0]
    outer = lax.axis_size("far")
    block = vocab // (outer * GROUP)
    inner = lax.axis_index(("near", "core", "seq"))
    here = group_index([CORE_BIT, NEAR_BIT, SEQ_BIT])
    ckv = matmul(source, w_cross_kv).astype(bf16)
    hidden_far = after(hidden_far, ckv, qkv, chosen)
    kv_far = matmul(hidden_far, w_self_qkv[:, features:]).astype(bf16)
    source_far = swapped(after(source, hidden_far), SEQ_BIT)
    self_mix, self_lse = attend(qkv, 0, qkv, 4, 8, kv_far, 0, 4, segment, segment, segment_far)
    chosen_row = jnp.stack([chosen, ids_far[2]])
    chosen_near = swapped(chosen_row, NEAR_BIT)
    self_mix, self_lse, source_far, chosen_near = lax.optimization_barrier(
        (self_mix, self_lse, source_far, chosen_near)
    )
    layer_one, normed_one, invert_one = norm_forward(
        hidden.astype(f32) + matmul(self_mix, w_self_out), norm_gains[0], norm_shifts[0]
    )

    chosen_chip = jnp.stack([chosen_row[0], chosen_near[0], chosen_row[1], chosen_near[1]])
    chosen_core = swapped(chosen_chip, CORE_BIT)
    one_low = layer_one.astype(bf16)
    cross_query = matmul(one_low, w_cross_q).astype(bf16)
    ckv_far = matmul(source_far, w_cross_kv).astype(bf16)
    cross_mix, cross_lse = attend(
        cross_query, 0, ckv, 0, 4, ckv_far, 0, 4, segment, source_seg, source_seg_far
    )
    cross_mix, cross_lse, chosen_core = lax.optimization_barrier((cross_mix, cross_lse, chosen_core))
    chosen_all = jnp.concatenate([chosen_chip, chosen_core])
    index = chosen_all - 1
    local = (index // (block * GROUP)) * block + index % block + 1
    mine = (chosen_all > 0) & ((index // block) % GROUP == inner)
    local_targets = jnp.where(mine, local, 0).astype(f32)
    counts_rel = jnp.sum((chosen_all > 0).astype(jnp.int32), 1)
    relative = jnp.array([c | (n << 1) for c in range(2) for n in range(4)], jnp.int32) ^ here
    counts = jnp.sum(
        jnp.where(relative[:, None] == jnp.arange(GROUP)[None, :], counts_rel[:, None], 0), 0
    )
    rounded = (counts + 15) // 16 * 16
    before = jnp.arange(GROUP)[:, None] < jnp.arange(GROUP)[None, :]
    offsets = jnp.sum(jnp.where(before, rounded[:, None], 0), 0)
    info = jnp.concatenate([counts, offsets, jnp.sum(rounded)[None], here[None], inner[None]]).astype(jnp.int32)

    layer_two, normed_two, invert_two = norm_forward(
        layer_one + matmul(cross_mix, w_cross_out), norm_gains[1], norm_shifts[1]
    )
    two_low = layer_two.astype(bf16)
    pre_act = matmul(two_low, w_ffn_in) + b_ffn_in
    activ, gate_back = jax.vjp(smooth_gate, pre_act)
    activ_low = activ.astype(bf16)
    layer_three, normed_three, invert_three = norm_forward(
        layer_two + (matmul(activ_low, w_ffn_out) + b_ffn_out), norm_gains[2], norm_shifts[2]
    )
    three_low = layer_three.astype(bf16)

    kept = matmul(chooser, three_low).astype(bf16)
    kept_core = swapped(kept, CORE_BIT)
    kept_chip = [swapped(kept, NEAR_BIT), swapped(kept, SEQ_BIT), swapped(kept, NEAR_BIT | SEQ_BIT)]
    next_row = passed_along(three_low[:1], "seq", -1)
    w_parts = w_vocab.reshape(outer, GROUP, block, features)
    target_rows = jnp.take(w_vocab, after(targets, kept), axis=0).astype(f32)
    kept_chip = [after(k, target_rows) for k in kept_chip]
    kept_other = [swapped(k, CORE_BIT) for k in kept_chip]

    delete_keep = keep_float * (passes == 0).astype(f32)

    def label_grad(logits, labels, keep_mask):
        shifted = logits - jnp.max(logits, -1, keepdims=True)
        exponent = jnp.exp(shifted)
        weights = exponent / jnp.sum(exponent, -1, keepdims=True)
        onehot = labels[:, None] == lax.broadcasted_iota(jnp.int32, logits.shape, 1)
        return ((weights - onehot.astype(f32)) * keep_mask[:, None]).astype(bf16)

    delete_grad = label_grad(matmul(three_low, w_delete), delete_labels[0], delete_keep)

    delete_back = matmul_right(delete_grad, w_delete) - target_rows * token_keep[:, None]
    d_delete = matmul_left(delete_grad, three_low)
    segment_col, segment_far_col, source_col, source_far_col = as_columns(
        segment, segment_far, source_seg, source_seg_far
    )
    info, segment_col, segment_far_col, source_col, source_far_col = lax.optimization_barrier(
        (info, segment_col, segment_far_col, source_col, source_far_col)
    )
    info = after(info, delete_back, d_delete)
    e, stat_rows, kept_all = vocab_forward(
        info, [kept] + kept_chip + [kept_core] + kept_other, local_targets, w_parts
    )
    stats = stat_rows[:2]

    def merged(first, *others):
        most = functools.reduce(jnp.maximum, [o[0] for o in others], first[0])
        added = sum((o[1] * jnp.exp(o[0] - most) for o in others), first[1] * jnp.exp(first[0] - most))
        return jnp.stack([most, added])

    stats_pair = merged(stats, swapped(stats, CORE_BIT))
    stats_all = merged(stats_pair, *[swapped(stats_pair, group_mask(chip, r)) for r in (1, 2, 3)])
    factor = jnp.exp(stats[0] - stats_all[0] - jnp.log(stats_all[1]))[None, :]
    back_raw = vocab_back(info, e, stat_rows, w_parts)
    back = spread(info, back_raw, factor, tokens)
    back_core = [swapped(b, CORE_BIT) for b in back[:4]]
    back_near = back[4:]
    back_low = added(back_near[1:], back_core[1:])
    position = seq * tokens + jnp.arange(tokens, dtype=jnp.int32)
    row_length = tokens * lax.axis_size("seq")
    follow = jnp.concatenate([three_low[1:], after(next_row, *back_low)], 0)
    follow_seg = jnp.concatenate([segment[1:], segment_far[:1]], 0)
    pair_ok = (follow_seg == segment) & (position < row_length - 1)
    pair_keep = keep_float * (passes == 1).astype(f32) * pair_ok.astype(f32)
    pair_logits = matmul(three_low, w_pair[:features]) + matmul(follow, w_pair[features:]) + b_pair
    pair_grad = label_grad(pair_logits, placeholder_counts[0], pair_keep)
    follow_grad = matmul_right(pair_grad, w_pair[features:])
    back_row = passed_along(follow_grad[-1:], "seq", 1)
    d_b_pair = jnp.sum(pair_grad.astype(f32), 0, keepdims=True)
    d_b_pair = jnp.pad(d_b_pair, ((0, 0), (0, features - d_b_pair.shape[1])))
    head_back = [swapped(back_low[r - 1], group_mask(chip, r)).astype(f32) for r in (1, 2, 3)]
    head_back = sum(head_back, back_near[0].astype(f32) + back_core[0].astype(f32))
    vocab_part = vocab_grad(
        info, e, kept_all, stat_rows, after(factor, *back_low), block
    )
    d_vocab = lax.psum_scatter(vocab_part, "far", scatter_dimension=0, tiled=True)
    grad_local = (
        delete_back
        + matmul_right(pair_grad, w_pair[:features])
        + jnp.concatenate([back_row, follow_grad[:-1]], 0)
    )
    grad_local = after(grad_local, vocab_part)

    grad_three = grad_local + matmul_left(chooser, head_back.astype(bf16))
    grad_sum3, gain_three, shift_three = norm_backward(
        grad_three, normed_three, invert_three, norm_gains[2]
    )
    branch_three = grad_sum3.astype(bf16)
    row_sum = lambda value: jnp.sum(value.astype(f32), 0, keepdims=True)
    d_b_ffn_out = row_sum(branch_three)
    grad_pre = gate_back(matmul_right(branch_three, w_ffn_out))[0].astype(bf16)
    d_b_ffn_in = row_sum(grad_pre)
    hidden_units = w_ffn_in.shape[1]
    pair_count = w_pair.shape[1]
    send_ffn, keep_ffn = weight_halves(
        [(hidden_units, [(two_low, 0, grad_pre, 0)])]
        + [(features, [(activ_low, at, branch_three, 0)]) for at in range(0, hidden_units, features)],
        features,
    )
    sum_ffn = core_summed(send_ffn, keep_ffn)
    grad_two = grad_sum3 + matmul_right(grad_pre, w_ffn_in)
    grad_sum2, gain_two, shift_two = norm_backward(grad_two, normed_two, invert_two, norm_gains[1])
    branch_two = grad_sum2.astype(bf16)
    cross_up = matmul_right(branch_two, w_cross_out).astype(bf16)
    cross_up = after(cross_up, sum_ffn)
    sum_ffn = scatter_sum(sum_ffn, chip)
    dcq, dck, dcv, dck_far, dcv_far = attend_back(
        cross_query, 0, cross_up, cross_mix, cross_lse, ckv, 0, 4, ckv_far, 0, 4,
        segment, source_col, source_far_col,
    )
    w_ckey, w_cvalue = w_cross_kv[:, :features], w_cross_kv[:, features:]
    d_enc_low = (matmul_right(dck_far, w_ckey) + matmul_right(dcv_far, w_cvalue)).astype(bf16)
    d_enc_far = swapped(d_enc_low, SEQ_BIT)
    dcq = after(dcq, d_enc_low)
    send_mid, keep_mid = weight_halves(
        [
            (features, [(cross_mix, 0, branch_two, 0)]),
            (features, [(one_low, 0, dcq, 0)]),
            (features, [(source, 0, dck, 0), (source_far, 0, dck_far, 0)]),
            (features, [(source, 0, dcv, 0), (source_far, 0, dcv_far, 0)]),
            (pair_count, [(three_low, 0, pair_grad, 0)]),
            (pair_count, [(follow, 0, pair_grad, 0)]),
        ],
        features,
    )
    keep_mid, send_mid, sum_ffn = lax.optimization_barrier((keep_mid, send_mid, sum_ffn))
    sum_mid = core_summed(send_mid, keep_mid)
    grad_one = grad_sum2 + matmul_right(after(dcq, keep_mid), w_cross_q)
    grad_sum1, gain_one, shift_one = norm_backward(grad_one, normed_one, invert_one, norm_gains[0])
    branch_one = grad_sum1.astype(bf16)
    self_up = matmul_right(branch_one, w_self_out).astype(bf16)
    self_up = after(self_up, sum_mid)
    sum_mid = scatter_sum(after(sum_mid, self_up), chip)
    sum_ffn = scatter_sum(after(sum_ffn, self_up), far[:1])
    dq, dk, dv, dk_far, dv_far = attend_back(
        qkv, 0, self_up, self_mix, self_lse, qkv, 4, 8, kv_far, 0, 4, segment, segment_col, segment_far_col
    )
    dq, dk, dv, dk_far, dv_far, sum_mid, sum_ffn, d_enc_far = lax.optimization_barrier(
        (dq, dk, dv, dk_far, dv_far, sum_mid, sum_ffn, d_enc_far)
    )

    w_key, w_value = w_self_qkv[:, features : 2 * features], w_self_qkv[:, 2 * features :]
    d_hidden_low = (matmul_right(dk_far, w_key) + matmul_right(dv_far, w_value)).astype(bf16)
    dq = after(dq, d_hidden_low)
    send_qkv, keep_qkv = weight_halves(
        [
            (features, [(hidden, 0, dq, 0)]),
            (features, [(hidden, 0, dk, 0), (hidden_far, 0, dk_far, 0)]),
            (features, [(hidden, 0, dv, 0), (hidden_far, 0, dv_far, 0)]),
            (features, [(self_mix, 0, branch_one, 0)]),
            (
                LANES,
                [
                    (
                        [(d_b_ffn_in, at) for at in range(0, hidden_units, features)]
                        + [(row, 0) for row in (d_b_ffn_out, gain_one, gain_two, gain_three)]
                        + [(row, 0) for row in (shift_one, shift_two, shift_three, d_b_pair)]
                        + [(d_delete, 0)],
                        0,
                        None,
                        0,
                    )
                ],
            ),
        ],
        features,
        58,
    )
    d_hidden_far = swapped(d_hidden_low, SEQ_BIT)
    sum_ffn = doubled(sum_ffn, far[1:], keep_qkv)
    sum_qkv, d_hidden_far, d_vocab, sum_ffn = lax.optimization_barrier((core_summed(send_qkv, keep_qkv), d_hidden_far, d_vocab, sum_ffn))
    sum_qkv = scatter_sum(sum_qkv, chip)
    sum_mid = scatter_sum(after(sum_mid, sum_ffn), far[:1], sum_qkv)
    sum_ffn = gathered(sum_ffn, far[:1], sum_qkv)
    sum_mid = doubled(sum_mid, far[1:])
    sum_mid = gathered(sum_mid, far[:1])
    sum_qkv = doubled(sum_qkv, far)
    sum_rest = jnp.concatenate([sum_mid, sum_qkv], 1)
    sum_ffn = gathered(sum_ffn, chip, sum_rest)
    ffn_other = swapped(sum_ffn, CORE_BIT)
    out_ffn_in, out_ffn_out = joined(
        sum_ffn,
        ffn_other,
        [
            ([0], hidden_units, False),
            (list(range(hidden_units, 2 * hidden_units, features)), features, False),
        ],
    )
    rest_at = sum_mid.shape[1]
    sum_rest = gathered(after(sum_rest, sum_ffn), chip, out_ffn_in, out_ffn_out)
    d_hidden = (
        grad_sum1
        + matmul_right(dq, w_self_qkv[:, :features])
        + matmul_right(dk, w_key)
        + matmul_right(dv, w_value)
        + d_hidden_far.astype(f32)
    )
    d_enc = matmul_right(dck, w_ckey) + matmul_right(dcv, w_cvalue) + d_enc_far.astype(f32)

    d_vocab = d_vocab.astype(f32)
    rest_other = after(swapped(sum_rest, CORE_BIT), d_hidden, d_enc, d_vocab)
    pair_at = 4 * features
    out_cross_out, out_cross_q, out_cross_kv, out_pair, out_self_qkv, out_self_out, small = joined(
        sum_rest,
        rest_other,
        [
            ([0], features, False),
            ([features], features, False),
            ([2 * features], 2 * features, False),
            ([pair_at, pair_at + pair_count], pair_count, False),
            ([rest_at], 3 * features, False),
            ([rest_at + 3 * features], features, False),
            ([rest_at + 4 * features], LANES, True),
        ],
    )
    units = hidden_units // features
    out_b_ffn_in = small[:units].reshape(-1)
    out_b_ffn_out = small[units]
    out_gains = small[units + 1 : units + 4]
    out_shifts = small[units + 4 : units + 7]
    out_b_pair = small[units + 7, :pair_count]
    out_delete = jnp.transpose(small[units + 8 : units + 10])
    return (
        three_low[None],
        d_hidden[None],
        d_enc[None],
        out_self_qkv,
        out_self_out,
        out_cross_q,
        out_cross_kv,
        out_cross_out,
        out_ffn_in,
        out_b_ffn_in,
        out_ffn_out,
        out_b_ffn_out,
        out_gains,
        out_shifts,
        d_vocab,
        out_pair,
        out_b_pair,
        out_delete,
    )


def solution(mesh):
    split_mesh = Mesh(mesh.devices.reshape(-1, 2, 2, mesh.shape["seq"]), AXES)
    rows = ("far", "near", "core")
    split = P(rows, "seq", None)
    ids = P(rows, "seq")
    return jax.shard_map(
        per_device,
        mesh=split_mesh,
        in_specs=(split, split) + (ids,) * 7 + (P(),) * 15,
        out_specs=(split,) * 3 + (P(),) * 11 + (P(AXES, None),) + (P(),) * 3,
        check_vma=False,
    )
```

```python
import functools

import jax
import jax.numpy as jnp
from jax import lax
from jax.experimental import pallas as pl
from jax.experimental.pallas import tpu as pltpu
from jax.sharding import Mesh
from jax.sharding import PartitionSpec as P

HEADS = 8
HEAD_DIM = 64
LANES = 128
SCALE = HEAD_DIM**-0.5
EPSILON = 1e-05
NEGATIVE = -1e30
TILE = 256
STEP_PAIRS = 2

SEQ_BIT, CORE_BIT, NEAR_BIT = 1, 2, 4
GROUP = 8

bf16 = jnp.bfloat16
f32 = jnp.float32


def matmul(left, right):
    return jnp.dot(left, right, preferred_element_type=f32)


def matmul_left(left, right):
    return lax.dot_general(left, right, (((0,), (0,)), ((), ())), preferred_element_type=f32)


def matmul_right(left, right):
    return lax.dot_general(left, right, (((1,), (1,)), ((), ())), preferred_element_type=f32)


def smooth_gate(value):
    return jax.nn.gelu(value, approximate=True)


def norm_forward(summed, gain_row, shift_row):
    centered = summed - jnp.mean(summed, -1, keepdims=True)
    invert = lax.rsqrt(jnp.mean(centered * centered, -1, keepdims=True) + EPSILON)
    normed = centered * invert
    return (normed * gain_row + shift_row, normed, invert)


def norm_backward(upstream, normed, invert, gain_row):
    scaled = upstream * gain_row
    centered = (
        scaled
        - jnp.mean(scaled, -1, keepdims=True)
        - normed * jnp.mean(scaled * normed, -1, keepdims=True)
    )
    return (
        centered * invert,
        jnp.sum(upstream * normed, 0, keepdims=True),
        jnp.sum(upstream, 0, keepdims=True),
    )


def passed_along(value, axis, steps):
    count = lax.axis_size(axis)
    leading, last = (max(0, -steps), min(count, count - steps))
    return lax.ppermute(value, axis, [(source, source + steps) for source in range(leading, last)])


AXES = ("far", "near", "core", "seq")


def place():
    return lax.axis_index(AXES)


def place_count():
    return lax.axis_size("far") * GROUP


def swapped(value, mask):
    return lax.ppermute(value, AXES, [(i, i ^ mask) for i in range(place_count())])


def after(value, *others):
    return lax.optimization_barrier((value,) + others)[0]


def group_index(bits):
    me = place()
    return sum(((me & bit) != 0).astype(jnp.int32) << n for n, bit in enumerate(bits))


def group_mask(bits, relative):
    return sum(bit for n, bit in enumerate(bits) if (relative >> n) & 1)


def scattered(value, bits):
    count = 1 << len(bits)
    rows = value.shape[0] // count
    index = group_index(bits)
    part = lambda relative: lax.dynamic_slice_in_dim(value, (index ^ relative) * rows, rows)
    return part(0), [swapped(part(r), group_mask(bits, r)) for r in range(1, count)]


def part_sum(own, others):
    total = own.astype(f32)
    for other in others:
        total = total + other.astype(f32)
    return total.astype(bf16)


def scatter_sum(value, bits, *late):
    own, others = scattered(value, bits)
    if late:
        others = [after(other, *late) for other in others]
    return part_sum(own, others)


def gathered(value, bits, *late):
    count = 1 << len(bits)
    index = group_index(bits)
    parts = [value] + [swapped(value, group_mask(bits, r)) for r in range(1, count)]
    if late:
        parts = [after(part, *late) for part in parts]
    for n in range(len(bits)):
        odd = ((index >> n) & 1) == 1
        parts = [
            jnp.where(odd, jnp.concatenate([second, first], 0), jnp.concatenate([first, second], 0))
            for first, second in zip(parts[::2], parts[1::2])
        ]
    return parts[0]


def doubled(value, bits, *late):
    for bit in bits:
        other = swapped(value, bit)
        if late:
            other = after(other, *late)
        value = (value.astype(f32) + other.astype(f32)).astype(bf16)
    return value


def far_bits():
    count = place_count()
    return [1 << n for n in range(3, count.bit_length() - 1)]


def kernel_call(body, grid, in_specs, out_specs, out_shape, scratch, flops, vmem, prefetch=0):
    return pl.pallas_call(
        body,
        grid_spec=pltpu.PrefetchScalarGridSpec(
            num_scalar_prefetch=prefetch,
            grid=grid,
            in_specs=in_specs,
            out_specs=out_specs,
            scratch_shapes=scratch,
        ),
        out_shape=out_shape,
        compiler_params=pltpu.CompilerParams(vmem_limit_bytes=vmem << 20),
        cost_estimate=pl.CostEstimate(flops=flops, bytes_accessed=8 << 20, transcendentals=0),
    )


def dot_nt(left, right):
    return lax.dot_general(left, right, (((1,), (1,)), ((), ())), preferred_element_type=f32)


def dot_tn(left, right):
    return lax.dot_general(left, right, (((0,), (0,)), ((), ())), preferred_element_type=f32)


def head_lanes(shape, head):
    lane = lax.broadcasted_iota(jnp.int32, shape, 1)
    return (lane >= HEAD_DIM) == (head == 1)


def attend_body(q_ref, ko_ref, kr_ref, vo_ref, vr_ref, sq_ref, so_ref, sr_ref, out_ref, lse_ref, stat):
    step = pl.program_id(0)
    rows = q_ref.shape[0]
    heads = 2 * STEP_PAIRS

    @pl.when(step == 0)
    def _():
        stat[...] = jnp.zeros_like(stat)

    lane = lax.broadcasted_iota(jnp.int32, (rows, LANES), 1)
    same_own = sq_ref[...] == so_ref[...]
    same_far = sq_ref[...] == sr_ref[...]

    def scores(head):
        at = slice(head // 2 * LANES, (head // 2 + 1) * LANES)
        queries = q_ref[:, at].astype(f32) * SCALE
        queries = jnp.where(head_lanes((rows, LANES), head % 2), queries, 0.0).astype(bf16)
        return (
            jnp.where(same_own, dot_nt(queries, ko_ref[:, at]), NEGATIVE),
            jnp.where(same_far, dot_nt(queries, kr_ref[:, at]), NEGATIVE),
        )

    kept = stat[...]
    mixed = []
    ahead = scores(0)
    for head in range(heads):
        s_own, s_far = ahead
        if head + 1 < heads:
            ahead = scores(head + 1)
        top = jnp.maximum(jnp.max(s_own, 1, keepdims=True), jnp.max(s_far, 1, keepdims=True))
        e_own = jnp.exp(s_own - top)
        e_far = jnp.exp(s_far - top)
        total = jnp.sum(e_own, 1, keepdims=True) + jnp.sum(e_far, 1, keepdims=True)
        at = slice(head // 2 * LANES, (head // 2 + 1) * LANES)
        mix = matmul(e_own.astype(bf16), vo_ref[:, at]) + matmul(e_far.astype(bf16), vr_ref[:, at])
        mixed.append(mix / total)
        kept = jnp.where(lane == heads * step + head, top + jnp.log(total), kept)
    for pair in range(STEP_PAIRS):
        at = slice(pair * LANES, (pair + 1) * LANES)
        out_ref[:, at] = jnp.where(lane < HEAD_DIM, mixed[2 * pair], mixed[2 * pair + 1]).astype(bf16)
    stat[...] = kept

    @pl.when(step == pl.num_programs(0) - 1)
    def _():
        turned = jnp.transpose(stat[...])
        for pair in range(HEADS // 2):
            lse_ref[pair] = turned[2 * pair : 2 * pair + 2, :]


def attend(query, q_at, own, ko_at, vo_at, far, kr_at, vr_at, seg_q, seg_own, seg_far):
    rows, keys = query.shape[0], own.shape[0]
    pick = lambda n, at: pl.BlockSpec(
        (n, STEP_PAIRS * LANES), lambda h, at=at: (0, at // STEP_PAIRS + h)
    )
    whole = lambda *shape: pl.BlockSpec(shape, lambda h: (0, 0))
    return kernel_call(
        attend_body,
        (HEADS // 2 // STEP_PAIRS,),
        [
            pick(rows, q_at),
            pick(keys, ko_at),
            pick(keys, kr_at),
            pick(keys, vo_at),
            pick(keys, vr_at),
            whole(rows, 1),
            whole(1, keys),
            whole(1, keys),
        ],
        [pick(rows, 0), pl.BlockSpec((HEADS // 2, 2, rows), lambda h: (0, 0, 0))],
        [
            jax.ShapeDtypeStruct((rows, HEADS * HEAD_DIM), bf16),
            jax.ShapeDtypeStruct((HEADS // 2, 2, rows), f32),
        ],
        [pltpu.VMEM((rows, LANES), f32)],
        16 * rows * keys * 512,
        40,
    )(query, own, far, own, far, seg_q.reshape(rows, 1), seg_own.reshape(1, keys), seg_far.reshape(1, keys))


def attend_back_body(
    q_ref, g_ref, o_ref, lse_ref, ko_ref, kr_ref, vo_ref, vr_ref, sq_ref, so_ref, sr_ref,
    dq_ref, dko_ref, dvo_ref, dkr_ref, dvr_ref,
):
    rows = q_ref.shape[0]
    which = lax.broadcasted_iota(jnp.int32, (8, LANES), 0)
    lane = lax.broadcasted_iota(jnp.int32, (8, LANES), 1)
    chooser = jnp.where((lane >= HEAD_DIM) == (which == 1), 1.0, 0.0).astype(f32)
    along, q_of, g_of = [], [], []
    for pair in range(STEP_PAIRS):
        at = slice(pair * LANES, (pair + 1) * LANES)
        queries = q_ref[:, at].astype(f32) * SCALE
        upstream = g_ref[:, at].astype(f32)
        rows_along = lax.dot_general(
            chooser,
            upstream * o_ref[:, at].astype(f32),
            (((1,), (1,)), ((), ())),
            precision=lax.Precision.HIGHEST,
            preferred_element_type=f32,
        )
        for head in range(2):
            mine = head_lanes((rows, LANES), head)
            along.append(rows_along[head : head + 1, :])
            q_of.append(jnp.where(mine, queries, 0.0).astype(bf16))
            g_of.append(jnp.where(mine, upstream, 0.0).astype(bf16))
    halves = (
        (ko_ref, vo_ref, so_ref, dko_ref, dvo_ref),
        (kr_ref, vr_ref, sr_ref, dkr_ref, dvr_ref),
    )
    units = [
        (pair, head, half) for pair in range(STEP_PAIRS) for half in range(2) for head in range(2)
    ]

    def products(unit):
        pair, head, half = unit
        at = slice(pair * LANES, (pair + 1) * LANES)
        k_ref, v_ref = halves[half][:2]
        return dot_nt(k_ref[:, at], q_of[2 * pair + head]), dot_nt(v_ref[:, at], g_of[2 * pair + head])

    dq_of = [None] * (2 * STEP_PAIRS)
    ahead = products(units[0])
    for n, unit in enumerate(units):
        pair, head, half = unit
        index = 2 * pair + head
        at = slice(pair * LANES, (pair + 1) * LANES)
        k_ref, _, s_ref, dk_ref, dv_ref = halves[half]
        scores, back = ahead
        if n + 1 < len(units):
            ahead = products(units[n + 1])
        same = s_ref[...] == sq_ref[...]
        weights = jnp.exp(jnp.where(same, scores, NEGATIVE) - lse_ref[pair, head : head + 1, :])
        grad = (weights * (back - along[index])).astype(bf16)
        dv = matmul(weights.astype(bf16), g_of[index])
        dk = matmul(grad, q_of[index])
        if head == 0:
            key_t = jnp.transpose(k_ref[:, at].astype(f32)).astype(bf16)
            first = (dk, dv)
        else:
            dk_ref[:, at] = (first[0] + dk).astype(bf16)
            dv_ref[:, at] = (first[1] + dv).astype(bf16)
        dq = matmul(key_t[head * HEAD_DIM : (head + 1) * HEAD_DIM, :], grad)
        dq_of[index] = dq if dq_of[index] is None else dq_of[index] + dq
    for pair in range(STEP_PAIRS):
        at = slice(pair * LANES, (pair + 1) * LANES)
        dq = jnp.concatenate(dq_of[2 * pair : 2 * pair + 2], 0)
        dq_ref[:, at] = (jnp.transpose(dq) * SCALE).astype(bf16)


def attend_back(query, q_at, upstream, mixed, lse, own, ko_at, vo_at, far, kr_at, vr_at, seg_q, seg_own, seg_far):
    rows, keys = query.shape[0], own.shape[0]
    pick = lambda n, at: pl.BlockSpec(
        (n, STEP_PAIRS * LANES), lambda h, at=at: (0, at // STEP_PAIRS + h)
    )
    whole = lambda *shape: pl.BlockSpec(shape, lambda h: (0, 0))
    width = HEADS * HEAD_DIM
    return kernel_call(
        attend_back_body,
        (HEADS // 2 // STEP_PAIRS,),
        [
            pick(rows, q_at),
            pick(rows, 0),
            pick(rows, 0),
            pl.BlockSpec((STEP_PAIRS, 2, rows), lambda h: (h, 0, 0)),
            pick(keys, ko_at),
            pick(keys, kr_at),
            pick(keys, vo_at),
            pick(keys, vr_at),
            whole(1, rows),
            whole(keys, 1),
            whole(keys, 1),
        ],
        [pick(rows, 0)] + [pick(keys, 0)] * 4,
        [jax.ShapeDtypeStruct((rows, width), bf16)] + [jax.ShapeDtypeStruct((keys, width), bf16)] * 4,
        [],
        40 * rows * keys * 512,
        40,
    )(
        query, upstream, mixed, lse, own, far, own, far,
        seg_q.reshape(1, rows), seg_own.reshape(keys, 1), seg_far.reshape(keys, 1),
    )


def columns_of(row):
    return jnp.transpose(jnp.broadcast_to(row, (LANES, row.shape[1])))


def vocab_body(info, *refs):
    blocks, (t_ref, w_ref, e_ref, stat_ref, hidden_ref, kept, targets) = refs[:GROUP], refs[GROUP:]
    step = pl.program_id(0)
    chunk = 128

    @pl.when(step == 0)
    def _():
        for start in range(0, kept.shape[0], TILE):

            @pl.when(start < info[16])
            def _(start=start):
                kept[start : start + TILE, :] = jnp.zeros((TILE, kept.shape[1]), kept.dtype)
                targets[start : start + TILE, :] = jnp.zeros((TILE, LANES), f32)

        for rel in range(GROUP):
            core, near = rel // 4, rel % 4
            block = (core | (near << 1)) ^ info[17]
            count, offset = info[block], info[8 + block]
            src = blocks[rel]
            for start in range(0, src.shape[0], chunk):

                @pl.when(start < count)
                def _(src=src, rel=rel, start=start, offset=offset):
                    for piece in range(start, start + chunk, 16):

                        @pl.when(piece < count)
                        def _(piece=piece):
                            to = pl.ds(pl.multiple_of(offset + piece, 16), 16)
                            kept[to, :] = src[piece : piece + 16, :]

                    value = columns_of(t_ref[rel : rel + 1, start : start + chunk])
                    for piece in range(start, start + chunk, 16):

                        @pl.when(piece < count)
                        def _(piece=piece):
                            to = pl.ds(pl.multiple_of(offset + piece, 16), 16)
                            targets[to, :] = value[piece - start : piece - start + 16, :]

    @pl.when(step * TILE < info[16])
    def _():
        rows = pl.ds(pl.multiple_of(step * TILE, TILE), TILE)
        hidden = kept[rows, :]
        hidden_ref[...] = hidden
        outer, _, piece, _ = w_ref.shape
        tops, totals = [], []
        ahead = dot_nt(w_ref[0, 0], hidden)
        for n in range(outer):
            value = ahead
            if n + 1 < outer:
                ahead = dot_nt(w_ref[n + 1, 0], hidden)
            top = jnp.max(value, 0, keepdims=True)
            value = jnp.exp(value - top)
            tops.append(top)
            totals.append(jnp.sum(value, 0, keepdims=True))
            e_ref[0, n * piece : (n + 1) * piece, :] = value.astype(bf16)
        top = functools.reduce(jnp.maximum, tops)
        shares = [jnp.exp(part - top) for part in tops]
        total = sum(part * share for part, share in zip(totals, shares))
        target = jnp.transpose(targets[rows, :])[:1, :]
        lines = [top, total, target] + shares
        lines.append(jnp.zeros((stat_ref.shape[0] - len(lines), TILE), f32))
        stat_ref[...] = jnp.concatenate(lines, 0)


def stat_lines(outer):
    return -(-(3 + outer + 1) // 8) * 8


def last_active(i, info):
    return jnp.minimum(i, jnp.maximum((info[16] + TILE - 1) // TILE - 1, 0))


def vocab_slice(w):
    outer, _, block, width = w.shape
    return pl.BlockSpec(
        (outer, 1, block, width), lambda i, info: (0, info[18], 0, 0), pipeline_mode=pl.Buffered(1)
    )


def vocab_forward(info, blocks, targets, w):
    rows, width = blocks[0].shape
    total = GROUP * rows
    wide = w.shape[0] * w.shape[2]
    once = lambda *shape: pl.BlockSpec(
        shape, lambda i, info: (0,) * len(shape), pipeline_mode=pl.Buffered(1)
    )
    return kernel_call(
        vocab_body,
        (total // TILE,),
        [once(rows, width)] * GROUP + [once(GROUP, rows), vocab_slice(w)],
        [
            pl.BlockSpec((1, wide, TILE), lambda i, info: (last_active(i, info), 0, 0)),
            pl.BlockSpec((stat_lines(w.shape[0]), TILE), lambda i, info: (0, last_active(i, info))),
            pl.BlockSpec((TILE, width), lambda i, info: (last_active(i, info), 0)),
        ],
        [
            jax.ShapeDtypeStruct((total // TILE, wide, TILE), bf16),
            jax.ShapeDtypeStruct((stat_lines(w.shape[0]), total), f32),
            jax.ShapeDtypeStruct((total, width), bf16),
        ],
        [
            pltpu.VMEM((total, width), bf16),
            pltpu.VMEM((total, LANES), f32),
        ],
        1400 * wide * width * 2,
        34,
        prefetch=1,
    )(info, *blocks, targets, w)


def vocab_back_body(info, e_ref, s_ref, w_ref, out_ref):
    @pl.when(pl.program_id(0) * out_ref.shape[0] < info[16])
    def _():
        outer, _, piece, width = w_ref.shape
        back = None
        for n in range(outer):
            at = slice(n * piece, (n + 1) * piece)
            weights = jnp.concatenate([e_ref[t, at, :] for t in range(e_ref.shape[0])], 1)
            share = columns_of(s_ref[3 + n : 4 + n, :])
            share = jnp.concatenate([share] * (width // LANES), 1)
            value = dot_tn(weights, w_ref[n, 0]) * share
            back = value if back is None else back + value
        out_ref[...] = back.astype(bf16)


def vocab_back(info, e, stats, w):
    tiles, wide, _ = e.shape
    width = w.shape[3]
    both = 2 * TILE
    at = lambda i, info: jnp.minimum(i, jnp.maximum((info[16] + both - 1) // both - 1, 0))
    return kernel_call(
        vocab_back_body,
        (tiles // 2,),
        [
            pl.BlockSpec((2, wide, TILE), lambda i, info: (at(i, info), 0, 0)),
            pl.BlockSpec((stats.shape[0], both), lambda i, info: (0, at(i, info))),
            vocab_slice(w),
        ],
        pl.BlockSpec((both, width), lambda i, info: (at(i, info), 0)),
        jax.ShapeDtypeStruct((tiles * TILE, width), bf16),
        [],
        1400 * wide * width * 2,
        26,
        prefetch=1,
    )(info, e, stats, w)


def spread_body(info, g_ref, f_ref, *refs):
    outs, columns = refs[:-1], refs[-1]
    step = pl.program_id(0)
    total, width = g_ref.shape
    rows = outs[0].shape[0]

    @pl.when(step == 0)
    def _():
        for start in range(0, total, TILE):
            columns[start : start + TILE, :] = columns_of(f_ref[:, start : start + TILE])

    def block_of(core, near):
        block = (core | (near << 1)) ^ info[17]
        at = pl.ds(pl.multiple_of(info[8 + block], 16), rows)
        row = lax.broadcasted_iota(jnp.int32, (rows, LANES), 0)
        factor = jnp.where(row < info[block], columns[at, :], 0.0)
        live = row < info[block]
        pieces = [
            jnp.where(live, g_ref[at, start : start + LANES].astype(f32) * factor, 0.0)
            for start in range(0, width, LANES)
        ]
        return jnp.concatenate(pieces, 1).astype(bf16)

    for n, out_ref in enumerate(outs):

        @pl.when(step == n)
        def _(n=n, out_ref=out_ref):
            out_ref[...] = block_of(1 - n // 4, n % 4)


def spread(info, g, factor, rows):
    total, width = g.shape
    once = lambda *shape: pl.BlockSpec(
        shape, lambda i, info: (0,) * len(shape), pipeline_mode=pl.Buffered(1)
    )
    return kernel_call(
        spread_body,
        (GROUP,),
        [once(total, width), once(1, total)],
        [once(rows, width)] * GROUP,
        [jax.ShapeDtypeStruct((rows, width), bf16)] * GROUP,
        [pltpu.VMEM((total, LANES), f32)],
        total * width,
        58,
        prefetch=1,
    )(info, g, factor)


def vocab_grad_body(piece, info, e_ref, h_ref, s_ref, f_ref, out_ref, total):
    step = pl.program_id(0)

    @pl.when(step == 0)
    def _():
        total[...] = jnp.zeros_like(total)

    @pl.when(step * TILE < info[16])
    def _():
        wide = e_ref.shape[1]
        factor = f_ref[...]
        target = s_ref[2:3, :].astype(jnp.int32)
        row = 1 + lax.broadcasted_iota(jnp.int32, (piece, TILE), 0)
        for start in range(0, wide, piece):
            at = slice(start, start + piece)
            share = 3 + start // piece
            weights = e_ref[0, at, :].astype(f32) * (factor * s_ref[share : share + 1, :])
            weights = (weights - jnp.where(row == target - start, 1.0, 0.0)).astype(bf16)
            total[at, :] += matmul(weights, h_ref[...])

    @pl.when(step == pl.num_programs(0) - 1)
    def _():
        out_ref[...] = total[...].astype(bf16)


def vocab_grad(info, e, hidden, stats, factor, piece):
    tiles, wide, _ = e.shape
    width = hidden.shape[1]
    tile = lambda n: pl.BlockSpec((TILE, n), lambda i, info: (last_active(i, info), 0))
    return kernel_call(
        functools.partial(vocab_grad_body, piece),
        (tiles,),
        [
            pl.BlockSpec((1, wide, TILE), lambda i, info: (last_active(i, info), 0, 0)),
            tile(width),
            pl.BlockSpec((stats.shape[0], TILE), lambda i, info: (0, last_active(i, info))),
            pl.BlockSpec((1, TILE), lambda i, info: (0, last_active(i, info))),
        ],
        pl.BlockSpec((wide, width), lambda i, info: (0, 0)),
        jax.ShapeDtypeStruct((wide, width), bf16),
        [pltpu.VMEM((wide, width), f32)],
        1400 * wide * width * 2,
        40,
        prefetch=1,
    )(info, e, hidden, stats, factor)


def halves_body(plan, info, *refs):
    plan, parts = plan
    operands, outs = refs[: -2 * parts], refs[-2 * parts :]
    rows = outs[0].shape[0]

    def fill(half, out_refs):
        at, part = 0, 0
        for terms, width in plan:
            if at == out_refs[part].shape[1]:
                at, part = 0, part + 1
            out_ref = out_refs[part]
            total = None
            for left, left_at, right, right_at in terms:
                if right is None:
                    lines = [operands[n][:, start : start + 2 * rows] for n, start in left]
                    blank = width - sum(line.shape[0] for line in lines)
                    lines.append(jnp.zeros((blank, 2 * rows), f32))
                    turned = jnp.transpose(jnp.concatenate(lines, 0))
                    value = jnp.where(half == 0, turned[:rows], turned[rows:])
                else:
                    lanes = pl.ds(pl.multiple_of(left_at + half * rows, rows), rows)
                    value = dot_tn(
                        operands[left][:, lanes], operands[right][:, right_at : right_at + width]
                    )
                total = value if total is None else total + value
            out_ref[:, at : at + width] = total.astype(bf16)
            at += width

    @pl.when(pl.program_id(0) == 0)
    def _():
        fill(1 - info[0], outs[:parts])

    @pl.when(pl.program_id(0) == 1)
    def _():
        fill(info[0], outs[parts:])


def weight_halves(columns, rows, vmem=36, parts=1):
    operands, plan = [], []

    def index_of(array):
        for n, known in enumerate(operands):
            if known is array:
                return n
        operands.append(array)
        return len(operands) - 1

    for width, terms in columns:
        taken = []
        for left, left_at, right, right_at in terms:
            if right is None:
                taken.append(([(index_of(row), start) for row, start in left], 0, None, 0))
            else:
                taken.append((index_of(left), left_at, index_of(right), right_at))
        plan.append((taken, width))
    total = sum(width for width, _ in columns)
    whole = lambda shape: pl.BlockSpec(shape, lambda i, info: (0, 0), pipeline_mode=pl.Buffered(1))
    return kernel_call(
        functools.partial(halves_body, (plan, parts)),
        (2,),
        [whole(o.shape) for o in operands],
        [whole((rows // 2, total // parts))] * (2 * parts),
        [jax.ShapeDtypeStruct((rows // 2, total // parts), bf16)] * (2 * parts),
        [],
        rows * total * 1024,
        vmem,
        prefetch=1,
    )(group_index([CORE_BIT])[None], *operands)


def core_summed(send, keep):
    return (keep.astype(f32) + swapped(send, CORE_BIT).astype(f32)).astype(bf16)


def joined_body(plan, info, own_ref, other_ref, *outs):
    rows = own_ref.shape[0]
    mine, far = pl.multiple_of(info[0] * rows, rows), pl.multiple_of((1 - info[0]) * rows, rows)
    for (starts, width, turned), out_ref in zip(plan, outs):
        for n, start in enumerate(starts):
            for ref, at in ((own_ref, mine), (other_ref, far)):
                value = ref[:, start : start + width].astype(f32)
                if turned:
                    out_ref[:, pl.ds(at, rows)] = jnp.transpose(value)
                else:
                    out_ref[pl.ds(n * 2 * rows + at, rows), :] = value


def joined(own, other, plan):
    rows = own.shape[0]
    shapes = [
        (width, 2 * rows) if turned else (2 * rows * len(starts), width)
        for starts, width, turned in plan
    ]
    once = lambda shape: pl.BlockSpec(shape, lambda i, info: (0, 0), pipeline_mode=pl.Buffered(1))
    return kernel_call(
        functools.partial(joined_body, plan),
        (1,),
        [once(own.shape)] * 2,
        [once(shape) for shape in shapes],
        [jax.ShapeDtypeStruct(shape, f32) for shape in shapes],
        [],
        own.size,
        36,
        prefetch=1,
    )(group_index([CORE_BIT])[None], own, other)


def as_columns_body(rows_ref, *outs):
    for n, out_ref in enumerate(outs):
        out_ref[...] = columns_of(rows_ref[n : n + 1, :])[:, :1].astype(jnp.int32)


def as_columns(*rows):
    count = rows[0].shape[0]
    whole = lambda *shape: pl.BlockSpec(shape, lambda i, info: (0, 0))
    return kernel_call(
        as_columns_body_with_info,
        (1,),
        [whole(len(rows), count)],
        [whole(count, 1)] * len(rows),
        [jax.ShapeDtypeStruct((count, 1), jnp.int32)] * len(rows),
        [],
        count,
        16,
        prefetch=1,
    )(jnp.zeros((1,), jnp.int32), jnp.stack(rows).astype(f32))


def as_columns_body_with_info(info, *refs):
    as_columns_body(*refs)


def added_body(info, *refs):
    count = len(refs) // 3
    for n in range(count):
        total = refs[n][...].astype(f32) + refs[count + n][...].astype(f32)
        refs[2 * count + n][...] = total.astype(bf16)


def added(firsts, seconds):
    rows, width = firsts[0].shape
    piece = pl.BlockSpec((rows // 4, width), lambda i, info: (i, 0))
    return kernel_call(
        added_body,
        (4,),
        [piece] * (2 * len(firsts)),
        [piece] * len(firsts),
        [jax.ShapeDtypeStruct((rows, width), bf16)] * len(firsts),
        [],
        rows * width,
        58,
        prefetch=1,
    )(jnp.zeros((1,), jnp.int32), *firsts, *seconds)


def per_device(
    hidden_in,
    enc_states,
    segment_ids,
    edit_pass,
    enc_segments,
    target_tokens,
    placeholder_counts,
    delete_labels,
    loss_mask,
    w_self_qkv,
    w_self_out,
    w_cross_q,
    w_cross_kv,
    w_cross_out,
    w_ffn_in,
    b_ffn_in,
    w_ffn_out,
    b_ffn_out,
    norm_gains,
    norm_shifts,
    w_vocab,
    w_pair,
    b_pair,
    w_delete,
):
    _, tokens, features = hidden_in.shape
    seq = lax.axis_index("seq")
    chip = [NEAR_BIT, SEQ_BIT]
    far = far_bits()
    hidden = hidden_in[0]
    source = enc_states[0]
    hidden_far = swapped(hidden, SEQ_BIT)
    qkv = matmul(hidden, w_self_qkv).astype(bf16)
    segment, passes, source_seg = segment_ids[0], edit_pass[0], enc_segments[0]

    keep_float = loss_mask[0].astype(f32)
    token_keep = keep_float * (passes == 2).astype(f32)
    row = lax.broadcasted_iota(jnp.int32, (tokens, tokens), 0)
    col = lax.broadcasted_iota(jnp.int32, (tokens, tokens), 1)
    rank = matmul(token_keep.astype(bf16)[None, :], (row <= col).astype(bf16)) - 1.0
    selects = (rank.astype(jnp.int32) == row) & (token_keep[None, :] > 0)
    chooser = selects.astype(bf16)
    targets = target_tokens[0]
    chosen = jnp.sum(jnp.where(selects, targets[None, :] + 1, 0), 1)
    ids_far = swapped(jnp.stack([segment, source_seg, chosen]), SEQ_BIT)
    segment_far, source_seg_far = ids_far[0], ids_far[1]

    vocab = w_vocab.shape[0]
    outer = lax.axis_size("far")
    block = vocab // (outer * GROUP)
    inner = lax.axis_index(("near", "core", "seq"))
    here = group_index([CORE_BIT, NEAR_BIT, SEQ_BIT])
    ckv = matmul(source, w_cross_kv).astype(bf16)
    hidden_far = after(hidden_far, ckv, qkv, chosen)
    kv_far = matmul(hidden_far, w_self_qkv[:, features:]).astype(bf16)
    source_far = swapped(after(source, hidden_far), SEQ_BIT)
    self_mix, self_lse = attend(qkv, 0, qkv, 4, 8, kv_far, 0, 4, segment, segment, segment_far)
    chosen_row = jnp.stack([chosen, ids_far[2]])
    chosen_near = swapped(chosen_row, NEAR_BIT)
    self_mix, self_lse, source_far, chosen_near = lax.optimization_barrier(
        (self_mix, self_lse, source_far, chosen_near)
    )
    layer_one, normed_one, invert_one = norm_forward(
        hidden.astype(f32) + matmul(self_mix, w_self_out), norm_gains[0], norm_shifts[0]
    )

    chosen_chip = jnp.stack([chosen_row[0], chosen_near[0], chosen_row[1], chosen_near[1]])
    chosen_core = swapped(chosen_chip, CORE_BIT)
    one_low = layer_one.astype(bf16)
    cross_query = matmul(one_low, w_cross_q).astype(bf16)
    ckv_far = matmul(source_far, w_cross_kv).astype(bf16)
    cross_mix, cross_lse = attend(
        cross_query, 0, ckv, 0, 4, ckv_far, 0, 4, segment, source_seg, source_seg_far
    )
    cross_mix, cross_lse, chosen_core = lax.optimization_barrier((cross_mix, cross_lse, chosen_core))
    chosen_all = jnp.concatenate([chosen_chip, chosen_core])
    index = chosen_all - 1
    local = (index // (block * GROUP)) * block + index % block + 1
    mine = (chosen_all > 0) & ((index // block) % GROUP == inner)
    local_targets = jnp.where(mine, local, 0).astype(f32)
    counts_rel = jnp.sum((chosen_all > 0).astype(jnp.int32), 1)
    relative = jnp.array([c | (n << 1) for c in range(2) for n in range(4)], jnp.int32) ^ here
    counts = jnp.sum(
        jnp.where(relative[:, None] == jnp.arange(GROUP)[None, :], counts_rel[:, None], 0), 0
    )
    rounded = (counts + 15) // 16 * 16
    before = jnp.arange(GROUP)[:, None] < jnp.arange(GROUP)[None, :]
    offsets = jnp.sum(jnp.where(before, rounded[:, None], 0), 0)
    info = jnp.concatenate([counts, offsets, jnp.sum(rounded)[None], here[None], inner[None]]).astype(jnp.int32)

    layer_two, normed_two, invert_two = norm_forward(
        layer_one + matmul(cross_mix, w_cross_out), norm_gains[1], norm_shifts[1]
    )
    two_low = layer_two.astype(bf16)
    pre_act = matmul(two_low, w_ffn_in) + b_ffn_in
    activ, gate_back = jax.vjp(smooth_gate, pre_act)
    activ_low = activ.astype(bf16)
    layer_three, normed_three, invert_three = norm_forward(
        layer_two + (matmul(activ_low, w_ffn_out) + b_ffn_out), norm_gains[2], norm_shifts[2]
    )
    three_low = layer_three.astype(bf16)

    kept = matmul(chooser, three_low).astype(bf16)
    kept_core = swapped(kept, CORE_BIT)
    kept_chip = [swapped(kept, NEAR_BIT), swapped(kept, SEQ_BIT), swapped(kept, NEAR_BIT | SEQ_BIT)]
    next_row = passed_along(three_low[:1], "seq", -1)
    w_parts = w_vocab.reshape(outer, GROUP, block, features)
    target_rows = jnp.take(w_vocab, after(targets, kept), axis=0).astype(f32)
    kept_chip = [after(k, target_rows) for k in kept_chip]
    kept_other = [swapped(k, CORE_BIT) for k in kept_chip]

    delete_keep = keep_float * (passes == 0).astype(f32)

    def label_grad(logits, labels, keep_mask):
        shifted = logits - jnp.max(logits, -1, keepdims=True)
        exponent = jnp.exp(shifted)
        weights = exponent / jnp.sum(exponent, -1, keepdims=True)
        onehot = labels[:, None] == lax.broadcasted_iota(jnp.int32, logits.shape, 1)
        return ((weights - onehot.astype(f32)) * keep_mask[:, None]).astype(bf16)

    delete_grad = label_grad(matmul(three_low, w_delete), delete_labels[0], delete_keep)

    delete_back = matmul_right(delete_grad, w_delete) - target_rows * token_keep[:, None]
    d_delete = matmul_left(delete_grad, three_low)
    segment_col, segment_far_col, source_col, source_far_col = as_columns(
        segment, segment_far, source_seg, source_seg_far
    )
    info, segment_col, segment_far_col, source_col, source_far_col = lax.optimization_barrier(
        (info, segment_col, segment_far_col, source_col, source_far_col)
    )
    pair_own = matmul(three_low, w_pair[:features]) + b_pair
    w_pair_next = after(w_pair[features:], kept)
    info = after(info, delete_back, d_delete, pair_own, w_pair_next)
    e, stat_rows, kept_all = vocab_forward(
        info, [kept] + kept_chip + [kept_core] + kept_other, local_targets, w_parts
    )
    stats = stat_rows[:2]

    def merged(first, *others):
        most = functools.reduce(jnp.maximum, [o[0] for o in others], first[0])
        added = sum((o[1] * jnp.exp(o[0] - most) for o in others), first[1] * jnp.exp(first[0] - most))
        return jnp.stack([most, added])

    stats_pair = merged(stats, swapped(stats, CORE_BIT))
    stats_all = merged(stats_pair, *[swapped(stats_pair, group_mask(chip, r)) for r in (1, 2, 3)])
    factor = jnp.exp(stats[0] - stats_all[0] - jnp.log(stats_all[1]))[None, :]
    back_raw = vocab_back(info, e, stat_rows, w_parts)
    back = spread(info, back_raw, factor, tokens)
    back_core = [swapped(b, CORE_BIT) for b in back[:4]]
    back_near = back[4:]
    back_low = added(back_near[1:], back_core[1:])
    position = seq * tokens + jnp.arange(tokens, dtype=jnp.int32)
    row_length = tokens * lax.axis_size("seq")
    follow = jnp.concatenate([three_low[1:], after(next_row, *back_low)], 0)
    follow_seg = jnp.concatenate([segment[1:], segment_far[:1]], 0)
    pair_ok = (follow_seg == segment) & (position < row_length - 1)
    pair_keep = keep_float * (passes == 1).astype(f32) * pair_ok.astype(f32)
    pair_logits = pair_own + matmul(follow, w_pair_next)
    pair_grad = label_grad(pair_logits, placeholder_counts[0], pair_keep)
    follow_grad = matmul_right(pair_grad, w_pair_next)
    back_row = passed_along(follow_grad[-1:], "seq", 1)
    d_b_pair = jnp.sum(pair_grad.astype(f32), 0, keepdims=True)
    d_b_pair = jnp.pad(d_b_pair, ((0, 0), (0, features - d_b_pair.shape[1])))
    head_back = [swapped(back_low[r - 1], group_mask(chip, r)).astype(f32) for r in (1, 2, 3)]
    head_back = sum(head_back, back_near[0].astype(f32) + back_core[0].astype(f32))
    vocab_part = vocab_grad(
        info, e, kept_all, stat_rows, after(factor, *back_low), block
    )
    d_vocab = lax.psum_scatter(vocab_part, "far", scatter_dimension=0, tiled=True)
    grad_local = (
        delete_back
        + matmul_right(pair_grad, w_pair[:features])
        + jnp.concatenate([back_row, follow_grad[:-1]], 0)
    )
    grad_local = after(grad_local, vocab_part)

    grad_three = grad_local + matmul_left(chooser, head_back.astype(bf16))
    grad_sum3, gain_three, shift_three = norm_backward(
        grad_three, normed_three, invert_three, norm_gains[2]
    )
    branch_three = grad_sum3.astype(bf16)
    row_sum = lambda value: jnp.sum(value.astype(f32), 0, keepdims=True)
    d_b_ffn_out = row_sum(branch_three)
    grad_pre = gate_back(matmul_right(branch_three, w_ffn_out))[0].astype(bf16)
    d_b_ffn_in = row_sum(grad_pre)
    hidden_units = w_ffn_in.shape[1]
    pair_count = w_pair.shape[1]
    halves_ffn = weight_halves(
        [(hidden_units, [(two_low, 0, grad_pre, 0)])]
        + [(features, [(activ_low, at, branch_three, 0)]) for at in range(0, hidden_units, features)],
        features,
        parts=2,
    )
    sum_ffn = jnp.concatenate(
        [core_summed(send, keep) for send, keep in zip(halves_ffn[:2], halves_ffn[2:])], 1
    )
    grad_two = grad_sum3 + matmul_right(grad_pre, w_ffn_in)
    grad_sum2, gain_two, shift_two = norm_backward(grad_two, normed_two, invert_two, norm_gains[1])
    branch_two = grad_sum2.astype(bf16)
    cross_up = matmul_right(branch_two, w_cross_out).astype(bf16)
    cross_up, sum_ffn = lax.optimization_barrier((cross_up, sum_ffn))
    own_ffn, others_ffn = scattered(sum_ffn, chip)
    dcq, dck, dcv, dck_far, dcv_far = attend_back(
        cross_query, 0, cross_up, cross_mix, cross_lse, ckv, 0, 4, ckv_far, 0, 4,
        segment, source_col, source_far_col,
    )
    w_ckey, w_cvalue = w_cross_kv[:, :features], w_cross_kv[:, features:]
    d_enc_low = (matmul_right(dck_far, w_ckey) + matmul_right(dcv_far, w_cvalue)).astype(bf16)
    d_enc_far = swapped(d_enc_low, SEQ_BIT)
    dcq = after(dcq, d_enc_low)
    send_mid, keep_mid = weight_halves(
        [
            (features, [(cross_mix, 0, branch_two, 0)]),
            (features, [(one_low, 0, dcq, 0)]),
            (features, [(source, 0, dck, 0), (source_far, 0, dck_far, 0)]),
            (features, [(source, 0, dcv, 0), (source_far, 0, dcv_far, 0)]),
            (pair_count, [(three_low, 0, pair_grad, 0)]),
            (pair_count, [(follow, 0, pair_grad, 0)]),
        ],
        features,
    )
    keep_mid, send_mid, others_ffn = lax.optimization_barrier((keep_mid, send_mid, others_ffn))
    sum_ffn = part_sum(own_ffn, others_ffn)
    sum_mid = core_summed(send_mid, keep_mid)
    grad_one = grad_sum2 + matmul_right(after(dcq, keep_mid), w_cross_q)
    grad_sum1, gain_one, shift_one = norm_backward(grad_one, normed_one, invert_one, norm_gains[0])
    branch_one = grad_sum1.astype(bf16)
    self_up = matmul_right(branch_one, w_self_out).astype(bf16)
    self_up = after(self_up, sum_mid)
    sum_mid = scatter_sum(after(sum_mid, self_up), chip)
    own_ffn, others_ffn = scattered(sum_ffn, far[:1])
    dq, dk, dv, dk_far, dv_far = attend_back(
        qkv, 0, self_up, self_mix, self_lse, qkv, 4, 8, kv_far, 0, 4, segment, segment_col, segment_far_col
    )
    dq, dk, dv, dk_far, dv_far, sum_mid, others_ffn, d_enc_far = lax.optimization_barrier(
        (dq, dk, dv, dk_far, dv_far, sum_mid, others_ffn, d_enc_far)
    )
    sum_ffn = part_sum(own_ffn, others_ffn)

    w_key, w_value = w_self_qkv[:, features : 2 * features], w_self_qkv[:, 2 * features :]
    d_hidden_low = (matmul_right(dk_far, w_key) + matmul_right(dv_far, w_value)).astype(bf16)
    dq = after(dq, d_hidden_low)
    send_qkv, keep_qkv = weight_halves(
        [
            (features, [(hidden, 0, dq, 0)]),
            (features, [(hidden, 0, dk, 0), (hidden_far, 0, dk_far, 0)]),
            (features, [(hidden, 0, dv, 0), (hidden_far, 0, dv_far, 0)]),
            (features, [(self_mix, 0, branch_one, 0)]),
            (
                LANES,
                [
                    (
                        [(d_b_ffn_in, at) for at in range(0, hidden_units, features)]
                        + [(row, 0) for row in (d_b_ffn_out, gain_one, gain_two, gain_three)]
                        + [(row, 0) for row in (shift_one, shift_two, shift_three, d_b_pair)]
                        + [(d_delete, 0)],
                        0,
                        None,
                        0,
                    )
                ],
            ),
        ],
        features,
        58,
    )
    d_hidden_far = swapped(d_hidden_low, SEQ_BIT)
    sum_ffn = doubled(sum_ffn, far[1:], keep_qkv)
    sum_qkv, d_hidden_far, d_vocab, sum_ffn = lax.optimization_barrier((core_summed(send_qkv, keep_qkv), d_hidden_far, d_vocab, sum_ffn))
    sum_qkv = scatter_sum(sum_qkv, chip)
    sum_mid = scatter_sum(after(sum_mid, sum_ffn), far[:1], sum_qkv)
    sum_ffn = gathered(sum_ffn, far[:1], sum_qkv)
    sum_mid = doubled(sum_mid, far[1:])
    sum_mid = gathered(sum_mid, far[:1])
    sum_qkv = doubled(sum_qkv, far)
    sum_rest = jnp.concatenate([sum_mid, sum_qkv], 1)
    sum_ffn = gathered(sum_ffn, chip, sum_rest)
    ffn_other = swapped(sum_ffn, CORE_BIT)
    out_ffn_in, out_ffn_out = joined(
        sum_ffn,
        ffn_other,
        [
            ([0], hidden_units, False),
            (list(range(hidden_units, 2 * hidden_units, features)), features, False),
        ],
    )
    d_hidden = (
        grad_sum1
        + matmul_right(dq, w_self_qkv[:, :features])
        + matmul_right(dk, w_key)
        + matmul_right(dv, w_value)
        + d_hidden_far.astype(f32)
    )
    d_enc = matmul_right(dck, w_ckey) + matmul_right(dcv, w_cvalue) + d_enc_far.astype(f32)

    d_vocab = d_vocab.astype(f32)
    rest_at = sum_mid.shape[1]
    sum_rest = gathered(after(sum_rest, sum_ffn), chip, out_ffn_in, out_ffn_out, d_enc)
    rest_other = after(swapped(sum_rest, CORE_BIT), d_hidden, d_vocab)
    pair_at = 4 * features
    out_cross_out, out_cross_q, out_cross_kv, out_pair, out_self_qkv, out_self_out, small = joined(
        sum_rest,
        rest_other,
        [
            ([0], features, False),
            ([features], features, False),
            ([2 * features], 2 * features, False),
            ([pair_at, pair_at + pair_count], pair_count, False),
            ([rest_at], 3 * features, False),
            ([rest_at + 3 * features], features, False),
            ([rest_at + 4 * features], LANES, True),
        ],
    )
    units = hidden_units // features
    out_b_ffn_in = small[:units].reshape(-1)
    out_b_ffn_out = small[units]
    out_gains = small[units + 1 : units + 4]
    out_shifts = small[units + 4 : units + 7]
    out_b_pair = small[units + 7, :pair_count]
    out_delete = jnp.transpose(small[units + 8 : units + 10])
    return (
        three_low[None],
        d_hidden[None],
        d_enc[None],
        out_self_qkv,
        out_self_out,
        out_cross_q,
        out_cross_kv,
        out_cross_out,
        out_ffn_in,
        out_b_ffn_in,
        out_ffn_out,
        out_b_ffn_out,
        out_gains,
        out_shifts,
        d_vocab,
        out_pair,
        out_b_pair,
        out_delete,
    )


def solution(mesh):
    split_mesh = Mesh(mesh.devices.reshape(-1, 2, 2, mesh.shape["seq"]), AXES)
    rows = ("far", "near", "core")
    split = P(rows, "seq", None)
    ids = P(rows, "seq")
    return jax.shard_map(
        per_device,
        mesh=split_mesh,
        in_specs=(split, split) + (ids,) * 7 + (P(),) * 15,
        out_specs=(split,) * 3 + (P(),) * 11 + (P(AXES, None),) + (P(),) * 3,
        check_vma=False,
    )
```

```python
import functools

import jax
import jax.numpy as jnp
from jax import lax
from jax.experimental import pallas as pl
from jax.experimental.pallas import tpu as pltpu
from jax.sharding import Mesh
from jax.sharding import PartitionSpec as P

HEADS = 8
HEAD_DIM = 64
LANES = 128
SCALE = HEAD_DIM**-0.5
EPSILON = 1e-05
NEGATIVE = -1e30
TILE = 256
STEP_PAIRS = 2

SEQ_BIT, CORE_BIT, NEAR_BIT = 1, 2, 4
GROUP = 8

bf16 = jnp.bfloat16
f32 = jnp.float32


def matmul(left, right):
    return jnp.dot(left, right, preferred_element_type=f32)


def matmul_left(left, right):
    return lax.dot_general(left, right, (((0,), (0,)), ((), ())), preferred_element_type=f32)


def matmul_right(left, right):
    return lax.dot_general(left, right, (((1,), (1,)), ((), ())), preferred_element_type=f32)


def smooth_gate(value):
    return jax.nn.gelu(value, approximate=True)


def norm_forward(summed, gain_row, shift_row):
    centered = summed - jnp.mean(summed, -1, keepdims=True)
    invert = lax.rsqrt(jnp.mean(centered * centered, -1, keepdims=True) + EPSILON)
    normed = centered * invert
    return (normed * gain_row + shift_row, normed, invert)


def norm_backward(upstream, normed, invert, gain_row):
    scaled = upstream * gain_row
    centered = (
        scaled
        - jnp.mean(scaled, -1, keepdims=True)
        - normed * jnp.mean(scaled * normed, -1, keepdims=True)
    )
    return (
        centered * invert,
        jnp.sum(upstream * normed, 0, keepdims=True),
        jnp.sum(upstream, 0, keepdims=True),
    )


def passed_along(value, axis, steps):
    count = lax.axis_size(axis)
    leading, last = (max(0, -steps), min(count, count - steps))
    return lax.ppermute(value, axis, [(source, source + steps) for source in range(leading, last)])


AXES = ("far", "near", "core", "seq")


def place():
    return lax.axis_index(AXES)


def place_count():
    return lax.axis_size("far") * GROUP


def swapped(value, mask):
    return lax.ppermute(value, AXES, [(i, i ^ mask) for i in range(place_count())])


def after(value, *others):
    return lax.optimization_barrier((value,) + others)[0]


def group_index(bits):
    me = place()
    return sum(((me & bit) != 0).astype(jnp.int32) << n for n, bit in enumerate(bits))


def group_mask(bits, relative):
    return sum(bit for n, bit in enumerate(bits) if (relative >> n) & 1)


def scattered(value, bits):
    count = 1 << len(bits)
    rows = value.shape[0] // count
    index = group_index(bits)
    part = lambda relative: lax.dynamic_slice_in_dim(value, (index ^ relative) * rows, rows)
    return part(0), [swapped(part(r), group_mask(bits, r)) for r in range(1, count)]


def part_sum(own, others):
    total = own.astype(f32)
    for other in others:
        total = total + other.astype(f32)
    return total.astype(bf16)


def scatter_sum(value, bits, *late):
    own, others = scattered(value, bits)
    if late:
        others = [after(other, *late) for other in others]
    return part_sum(own, others)


def gathered(value, bits, *late):
    count = 1 << len(bits)
    index = group_index(bits)
    parts = [value] + [swapped(value, group_mask(bits, r)) for r in range(1, count)]
    if late:
        parts = [after(part, *late) for part in parts]
    for n in range(len(bits)):
        odd = ((index >> n) & 1) == 1
        parts = [
            jnp.where(odd, jnp.concatenate([second, first], 0), jnp.concatenate([first, second], 0))
            for first, second in zip(parts[::2], parts[1::2])
        ]
    return parts[0]


def doubled(value, bits, *late):
    for bit in bits:
        other = swapped(value, bit)
        if late:
            other = after(other, *late)
        value = (value.astype(f32) + other.astype(f32)).astype(bf16)
    return value


def far_bits():
    count = place_count()
    return [1 << n for n in range(3, count.bit_length() - 1)]


def kernel_call(body, grid, in_specs, out_specs, out_shape, scratch, flops, vmem, prefetch=0):
    return pl.pallas_call(
        body,
        grid_spec=pltpu.PrefetchScalarGridSpec(
            num_scalar_prefetch=prefetch,
            grid=grid,
            in_specs=in_specs,
            out_specs=out_specs,
            scratch_shapes=scratch,
        ),
        out_shape=out_shape,
        compiler_params=pltpu.CompilerParams(vmem_limit_bytes=vmem << 20),
        cost_estimate=pl.CostEstimate(flops=flops, bytes_accessed=8 << 20, transcendentals=0),
    )


def dot_nt(left, right):
    return lax.dot_general(left, right, (((1,), (1,)), ((), ())), preferred_element_type=f32)


def dot_tn(left, right):
    return lax.dot_general(left, right, (((0,), (0,)), ((), ())), preferred_element_type=f32)


def head_lanes(shape, head):
    lane = lax.broadcasted_iota(jnp.int32, shape, 1)
    return (lane >= HEAD_DIM) == (head == 1)


def attend_body(q_ref, ko_ref, kr_ref, vo_ref, vr_ref, sq_ref, so_ref, sr_ref, out_ref, lse_ref, stat):
    step = pl.program_id(0)
    rows = q_ref.shape[0]
    heads = 2 * STEP_PAIRS

    @pl.when(step == 0)
    def _():
        stat[...] = jnp.zeros_like(stat)

    lane = lax.broadcasted_iota(jnp.int32, (rows, LANES), 1)
    same_own = sq_ref[...] == so_ref[...]
    same_far = sq_ref[...] == sr_ref[...]

    def scores(head):
        at = slice(head // 2 * LANES, (head // 2 + 1) * LANES)
        queries = q_ref[:, at].astype(f32) * SCALE
        queries = jnp.where(head_lanes((rows, LANES), head % 2), queries, 0.0).astype(bf16)
        return (
            jnp.where(same_own, dot_nt(queries, ko_ref[:, at]), NEGATIVE),
            jnp.where(same_far, dot_nt(queries, kr_ref[:, at]), NEGATIVE),
        )

    kept = stat[...]
    mixed = []
    ahead = scores(0)
    for head in range(heads):
        s_own, s_far = ahead
        if head + 1 < heads:
            ahead = scores(head + 1)
        top = jnp.maximum(jnp.max(s_own, 1, keepdims=True), jnp.max(s_far, 1, keepdims=True))
        e_own = jnp.exp(s_own - top)
        e_far = jnp.exp(s_far - top)
        total = jnp.sum(e_own, 1, keepdims=True) + jnp.sum(e_far, 1, keepdims=True)
        at = slice(head // 2 * LANES, (head // 2 + 1) * LANES)
        mix = matmul(e_own.astype(bf16), vo_ref[:, at]) + matmul(e_far.astype(bf16), vr_ref[:, at])
        mixed.append(mix / total)
        kept = jnp.where(lane == heads * step + head, top + jnp.log(total), kept)
    for pair in range(STEP_PAIRS):
        at = slice(pair * LANES, (pair + 1) * LANES)
        out_ref[:, at] = jnp.where(lane < HEAD_DIM, mixed[2 * pair], mixed[2 * pair + 1]).astype(bf16)
    stat[...] = kept

    @pl.when(step == pl.num_programs(0) - 1)
    def _():
        turned = jnp.transpose(stat[...])
        for pair in range(HEADS // 2):
            lse_ref[pair] = turned[2 * pair : 2 * pair + 2, :]


def attend(query, q_at, own, ko_at, vo_at, far, kr_at, vr_at, seg_q, seg_own, seg_far):
    rows, keys = query.shape[0], own.shape[0]
    pick = lambda n, at: pl.BlockSpec(
        (n, STEP_PAIRS * LANES), lambda h, at=at: (0, at // STEP_PAIRS + h)
    )
    whole = lambda *shape: pl.BlockSpec(shape, lambda h: (0, 0))
    return kernel_call(
        attend_body,
        (HEADS // 2 // STEP_PAIRS,),
        [
            pick(rows, q_at),
            pick(keys, ko_at),
            pick(keys, kr_at),
            pick(keys, vo_at),
            pick(keys, vr_at),
            whole(rows, 1),
            whole(1, keys),
            whole(1, keys),
        ],
        [pick(rows, 0), pl.BlockSpec((HEADS // 2, 2, rows), lambda h: (0, 0, 0))],
        [
            jax.ShapeDtypeStruct((rows, HEADS * HEAD_DIM), bf16),
            jax.ShapeDtypeStruct((HEADS // 2, 2, rows), f32),
        ],
        [pltpu.VMEM((rows, LANES), f32)],
        16 * rows * keys * 512,
        40,
    )(query, own, far, own, far, seg_q.reshape(rows, 1), seg_own.reshape(1, keys), seg_far.reshape(1, keys))


def attend_back_body(
    q_ref, g_ref, o_ref, lse_ref, ko_ref, kr_ref, vo_ref, vr_ref, sq_ref, so_ref, sr_ref,
    dq_ref, dko_ref, dvo_ref, dkr_ref, dvr_ref,
):
    rows = q_ref.shape[0]
    which = lax.broadcasted_iota(jnp.int32, (8, LANES), 0)
    lane = lax.broadcasted_iota(jnp.int32, (8, LANES), 1)
    chooser = jnp.where((lane >= HEAD_DIM) == (which == 1), 1.0, 0.0).astype(f32)
    along, q_of, g_of = [], [], []
    for pair in range(STEP_PAIRS):
        at = slice(pair * LANES, (pair + 1) * LANES)
        queries = q_ref[:, at].astype(f32) * SCALE
        upstream = g_ref[:, at].astype(f32)
        rows_along = lax.dot_general(
            chooser,
            upstream * o_ref[:, at].astype(f32),
            (((1,), (1,)), ((), ())),
            precision=lax.Precision.HIGHEST,
            preferred_element_type=f32,
        )
        for head in range(2):
            mine = head_lanes((rows, LANES), head)
            along.append(rows_along[head : head + 1, :])
            q_of.append(jnp.where(mine, queries, 0.0).astype(bf16))
            g_of.append(jnp.where(mine, upstream, 0.0).astype(bf16))
    halves = (
        (ko_ref, vo_ref, so_ref, dko_ref, dvo_ref),
        (kr_ref, vr_ref, sr_ref, dkr_ref, dvr_ref),
    )
    units = [
        (pair, head, half) for pair in range(STEP_PAIRS) for half in range(2) for head in range(2)
    ]

    def products(unit):
        pair, head, half = unit
        at = slice(pair * LANES, (pair + 1) * LANES)
        k_ref, v_ref = halves[half][:2]
        return dot_nt(k_ref[:, at], q_of[2 * pair + head]), dot_nt(v_ref[:, at], g_of[2 * pair + head])

    dq_of = [None] * (2 * STEP_PAIRS)
    ahead = products(units[0])
    for n, unit in enumerate(units):
        pair, head, half = unit
        index = 2 * pair + head
        at = slice(pair * LANES, (pair + 1) * LANES)
        k_ref, _, s_ref, dk_ref, dv_ref = halves[half]
        scores, back = ahead
        if n + 1 < len(units):
            ahead = products(units[n + 1])
        same = s_ref[...] == sq_ref[...]
        weights = jnp.exp(jnp.where(same, scores, NEGATIVE) - lse_ref[pair, head : head + 1, :])
        grad = (weights * (back - along[index])).astype(bf16)
        dv = matmul(weights.astype(bf16), g_of[index])
        dk = matmul(grad, q_of[index])
        if head == 0:
            key_t = jnp.transpose(k_ref[:, at].astype(f32)).astype(bf16)
            first = (dk, dv)
        else:
            dk_ref[:, at] = (first[0] + dk).astype(bf16)
            dv_ref[:, at] = (first[1] + dv).astype(bf16)
        dq = matmul(key_t[head * HEAD_DIM : (head + 1) * HEAD_DIM, :], grad)
        dq_of[index] = dq if dq_of[index] is None else dq_of[index] + dq
    for pair in range(STEP_PAIRS):
        at = slice(pair * LANES, (pair + 1) * LANES)
        dq = jnp.concatenate(dq_of[2 * pair : 2 * pair + 2], 0)
        dq_ref[:, at] = (jnp.transpose(dq) * SCALE).astype(bf16)


def attend_back(query, q_at, upstream, mixed, lse, own, ko_at, vo_at, far, kr_at, vr_at, seg_q, seg_own, seg_far):
    rows, keys = query.shape[0], own.shape[0]
    pick = lambda n, at: pl.BlockSpec(
        (n, STEP_PAIRS * LANES), lambda h, at=at: (0, at // STEP_PAIRS + h)
    )
    whole = lambda *shape: pl.BlockSpec(shape, lambda h: (0, 0))
    width = HEADS * HEAD_DIM
    return kernel_call(
        attend_back_body,
        (HEADS // 2 // STEP_PAIRS,),
        [
            pick(rows, q_at),
            pick(rows, 0),
            pick(rows, 0),
            pl.BlockSpec((STEP_PAIRS, 2, rows), lambda h: (h, 0, 0)),
            pick(keys, ko_at),
            pick(keys, kr_at),
            pick(keys, vo_at),
            pick(keys, vr_at),
            whole(1, rows),
            whole(keys, 1),
            whole(keys, 1),
        ],
        [pick(rows, 0)] + [pick(keys, 0)] * 4,
        [jax.ShapeDtypeStruct((rows, width), bf16)] + [jax.ShapeDtypeStruct((keys, width), bf16)] * 4,
        [],
        40 * rows * keys * 512,
        40,
    )(
        query, upstream, mixed, lse, own, far, own, far,
        seg_q.reshape(1, rows), seg_own.reshape(keys, 1), seg_far.reshape(keys, 1),
    )


def columns_of(row):
    return jnp.transpose(jnp.broadcast_to(row, (LANES, row.shape[1])))


def vocab_body(info, *refs):
    blocks, (t_ref, w_ref, e_ref, stat_ref, hidden_ref, kept, targets) = refs[:GROUP], refs[GROUP:]
    step = pl.program_id(0)
    chunk = 128

    @pl.when(step == 0)
    def _():
        for start in range(0, kept.shape[0], TILE):

            @pl.when(start < info[16])
            def _(start=start):
                kept[start : start + TILE, :] = jnp.zeros((TILE, kept.shape[1]), kept.dtype)
                targets[start : start + TILE, :] = jnp.zeros((TILE, LANES), f32)

        for rel in range(GROUP):
            core, near = rel // 4, rel % 4
            block = (core | (near << 1)) ^ info[17]
            count, offset = info[block], info[8 + block]
            src = blocks[rel]
            for start in range(0, src.shape[0], chunk):

                @pl.when(start < count)
                def _(src=src, rel=rel, start=start, offset=offset):
                    for piece in range(start, start + chunk, 16):

                        @pl.when(piece < count)
                        def _(piece=piece):
                            to = pl.ds(pl.multiple_of(offset + piece, 16), 16)
                            kept[to, :] = src[piece : piece + 16, :]

                    value = columns_of(t_ref[rel : rel + 1, start : start + chunk])
                    for piece in range(start, start + chunk, 16):

                        @pl.when(piece < count)
                        def _(piece=piece):
                            to = pl.ds(pl.multiple_of(offset + piece, 16), 16)
                            targets[to, :] = value[piece - start : piece - start + 16, :]

    @pl.when(step * TILE < info[16])
    def _():
        rows = pl.ds(pl.multiple_of(step * TILE, TILE), TILE)
        hidden = kept[rows, :]
        hidden_ref[...] = hidden
        outer, _, piece, _ = w_ref.shape
        tops, totals = [], []
        ahead = dot_nt(w_ref[0, 0], hidden)
        for n in range(outer):
            value = ahead
            if n + 1 < outer:
                ahead = dot_nt(w_ref[n + 1, 0], hidden)
            top = jnp.max(value, 0, keepdims=True)
            value = jnp.exp(value - top)
            tops.append(top)
            totals.append(jnp.sum(value, 0, keepdims=True))
            e_ref[0, n * piece : (n + 1) * piece, :] = value.astype(bf16)
        top = functools.reduce(jnp.maximum, tops)
        shares = [jnp.exp(part - top) for part in tops]
        total = sum(part * share for part, share in zip(totals, shares))
        target = jnp.transpose(targets[rows, :])[:1, :]
        lines = [top, total, target] + shares
        lines.append(jnp.zeros((stat_ref.shape[0] - len(lines), TILE), f32))
        stat_ref[...] = jnp.concatenate(lines, 0)


def stat_lines(outer):
    return -(-(3 + outer + 1) // 8) * 8


def last_active(i, info):
    return jnp.minimum(i, jnp.maximum((info[16] + TILE - 1) // TILE - 1, 0))


def vocab_slice(w):
    outer, _, block, width = w.shape
    return pl.BlockSpec(
        (outer, 1, block, width), lambda i, info: (0, info[18], 0, 0), pipeline_mode=pl.Buffered(1)
    )


def vocab_forward(info, blocks, targets, w):
    rows, width = blocks[0].shape
    total = GROUP * rows
    wide = w.shape[0] * w.shape[2]
    once = lambda *shape: pl.BlockSpec(
        shape, lambda i, info: (0,) * len(shape), pipeline_mode=pl.Buffered(1)
    )
    return kernel_call(
        vocab_body,
        (total // TILE,),
        [once(rows, width)] * GROUP + [once(GROUP, rows), vocab_slice(w)],
        [
            pl.BlockSpec((1, wide, TILE), lambda i, info: (last_active(i, info), 0, 0)),
            pl.BlockSpec((stat_lines(w.shape[0]), TILE), lambda i, info: (0, last_active(i, info))),
            pl.BlockSpec((TILE, width), lambda i, info: (last_active(i, info), 0)),
        ],
        [
            jax.ShapeDtypeStruct((total // TILE, wide, TILE), bf16),
            jax.ShapeDtypeStruct((stat_lines(w.shape[0]), total), f32),
            jax.ShapeDtypeStruct((total, width), bf16),
        ],
        [
            pltpu.VMEM((total, width), bf16),
            pltpu.VMEM((total, LANES), f32),
        ],
        1400 * wide * width * 2,
        34,
        prefetch=1,
    )(info, *blocks, targets, w)


def vocab_back_body(info, e_ref, s_ref, w_ref, out_ref):
    @pl.when(pl.program_id(0) * out_ref.shape[0] < info[16])
    def _():
        outer, _, piece, width = w_ref.shape
        back = None
        for n in range(outer):
            at = slice(n * piece, (n + 1) * piece)
            weights = jnp.concatenate([e_ref[t, at, :] for t in range(e_ref.shape[0])], 1)
            share = columns_of(s_ref[3 + n : 4 + n, :])
            share = jnp.concatenate([share] * (width // LANES), 1)
            value = dot_tn(weights, w_ref[n, 0]) * share
            back = value if back is None else back + value
        out_ref[...] = back.astype(bf16)


def vocab_back(info, e, stats, w):
    tiles, wide, _ = e.shape
    width = w.shape[3]
    both = 2 * TILE
    at = lambda i, info: jnp.minimum(i, jnp.maximum((info[16] + both - 1) // both - 1, 0))
    return kernel_call(
        vocab_back_body,
        (tiles // 2,),
        [
            pl.BlockSpec((2, wide, TILE), lambda i, info: (at(i, info), 0, 0)),
            pl.BlockSpec((stats.shape[0], both), lambda i, info: (0, at(i, info))),
            vocab_slice(w),
        ],
        pl.BlockSpec((both, width), lambda i, info: (at(i, info), 0)),
        jax.ShapeDtypeStruct((tiles * TILE, width), bf16),
        [],
        1400 * wide * width * 2,
        26,
        prefetch=1,
    )(info, e, stats, w)


def spread_body(info, g_ref, f_ref, *refs):
    outs, columns = refs[:-1], refs[-1]
    step = pl.program_id(0)
    total, width = g_ref.shape
    rows = outs[0].shape[0]

    @pl.when(step == 0)
    def _():
        for start in range(0, total, TILE):
            columns[start : start + TILE, :] = columns_of(f_ref[:, start : start + TILE])

    def block_of(core, near):
        block = (core | (near << 1)) ^ info[17]
        at = pl.ds(pl.multiple_of(info[8 + block], 16), rows)
        row = lax.broadcasted_iota(jnp.int32, (rows, LANES), 0)
        factor = jnp.where(row < info[block], columns[at, :], 0.0)
        live = row < info[block]
        pieces = [
            jnp.where(live, g_ref[at, start : start + LANES].astype(f32) * factor, 0.0)
            for start in range(0, width, LANES)
        ]
        return jnp.concatenate(pieces, 1).astype(bf16)

    for n, out_ref in enumerate(outs):

        @pl.when(step == n)
        def _(n=n, out_ref=out_ref):
            out_ref[...] = block_of(1 - n // 4, n % 4)


def spread(info, g, factor, rows):
    total, width = g.shape
    once = lambda *shape: pl.BlockSpec(
        shape, lambda i, info: (0,) * len(shape), pipeline_mode=pl.Buffered(1)
    )
    return kernel_call(
        spread_body,
        (GROUP,),
        [once(total, width), once(1, total)],
        [once(rows, width)] * GROUP,
        [jax.ShapeDtypeStruct((rows, width), bf16)] * GROUP,
        [pltpu.VMEM((total, LANES), f32)],
        total * width,
        44,
        prefetch=1,
    )(info, g, factor)


def vocab_grad_body(piece, info, e_ref, h_ref, s_ref, f_ref, out_ref, total):
    step = pl.program_id(0)

    @pl.when(step == 0)
    def _():
        total[...] = jnp.zeros_like(total)

    @pl.when(step * TILE < info[16])
    def _():
        wide = e_ref.shape[1]
        factor = f_ref[...]
        target = s_ref[2:3, :].astype(jnp.int32)
        row = 1 + lax.broadcasted_iota(jnp.int32, (piece, TILE), 0)
        for start in range(0, wide, piece):
            at = slice(start, start + piece)
            share = 3 + start // piece
            weights = e_ref[0, at, :].astype(f32) * (factor * s_ref[share : share + 1, :])
            weights = (weights - jnp.where(row == target - start, 1.0, 0.0)).astype(bf16)
            total[at, :] += matmul(weights, h_ref[...])

    @pl.when(step == pl.num_programs(0) - 1)
    def _():
        out_ref[...] = total[...].astype(bf16)


def vocab_grad(info, e, hidden, stats, factor, piece):
    tiles, wide, _ = e.shape
    width = hidden.shape[1]
    tile = lambda n: pl.BlockSpec((TILE, n), lambda i, info: (last_active(i, info), 0))
    return kernel_call(
        functools.partial(vocab_grad_body, piece),
        (tiles,),
        [
            pl.BlockSpec((1, wide, TILE), lambda i, info: (last_active(i, info), 0, 0)),
            tile(width),
            pl.BlockSpec((stats.shape[0], TILE), lambda i, info: (0, last_active(i, info))),
            pl.BlockSpec((1, TILE), lambda i, info: (0, last_active(i, info))),
        ],
        pl.BlockSpec((wide, width), lambda i, info: (0, 0)),
        jax.ShapeDtypeStruct((wide, width), bf16),
        [pltpu.VMEM((wide, width), f32)],
        1400 * wide * width * 2,
        40,
        prefetch=1,
    )(info, e, hidden, stats, factor)


def halves_body(plan, info, *refs):
    plan, parts = plan
    operands, outs = refs[: -2 * parts], refs[-2 * parts :]
    rows = outs[0].shape[0]

    def fill(half, out_refs):
        at, part = 0, 0
        for terms, width in plan:
            if at == out_refs[part].shape[1]:
                at, part = 0, part + 1
            out_ref = out_refs[part]
            total = None
            for left, left_at, right, right_at in terms:
                if right is None:
                    lines = [operands[n][:, start : start + 2 * rows] for n, start in left]
                    blank = width - sum(line.shape[0] for line in lines)
                    lines.append(jnp.zeros((blank, 2 * rows), f32))
                    turned = jnp.transpose(jnp.concatenate(lines, 0))
                    value = jnp.where(half == 0, turned[:rows], turned[rows:])
                else:
                    lanes = pl.ds(pl.multiple_of(left_at + half * rows, rows), rows)
                    value = dot_tn(
                        operands[left][:, lanes], operands[right][:, right_at : right_at + width]
                    )
                total = value if total is None else total + value
            out_ref[:, at : at + width] = total.astype(bf16)
            at += width

    @pl.when(pl.program_id(0) == 0)
    def _():
        fill(1 - info[0], outs[:parts])

    @pl.when(pl.program_id(0) == 1)
    def _():
        fill(info[0], outs[parts:])


def weight_halves(columns, rows, vmem=36, parts=1):
    operands, plan = [], []

    def index_of(array):
        for n, known in enumerate(operands):
            if known is array:
                return n
        operands.append(array)
        return len(operands) - 1

    for width, terms in columns:
        taken = []
        for left, left_at, right, right_at in terms:
            if right is None:
                taken.append(([(index_of(row), start) for row, start in left], 0, None, 0))
            else:
                taken.append((index_of(left), left_at, index_of(right), right_at))
        plan.append((taken, width))
    total = sum(width for width, _ in columns)
    whole = lambda shape: pl.BlockSpec(shape, lambda i, info: (0, 0), pipeline_mode=pl.Buffered(1))
    return kernel_call(
        functools.partial(halves_body, (plan, parts)),
        (2,),
        [whole(o.shape) for o in operands],
        [whole((rows // 2, total // parts))] * (2 * parts),
        [jax.ShapeDtypeStruct((rows // 2, total // parts), bf16)] * (2 * parts),
        [],
        rows * total * 1024,
        vmem,
        prefetch=1,
    )(group_index([CORE_BIT])[None], *operands)


def core_summed(send, keep):
    return (keep.astype(f32) + swapped(send, CORE_BIT).astype(f32)).astype(bf16)


def joined_body(plan, info, own_ref, other_ref, *outs):
    rows = own_ref.shape[0]
    mine, far = pl.multiple_of(info[0] * rows, rows), pl.multiple_of((1 - info[0]) * rows, rows)
    for (starts, width, turned), out_ref in zip(plan, outs):
        for n, start in enumerate(starts):
            for ref, at in ((own_ref, mine), (other_ref, far)):
                value = ref[:, start : start + width].astype(f32)
                if turned:
                    out_ref[:, pl.ds(at, rows)] = jnp.transpose(value)
                else:
                    out_ref[pl.ds(n * 2 * rows + at, rows), :] = value


def joined(own, other, plan):
    rows = own.shape[0]
    shapes = [
        (width, 2 * rows) if turned else (2 * rows * len(starts), width)
        for starts, width, turned in plan
    ]
    once = lambda shape: pl.BlockSpec(shape, lambda i, info: (0, 0), pipeline_mode=pl.Buffered(1))
    return kernel_call(
        functools.partial(joined_body, plan),
        (1,),
        [once(own.shape)] * 2,
        [once(shape) for shape in shapes],
        [jax.ShapeDtypeStruct(shape, f32) for shape in shapes],
        [],
        own.size,
        36,
        prefetch=1,
    )(group_index([CORE_BIT])[None], own, other)


def as_columns_body(rows_ref, *outs):
    for n, out_ref in enumerate(outs):
        out_ref[...] = columns_of(rows_ref[n : n + 1, :])[:, :1].astype(jnp.int32)


def as_columns(*rows):
    count = rows[0].shape[0]
    whole = lambda *shape: pl.BlockSpec(shape, lambda i, info: (0, 0))
    return kernel_call(
        as_columns_body_with_info,
        (1,),
        [whole(len(rows), count)],
        [whole(count, 1)] * len(rows),
        [jax.ShapeDtypeStruct((count, 1), jnp.int32)] * len(rows),
        [],
        count,
        16,
        prefetch=1,
    )(jnp.zeros((1,), jnp.int32), jnp.stack(rows).astype(f32))


def as_columns_body_with_info(info, *refs):
    as_columns_body(*refs)


def added_body(info, *refs):
    count = len(refs) // 3
    for n in range(count):
        total = refs[n][...].astype(f32) + refs[count + n][...].astype(f32)
        refs[2 * count + n][...] = total.astype(bf16)


def added(firsts, seconds):
    rows, width = firsts[0].shape
    piece = pl.BlockSpec((rows // 4, width), lambda i, info: (i, 0))
    return kernel_call(
        added_body,
        (4,),
        [piece] * (2 * len(firsts)),
        [piece] * len(firsts),
        [jax.ShapeDtypeStruct((rows, width), bf16)] * len(firsts),
        [],
        rows * width,
        58,
        prefetch=1,
    )(jnp.zeros((1,), jnp.int32), *firsts, *seconds)


def per_device(
    hidden_in,
    enc_states,
    segment_ids,
    edit_pass,
    enc_segments,
    target_tokens,
    placeholder_counts,
    delete_labels,
    loss_mask,
    w_self_qkv,
    w_self_out,
    w_cross_q,
    w_cross_kv,
    w_cross_out,
    w_ffn_in,
    b_ffn_in,
    w_ffn_out,
    b_ffn_out,
    norm_gains,
    norm_shifts,
    w_vocab,
    w_pair,
    b_pair,
    w_delete,
):
    _, tokens, features = hidden_in.shape
    seq = lax.axis_index("seq")
    chip = [NEAR_BIT, SEQ_BIT]
    far = far_bits()
    hidden = hidden_in[0]
    source = enc_states[0]
    hidden_far = swapped(hidden, SEQ_BIT)
    qkv = matmul(hidden, w_self_qkv).astype(bf16)
    segment, passes, source_seg = segment_ids[0], edit_pass[0], enc_segments[0]

    keep_float = loss_mask[0].astype(f32)
    token_keep = keep_float * (passes == 2).astype(f32)
    row = lax.broadcasted_iota(jnp.int32, (tokens, tokens), 0)
    col = lax.broadcasted_iota(jnp.int32, (tokens, tokens), 1)
    rank = matmul(token_keep.astype(bf16)[None, :], (row <= col).astype(bf16)) - 1.0
    selects = (rank.astype(jnp.int32) == row) & (token_keep[None, :] > 0)
    chooser = selects.astype(bf16)
    targets = target_tokens[0]
    chosen = jnp.sum(jnp.where(selects, targets[None, :] + 1, 0), 1)
    ids_far = swapped(jnp.stack([segment, source_seg, chosen]), SEQ_BIT)
    segment_far, source_seg_far = ids_far[0], ids_far[1]

    vocab = w_vocab.shape[0]
    outer = lax.axis_size("far")
    block = vocab // (outer * GROUP)
    inner = lax.axis_index(("near", "core", "seq"))
    here = group_index([CORE_BIT, NEAR_BIT, SEQ_BIT])
    ckv = matmul(source, w_cross_kv).astype(bf16)
    hidden_far = after(hidden_far, ckv, qkv, chosen)
    kv_far = matmul(hidden_far, w_self_qkv[:, features:]).astype(bf16)
    source_far = swapped(after(source, hidden_far), SEQ_BIT)
    self_mix, self_lse = attend(qkv, 0, qkv, 4, 8, kv_far, 0, 4, segment, segment, segment_far)
    chosen_row = jnp.stack([chosen, ids_far[2]])
    chosen_near = swapped(chosen_row, NEAR_BIT)
    self_mix, self_lse, source_far, chosen_near = lax.optimization_barrier(
        (self_mix, self_lse, source_far, chosen_near)
    )
    layer_one, normed_one, invert_one = norm_forward(
        hidden.astype(f32) + matmul(self_mix, w_self_out), norm_gains[0], norm_shifts[0]
    )

    chosen_chip = jnp.stack([chosen_row[0], chosen_near[0], chosen_row[1], chosen_near[1]])
    chosen_core = swapped(chosen_chip, CORE_BIT)
    one_low = layer_one.astype(bf16)
    cross_query = matmul(one_low, w_cross_q).astype(bf16)
    ckv_far = matmul(source_far, w_cross_kv).astype(bf16)
    cross_mix, cross_lse = attend(
        cross_query, 0, ckv, 0, 4, ckv_far, 0, 4, segment, source_seg, source_seg_far
    )
    cross_mix, cross_lse, chosen_core = lax.optimization_barrier((cross_mix, cross_lse, chosen_core))
    chosen_all = jnp.concatenate([chosen_chip, chosen_core])
    index = chosen_all - 1
    local = (index // (block * GROUP)) * block + index % block + 1
    mine = (chosen_all > 0) & ((index // block) % GROUP == inner)
    local_targets = jnp.where(mine, local, 0).astype(f32)
    counts_rel = jnp.sum((chosen_all > 0).astype(jnp.int32), 1)
    relative = jnp.array([c | (n << 1) for c in range(2) for n in range(4)], jnp.int32) ^ here
    counts = jnp.sum(
        jnp.where(relative[:, None] == jnp.arange(GROUP)[None, :], counts_rel[:, None], 0), 0
    )
    rounded = (counts + 15) // 16 * 16
    before = jnp.arange(GROUP)[:, None] < jnp.arange(GROUP)[None, :]
    offsets = jnp.sum(jnp.where(before, rounded[:, None], 0), 0)
    info = jnp.concatenate([counts, offsets, jnp.sum(rounded)[None], here[None], inner[None]]).astype(jnp.int32)

    layer_two, normed_two, invert_two = norm_forward(
        layer_one + matmul(cross_mix, w_cross_out), norm_gains[1], norm_shifts[1]
    )
    two_low = layer_two.astype(bf16)
    pre_act = matmul(two_low, w_ffn_in) + b_ffn_in
    activ, gate_back = jax.vjp(smooth_gate, pre_act)
    activ_low = activ.astype(bf16)
    layer_three, normed_three, invert_three = norm_forward(
        layer_two + (matmul(activ_low, w_ffn_out) + b_ffn_out), norm_gains[2], norm_shifts[2]
    )
    three_low = layer_three.astype(bf16)

    kept = matmul(chooser, three_low).astype(bf16)
    kept_core = swapped(kept, CORE_BIT)
    kept_chip = [swapped(kept, NEAR_BIT), swapped(kept, SEQ_BIT), swapped(kept, NEAR_BIT | SEQ_BIT)]
    next_row = passed_along(three_low[:1], "seq", -1)
    w_parts = w_vocab.reshape(outer, GROUP, block, features)
    target_rows = jnp.take(w_vocab, after(targets, kept), axis=0).astype(f32)
    kept_chip = [after(k, target_rows) for k in kept_chip]
    kept_other = [swapped(k, CORE_BIT) for k in kept_chip]

    delete_keep = keep_float * (passes == 0).astype(f32)

    def label_grad(logits, labels, keep_mask):
        shifted = logits - jnp.max(logits, -1, keepdims=True)
        exponent = jnp.exp(shifted)
        weights = exponent / jnp.sum(exponent, -1, keepdims=True)
        onehot = labels[:, None] == lax.broadcasted_iota(jnp.int32, logits.shape, 1)
        return ((weights - onehot.astype(f32)) * keep_mask[:, None]).astype(bf16)

    delete_grad = label_grad(matmul(three_low, w_delete), delete_labels[0], delete_keep)

    delete_back = matmul_right(delete_grad, w_delete) - target_rows * token_keep[:, None]
    d_delete = matmul_left(delete_grad, three_low)
    segment_col, segment_far_col, source_col, source_far_col = as_columns(
        segment, segment_far, source_seg, source_seg_far
    )
    info, segment_col, segment_far_col, source_col, source_far_col = lax.optimization_barrier(
        (info, segment_col, segment_far_col, source_col, source_far_col)
    )
    pair_own = matmul(three_low, w_pair[:features]) + b_pair
    w_pair_next = after(w_pair[features:], kept)
    info = after(info, delete_back, d_delete, pair_own, w_pair_next)
    e, stat_rows, kept_all = vocab_forward(
        info, [kept] + kept_chip + [kept_core] + kept_other, local_targets, w_parts
    )
    stats = stat_rows[:2]

    def merged(first, *others):
        most = functools.reduce(jnp.maximum, [o[0] for o in others], first[0])
        added = sum((o[1] * jnp.exp(o[0] - most) for o in others), first[1] * jnp.exp(first[0] - most))
        return jnp.stack([most, added])

    stats_pair = merged(stats, swapped(stats, CORE_BIT))
    stats_all = merged(stats_pair, *[swapped(stats_pair, group_mask(chip, r)) for r in (1, 2, 3)])
    factor = jnp.exp(stats[0] - stats_all[0] - jnp.log(stats_all[1]))[None, :]
    back_raw = vocab_back(info, e, stat_rows, w_parts)
    back = spread(info, back_raw, factor, tokens)
    back_core = [swapped(b, CORE_BIT) for b in back[:4]]
    back_near = back[4:]
    back_low = added(back_near[1:], back_core[1:])
    position = seq * tokens + jnp.arange(tokens, dtype=jnp.int32)
    row_length = tokens * lax.axis_size("seq")
    follow = jnp.concatenate([three_low[1:], after(next_row, *back_low)], 0)
    follow_seg = jnp.concatenate([segment[1:], segment_far[:1]], 0)
    pair_ok = (follow_seg == segment) & (position < row_length - 1)
    pair_keep = keep_float * (passes == 1).astype(f32) * pair_ok.astype(f32)
    pair_logits = pair_own + matmul(follow, w_pair_next)
    pair_grad = label_grad(pair_logits, placeholder_counts[0], pair_keep)
    follow_grad = matmul_right(pair_grad, w_pair_next)
    back_row = passed_along(follow_grad[-1:], "seq", 1)
    d_b_pair = jnp.sum(pair_grad.astype(f32), 0, keepdims=True)
    d_b_pair = jnp.pad(d_b_pair, ((0, 0), (0, features - d_b_pair.shape[1])))
    head_back = [swapped(back_low[r - 1], group_mask(chip, r)).astype(f32) for r in (1, 2, 3)]
    head_back = sum(head_back, back_near[0].astype(f32) + back_core[0].astype(f32))
    vocab_part = vocab_grad(
        info, e, kept_all, stat_rows, after(factor, *back_low), block
    )
    d_vocab = lax.psum_scatter(vocab_part, "far", scatter_dimension=0, tiled=True)
    grad_local = (
        delete_back
        + matmul_right(pair_grad, w_pair[:features])
        + jnp.concatenate([back_row, follow_grad[:-1]], 0)
    )
    grad_local = after(grad_local, vocab_part)

    grad_three = grad_local + matmul_left(chooser, head_back.astype(bf16))
    grad_sum3, gain_three, shift_three = norm_backward(
        grad_three, normed_three, invert_three, norm_gains[2]
    )
    branch_three = grad_sum3.astype(bf16)
    row_sum = lambda value: jnp.sum(value.astype(f32), 0, keepdims=True)
    d_b_ffn_out = row_sum(branch_three)
    grad_pre = gate_back(matmul_right(branch_three, w_ffn_out))[0].astype(bf16)
    d_b_ffn_in = row_sum(grad_pre)
    hidden_units = w_ffn_in.shape[1]
    pair_count = w_pair.shape[1]
    halves_ffn = weight_halves(
        [(hidden_units, [(two_low, 0, grad_pre, 0)])]
        + [(features, [(activ_low, at, branch_three, 0)]) for at in range(0, hidden_units, features)],
        features,
        parts=2,
    )
    sum_ffn = jnp.concatenate(
        [core_summed(send, keep) for send, keep in zip(halves_ffn[:2], halves_ffn[2:])], 1
    )
    grad_two = grad_sum3 + matmul_right(grad_pre, w_ffn_in)
    grad_sum2, gain_two, shift_two = norm_backward(grad_two, normed_two, invert_two, norm_gains[1])
    branch_two = grad_sum2.astype(bf16)
    cross_up = matmul_right(branch_two, w_cross_out).astype(bf16)
    cross_up, sum_ffn = lax.optimization_barrier((cross_up, sum_ffn))
    own_ffn, others_ffn = scattered(sum_ffn, chip)
    dcq, dck, dcv, dck_far, dcv_far = attend_back(
        cross_query, 0, cross_up, cross_mix, cross_lse, ckv, 0, 4, ckv_far, 0, 4,
        segment, source_col, source_far_col,
    )
    w_ckey, w_cvalue = w_cross_kv[:, :features], w_cross_kv[:, features:]
    d_enc_low = (matmul_right(dck_far, w_ckey) + matmul_right(dcv_far, w_cvalue)).astype(bf16)
    d_enc_far = swapped(d_enc_low, SEQ_BIT)
    dcq = after(dcq, d_enc_low)
    send_mid, keep_mid = weight_halves(
        [
            (features, [(cross_mix, 0, branch_two, 0)]),
            (features, [(one_low, 0, dcq, 0)]),
            (features, [(source, 0, dck, 0), (source_far, 0, dck_far, 0)]),
            (features, [(source, 0, dcv, 0), (source_far, 0, dcv_far, 0)]),
            (pair_count, [(three_low, 0, pair_grad, 0)]),
            (pair_count, [(follow, 0, pair_grad, 0)]),
        ],
        features,
    )
    keep_mid, send_mid, others_ffn = lax.optimization_barrier((keep_mid, send_mid, others_ffn))
    sum_ffn = part_sum(own_ffn, others_ffn)
    sum_mid = core_summed(send_mid, keep_mid)
    grad_one = grad_sum2 + matmul_right(after(dcq, keep_mid), w_cross_q)
    grad_sum1, gain_one, shift_one = norm_backward(grad_one, normed_one, invert_one, norm_gains[0])
    branch_one = grad_sum1.astype(bf16)
    self_up = matmul_right(branch_one, w_self_out).astype(bf16)
    self_up = after(self_up, sum_mid)
    sum_mid = scatter_sum(after(sum_mid, self_up), chip)
    own_ffn, others_ffn = scattered(sum_ffn, far[:1])
    dq, dk, dv, dk_far, dv_far = attend_back(
        qkv, 0, self_up, self_mix, self_lse, qkv, 4, 8, kv_far, 0, 4, segment, segment_col, segment_far_col
    )
    dq, dk, dv, dk_far, dv_far, sum_mid, others_ffn, d_enc_far = lax.optimization_barrier(
        (dq, dk, dv, dk_far, dv_far, sum_mid, others_ffn, d_enc_far)
    )
    sum_ffn = part_sum(own_ffn, others_ffn)

    w_key, w_value = w_self_qkv[:, features : 2 * features], w_self_qkv[:, 2 * features :]
    d_hidden_low = (matmul_right(dk_far, w_key) + matmul_right(dv_far, w_value)).astype(bf16)
    dq = after(dq, d_hidden_low)
    send_qkv, keep_qkv = weight_halves(
        [
            (features, [(hidden, 0, dq, 0)]),
            (features, [(hidden, 0, dk, 0), (hidden_far, 0, dk_far, 0)]),
            (features, [(hidden, 0, dv, 0), (hidden_far, 0, dv_far, 0)]),
            (features, [(self_mix, 0, branch_one, 0)]),
            (
                LANES,
                [
                    (
                        [(d_b_ffn_in, at) for at in range(0, hidden_units, features)]
                        + [(row, 0) for row in (d_b_ffn_out, gain_one, gain_two, gain_three)]
                        + [(row, 0) for row in (shift_one, shift_two, shift_three, d_b_pair)]
                        + [(d_delete, 0)],
                        0,
                        None,
                        0,
                    )
                ],
            ),
        ],
        features,
        58,
    )
    d_hidden_far = swapped(d_hidden_low, SEQ_BIT)
    sum_ffn = doubled(sum_ffn, far[1:], keep_qkv)
    sum_qkv, d_hidden_far, d_vocab, sum_ffn = lax.optimization_barrier((core_summed(send_qkv, keep_qkv), d_hidden_far, d_vocab, sum_ffn))
    sum_qkv = scatter_sum(sum_qkv, chip)
    sum_mid = scatter_sum(after(sum_mid, sum_ffn), far[:1], sum_qkv)
    sum_ffn = gathered(sum_ffn, far[:1], sum_qkv)
    sum_mid = doubled(sum_mid, far[1:])
    sum_mid = gathered(sum_mid, far[:1])
    sum_qkv = doubled(sum_qkv, far)
    sum_rest = jnp.concatenate([sum_mid, sum_qkv], 1)
    sum_ffn = gathered(sum_ffn, chip, sum_rest)
    ffn_other = swapped(sum_ffn, CORE_BIT)
    out_ffn_in, out_ffn_out = joined(
        sum_ffn,
        ffn_other,
        [
            ([0], hidden_units, False),
            (list(range(hidden_units, 2 * hidden_units, features)), features, False),
        ],
    )
    d_hidden = (
        grad_sum1
        + matmul_right(dq, w_self_qkv[:, :features])
        + matmul_right(dk, w_key)
        + matmul_right(dv, w_value)
        + d_hidden_far.astype(f32)
    )
    d_enc = matmul_right(dck, w_ckey) + matmul_right(dcv, w_cvalue) + d_enc_far.astype(f32)

    d_vocab = d_vocab.astype(f32)
    rest_at = sum_mid.shape[1]
    sum_rest = gathered(after(sum_rest, sum_ffn), chip, out_ffn_in, out_ffn_out, d_enc)
    rest_other = after(swapped(sum_rest, CORE_BIT), d_hidden, d_vocab)
    pair_at = 4 * features
    out_cross_out, out_cross_q, out_cross_kv, out_pair, out_self_qkv, out_self_out, small = joined(
        sum_rest,
        rest_other,
        [
            ([0], features, False),
            ([features], features, False),
            ([2 * features], 2 * features, False),
            ([pair_at, pair_at + pair_count], pair_count, False),
            ([rest_at], 3 * features, False),
            ([rest_at + 3 * features], features, False),
            ([rest_at + 4 * features], LANES, True),
        ],
    )
    units = hidden_units // features
    out_b_ffn_in = small[:units].reshape(-1)
    out_b_ffn_out = small[units]
    out_gains = small[units + 1 : units + 4]
    out_shifts = small[units + 4 : units + 7]
    out_b_pair = small[units + 7, :pair_count]
    out_delete = jnp.transpose(small[units + 8 : units + 10])
    return (
        three_low[None],
        d_hidden[None],
        d_enc[None],
        out_self_qkv,
        out_self_out,
        out_cross_q,
        out_cross_kv,
        out_cross_out,
        out_ffn_in,
        out_b_ffn_in,
        out_ffn_out,
        out_b_ffn_out,
        out_gains,
        out_shifts,
        d_vocab,
        out_pair,
        out_b_pair,
        out_delete,
    )


def solution(mesh):
    split_mesh = Mesh(mesh.devices.reshape(-1, 2, 2, mesh.shape["seq"]), AXES)
    rows = ("far", "near", "core")
    split = P(rows, "seq", None)
    ids = P(rows, "seq")
    return jax.shard_map(
        per_device,
        mesh=split_mesh,
        in_specs=(split, split) + (ids,) * 7 + (P(),) * 15,
        out_specs=(split,) * 3 + (P(),) * 11 + (P(AXES, None),) + (P(),) * 3,
        check_vma=False,
    )
```
